128 devices in a mesh: row: 16 (over x, z_lo, core), col: 8 (over z_hi, y).
Axes of the slice: x: 4, y: 4, z: 4 (z_hi: 2, z_lo: 2; z = z_hi * 2 + z_lo), core: 2. Of those that a mesh axis runs over, the one named last changes fastest.
Arguments:
- alignment: bfloat16 [640, 512, 256], P('col', 'row'), may hold values from -6 to 6
- pairwise: bfloat16 [512, 512, 128], P('row', 'col'), may hold values from -6 to 6
- residue_mask: int32 [512], replicated, may hold values 0 or 1
- sequence_mask: int32 [640], replicated, may hold values 0 or 1
- attention_input_weight: bfloat16 [256, 4, 256], replicated, may hold values from -0.375 to 0.375
- attention_output_weight: bfloat16 [256, 256], replicated, may hold values from -1 to 1
- bias_project: bfloat16 [128, 8], replicated, may hold values from -100 to 100
- outer_factor_weight: bfloat16 [256, 2, 32], replicated, may hold values from -0.375 to 0.375
- outer_output: bfloat16 [1024, 128], replicated, may hold values from -1 to 1
- tri_project: bfloat16 [128, 4, 128], replicated, may hold values from -0.5 to 0.5
- tri_gate: bfloat16 [128, 128], replicated, may hold values from -0.5 to 0.5
- tri_output: bfloat16 [128, 128], replicated, may hold values from -0.5 to 0.5
Outputs:
- alignment_output: bfloat16 [640, 512, 256], P('col', 'row')
- pair_output_state: bfloat16 [512, 512, 128], P('row', 'col')
The draws below stay inside these ranges and needn't reach their ends.
All inputs are finite; a program needn't handle non-finite values.
Results may differ from the reference program's by a relative error of at most 0.017.
Values may be sent and summed in bfloat16 or wider, within the bound.
No kernel may reach another device: no remote copies, remote signals or barrier semaphores. Data moves between devices by JAX's collectives and lax.ppermute only.
A program may use at most 128 MiB of HBM per device.

```python
import jax
import jax.numpy as jnp
from jax import lax

CM = 256
HEADS = 8
CZ = 128
C_OPM = 32
C_TRI = 128
N_RES = 512
S = 640


def draw_bias_project(key, part):
    base = jnp.clip(jax.random.normal(key, (CZ, HEADS), jnp.float32), -4.0, 4.0)
    return (base * 0.15).astype(jnp.bfloat16)


def touch_ends(values, own_key, least, high):
    shape = values.shape
    index_at = [jax.random.randint(jax.random.fold_in(own_key, axis), (), 0, shape[axis]) for axis in range(len(shape))]
    values = values.at[tuple(index_at)].set(least)
    longest = shape.index(max(shape))
    index_at[longest] = (index_at[longest] + 1) % shape[longest]
    return values.at[tuple(index_at)].set(high)


def levels(stream_key, extent, pieces, low, top_value):
    def one(axis_at, blocks):
        draws = jax.random.uniform(jax.random.fold_in(jax.random.fold_in(stream_key, 6), axis_at), (blocks,), jnp.float32, low / len(pieces), top_value / len(pieces))
        return jnp.repeat(jnp.exp(draws), extent[axis_at] // blocks).reshape((-1,) + (1,) * (len(extent) - axis_at - 1))

    factor_of = one(*pieces[0])
    for cut in pieces[1:]:
        factor_of = factor_of * one(*cut)
    return factor_of


def gaussian(rng, dims, scale, most, shards=(), dtype=jnp.bfloat16):
    level = levels(rng, dims, shards, -0.22, 0.18) if shards else 1.0
    drawn = jax.random.normal(rng, dims, jnp.float32) * scale * level
    return jnp.minimum(jnp.maximum(drawn, -most), most).astype(dtype)


def setup_inputs(seed: int = 0) -> dict:
    key_list = jax.random.split(jax.random.key(seed), 13)
    return {
        "alignment": gaussian(key_list[0], (S, N_RES, CM), 1.0, 6.0, ((0, 8), (1, 16))),
        "pairwise": gaussian(key_list[1], (N_RES, N_RES, CZ), 1.0, 6.0, ((0, 16), (1, 8))),
        "residue_mask": touch_ends((jax.random.randint(key_list[2], (N_RES,), 0, 8) < 7).astype(jnp.int32), jax.random.fold_in(key_list[2], 1), 0, 1),
        "sequence_mask": touch_ends((jax.random.randint(key_list[3], (S,), 0, 8) < 7).astype(jnp.int32), jax.random.fold_in(key_list[3], 1), 0, 1),
        "attention_input_weight": gaussian(key_list[4], (CM, 4, CM), CM ** -0.5, 0.375),
        "attention_output_weight": gaussian(key_list[5], (CM, CM), (CM // 8) ** -0.5, 1.0),
        "bias_project": draw_bias_project(jax.random.fold_in(key_list[12], 71), 0),
        "outer_factor_weight": gaussian(key_list[7], (CM, 2, C_OPM), CM ** -0.5, 0.375),
        "outer_output": gaussian(key_list[8], (C_OPM * C_OPM, CZ), C_OPM ** -0.5, 1.0),
        "tri_project": gaussian(key_list[9], (CZ, 4, C_TRI), CZ ** -0.5, 0.5),
        "tri_gate": gaussian(key_list[10], (CZ, CZ), CZ ** -0.5, 0.5),
        "tri_output": gaussian(key_list[11], (C_TRI, CZ), C_TRI ** -0.5, 0.5),
    }


EPS = 1e-05
BIG = 1000000000.0

def normalize_layer(inputs):
    inputs = inputs.astype(jnp.float32)
    centered = inputs - lax.optimization_barrier(jnp.mean(inputs, axis=-1, keepdims=True))
    variance = lax.optimization_barrier(jnp.mean(centered * centered, axis=-1, keepdims=True))
    return centered * lax.rsqrt(variance + EPS)

def reference(alignment, pairwise, residue_mask, sequence_mask, attention_input_weight, attention_output_weight, bias_project, outer_factor_weight, outer_output, tri_project, tri_gate, tri_output):
    sequence_total_count, residue_length, alignment_channel_width = alignment.shape
    number_of_heads = bias_project.shape[1]
    per_head_width = alignment_channel_width // number_of_heads
    outer_mean_width = outer_factor_weight.shape[2]
    channels = pairwise.shape[2]
    hidden = tri_project.shape[2]
    res_live = residue_mask.astype(jnp.float32)
    seq_live = sequence_mask.astype(jnp.float32)
    key_penalty = (res_live - 1.0) * BIG
    pair_normed = normalize_layer(pairwise).astype(jnp.bfloat16)
    bias_terms = jnp.dot(pair_normed.reshape(residue_length * residue_length, channels), bias_project, preferred_element_type=jnp.float32)
    bias_terms = jnp.transpose(bias_terms.reshape(residue_length, residue_length, number_of_heads), (2, 0, 1)).astype(jnp.bfloat16)
    alignment_normalized = normalize_layer(alignment).astype(jnp.bfloat16)
    projected_rows = jnp.dot(alignment_normalized.reshape(sequence_total_count * residue_length, alignment_channel_width), attention_input_weight.reshape(alignment_channel_width, 4 * alignment_channel_width), preferred_element_type=jnp.float32).reshape(sequence_total_count, residue_length, 4, alignment_channel_width)
    query_rows = (projected_rows[:, :, 0] * per_head_width ** (-0.5)).astype(jnp.bfloat16)
    keys_all = projected_rows[:, :, 1].astype(jnp.bfloat16)
    values_all = projected_rows[:, :, 2].astype(jnp.bfloat16)
    gate_activation = jax.nn.sigmoid(projected_rows[:, :, 3])

    def attend_sequence(operands):
        query_one, key_one, value_one, single_gate_value = operands
        query_heads = query_one.reshape(residue_length, number_of_heads, per_head_width).astype(jnp.float32)
        key_heads = key_one.reshape(residue_length, number_of_heads, per_head_width).astype(jnp.float32)
        value_heads = value_one.reshape(residue_length, number_of_heads, per_head_width).astype(jnp.float32)
        scores = jnp.einsum('ihd,jhd->hij', query_heads, key_heads)
        scores = scores + bias_terms.astype(jnp.float32) + key_penalty[None, None, :]
        scores = scores - lax.optimization_barrier(jnp.max(scores, axis=-1, keepdims=True))
        exponent = jnp.exp(scores)
        weights = (exponent / lax.optimization_barrier(jnp.sum(exponent, axis=-1, keepdims=True))).astype(jnp.bfloat16)
        weighted_value_mix = jnp.einsum('hij,jhd->ihd', weights.astype(jnp.float32), value_heads)
        return (weighted_value_mix.reshape(residue_length, alignment_channel_width) * single_gate_value).astype(jnp.bfloat16)
    attention_result_rows = lax.map(attend_sequence, (query_rows, keys_all, values_all, gate_activation))
    alignment_output = (alignment.astype(jnp.float32) + jnp.dot(attention_result_rows.reshape(sequence_total_count * residue_length, alignment_channel_width), attention_output_weight, preferred_element_type=jnp.float32).reshape(sequence_total_count, residue_length, alignment_channel_width)).astype(jnp.bfloat16)
    alignment_second_copy = normalize_layer(alignment_output).astype(jnp.bfloat16)
    outer_factor_pair = jnp.dot(alignment_second_copy.reshape(sequence_total_count * residue_length, alignment_channel_width), outer_factor_weight.reshape(alignment_channel_width, 2 * outer_mean_width), preferred_element_type=jnp.float32).reshape(sequence_total_count, residue_length, 2, outer_mean_width)
    live_both = seq_live[:, None] * res_live[None, :]
    left_outer = (outer_factor_pair[:, :, 0] * live_both[:, :, None]).astype(jnp.bfloat16)
    right_outer = (outer_factor_pair[:, :, 1] * live_both[:, :, None]).astype(jnp.bfloat16)
    counts = jnp.dot(live_both.T, live_both, precision=lax.Precision.HIGHEST)
    right_flat = right_outer.reshape(sequence_total_count, residue_length * outer_mean_width)

    def outer_row(operands):
        left_row, count_row = operands
        product = jnp.dot(left_row.T, right_flat, preferred_element_type=jnp.float32).astype(jnp.bfloat16)
        product = jnp.transpose(product.reshape(outer_mean_width, residue_length, outer_mean_width), (1, 0, 2)).reshape(residue_length, outer_mean_width * outer_mean_width)
        update = jnp.dot(product, outer_output, preferred_element_type=jnp.float32)
        return update / jnp.maximum(count_row, 1.0)[:, None]
    updates = lax.map(outer_row, (jnp.transpose(left_outer, (1, 0, 2)), counts))
    pair_mid = (pairwise.astype(jnp.float32) + updates).astype(jnp.bfloat16)
    tri_normed = normalize_layer(pair_mid).astype(jnp.bfloat16)
    flat_normed = tri_normed.reshape(residue_length * residue_length, channels)
    tri_terms = jnp.dot(flat_normed, tri_project.reshape(channels, 4 * hidden), preferred_element_type=jnp.float32).reshape(residue_length, residue_length, 4, hidden)
    pair_live = (res_live[:, None] * res_live[None, :])[:, :, None]
    left_tri = (jax.nn.sigmoid(tri_terms[:, :, 0]) * tri_terms[:, :, 1] * pair_live).astype(jnp.bfloat16)
    right_tri = (jax.nn.sigmoid(tri_terms[:, :, 2]) * tri_terms[:, :, 3] * pair_live).astype(jnp.bfloat16)
    combined = jnp.einsum('ikc,jkc->ijc', left_tri.astype(jnp.float32), right_tri.astype(jnp.float32))
    tri_result = normalize_layer(combined).astype(jnp.bfloat16)
    gate_out = jax.nn.sigmoid(jnp.dot(flat_normed, tri_gate, preferred_element_type=jnp.float32)).reshape(residue_length, residue_length, channels)
    update_tri = jnp.dot(tri_result.reshape(residue_length * residue_length, hidden), tri_output, preferred_element_type=jnp.float32).reshape(residue_length, residue_length, channels)
    pair_output_state = (pair_mid.astype(jnp.float32) + gate_out * update_tri).astype(jnp.bfloat16)
    return (alignment_output, pair_output_state)
```

```python
import jax
import jax.numpy as jnp
from jax import lax
from jax.experimental import pallas as pl
from jax.experimental.pallas import tpu as pltpu
from jax.sharding import Mesh, PartitionSpec as P

EPS = 1e-05
BIG = 1000000000.0
F32 = jnp.float32
BF16 = jnp.bfloat16
ROW = ("x", "zl", "core")
COL = ("zh", "y")
ALL = ROW + COL
CHIP = ("x", "zl", "zh", "y")
NT = (((1,), (1,)), ((), ()))
TN = (((0,), (0,)), ((), ()))
MB = 1 << 20


def layer_norm(v):
    v = v.astype(F32)
    centered = v - jnp.mean(v, axis=-1, keepdims=True)
    variance = jnp.mean(centered * centered, axis=-1, keepdims=True)
    return centered * lax.rsqrt(variance + EPS)


def low_lanes(shape):
    return lax.broadcasted_iota(jnp.int32, shape, len(shape) - 1) < 64


def mix(first, second):
    keep = low_lanes(first.shape)
    turn = len(first.shape) - 1
    return (
        jnp.where(keep, first, pltpu.roll(second, 64, turn)),
        jnp.where(keep, pltpu.roll(first, 64, turn), second),
    )


def params(mib):
    return pltpu.CompilerParams(vmem_limit_bytes=mib * MB)


def bias_kernel(pair_ref, weight_ref, out_ref):
    heads = weight_ref.shape[0]
    for u in range(16):
        block = jnp.concatenate([pair_ref[u], pair_ref[16 + u]], axis=0)
        normed = layer_norm(block).astype(BF16)
        out_ref[:, u, :] = lax.dot_general(
            weight_ref[...], normed, NT, preferred_element_type=F32
        ).astype(out_ref.dtype)


def pair_bias(pairwise, weight):
    heads = weight.shape[0]
    return pl.pallas_call(
        bias_kernel,
        out_shape=jax.ShapeDtypeStruct((heads, 16, 128), F32),
        compiler_params=params(16),
        name="pair_bias",
    )(pairwise, weight)


def attention_kernel(
    core_ref,
    seq_ref,
    own_ref,
    other_ref,
    x_ref,
    win_ref,
    wo_ref,
    wl_ref,
    wr_ref,
    live_ref,
    live_col_ref,
    out_ref,
    left_ref,
    right_ref,
    bias_ref,
    q_ref,
    k_ref,
    v_ref,
    acc_ref,
):
    heads = bias_ref.shape[0]
    step = pl.program_id(0)

    @pl.when(step == 0)
    def _():
        penalty = (live_ref[...] - 1.0) * BIG

        def assemble(xz, carry):
            for ref, core in ((own_ref, core_ref[0]), (other_ref, 1 - core_ref[0])):
                base = pl.multiple_of((xz * 2 + core) * 32, 32)
                for h in range(heads):
                    for m in range(4):
                        even = ref[xz * 8 + 2 * m, 16 * h : 16 * h + 16, :].astype(F32)
                        odd = ref[xz * 8 + 2 * m + 1, 16 * h : 16 * h + 16, :].astype(F32)
                        low, high = mix(even, odd)
                        pen = penalty[:, 128 * m : 128 * m + 128]
                        bias_ref[h, pl.ds(base, 16), 128 * m : 128 * m + 128] = low + pen
                        bias_ref[h, pl.ds(base + 16, 16), 128 * m : 128 * m + 128] = high + pen
            return carry

        lax.fori_loop(0, 8, assemble, 0)

    x = x_ref[:, 0].reshape(512, 256)
    normed = layer_norm(x).astype(BF16)

    def project(t):
        return jnp.dot(normed, win_ref[:, 256 * t : 256 * t + 256], preferred_element_type=F32)

    q_ref[...] = (project(0) * 32 ** (-0.5)).astype(BF16)
    k_ref[...] = project(1).astype(BF16)
    v_ref[...] = project(2).astype(BF16)
    acc_ref[...] = jnp.zeros_like(acc_ref)
    lane_head = lax.broadcasted_iota(jnp.int32, (512, 256), 1) // 32

    def head(h, carry):
        mine = lane_head == h
        k_h = jnp.where(mine, k_ref[...], jnp.zeros((), BF16))
        v_h = jnp.where(mine, v_ref[...], jnp.zeros((), BF16))
        for t in range(2):
            rows = slice(256 * t, 256 * t + 256)
            s = lax.dot_general(q_ref[rows], k_h, NT, preferred_element_type=F32)
            s = s + bias_ref[h, rows, :]
            p = jnp.exp(s - jnp.max(s, axis=-1, keepdims=True))
            total = jnp.sum(p, axis=-1, keepdims=True)
            o = jnp.dot(p.astype(BF16), v_h, preferred_element_type=F32)
            acc_ref[rows] += o * (1.0 / total)
        return carry

    lax.fori_loop(0, heads, head, 0)
    gate = jax.nn.sigmoid(project(3))
    attended = (acc_ref[...] * gate).astype(BF16)
    out = (
        x.astype(F32) + jnp.dot(attended, wo_ref[...], preferred_element_type=F32)
    ).astype(BF16)
    out_ref[:, 0] = out.reshape(16, 32, 256)
    second = layer_norm(out).astype(BF16)
    seq_live = seq_ref[step]
    left = jnp.dot(second, wl_ref[...], preferred_element_type=F32)
    left = (left * (live_col_ref[...] * seq_live)).reshape(16, 4, 8, 128)
    group = lax.broadcasted_iota(jnp.int32, (16, 8, 128), 2) // 32
    packed = left[:, 0]
    for q in range(1, 4):
        packed = jnp.where(group == q, left[:, q], packed)
    left_ref[:, 0] = packed.astype(BF16)
    right = lax.dot_general(wr_ref[...], second, NT, preferred_element_type=F32)
    right = right * (live_ref[...] * seq_live)
    for m in range(4):
        tile = right[:, 128 * m : 128 * m + 128]
        even, odd = mix(tile[:16], tile[16:])
        right_ref[2 * m, 0] = even.astype(BF16)
        right_ref[2 * m + 1, 0] = odd.astype(BF16)


def attention(core, seq_live, own, other, x, win, wo, wl, wr, live, live_col):
    count = x.shape[1]
    smem = pl.BlockSpec(memory_space=pltpu.SMEM)

    def whole(a):
        return pl.BlockSpec(a.shape, lambda s: (0,) * a.ndim)

    def per_seq(*dims):
        return pl.BlockSpec(dims, lambda s: (0, s) + (0,) * (len(dims) - 2))

    return pl.pallas_call(
        attention_kernel,
        grid=(count,),
        in_specs=[
            smem,
            smem,
            whole(own),
            whole(other),
            per_seq(16, 1, 32, 256),
            whole(win),
            whole(wo),
            whole(wl),
            whole(wr),
            whole(live),
            whole(live_col),
        ],
        out_specs=[
            per_seq(16, 1, 32, 256),
            per_seq(16, 1, 8, 128),
            per_seq(8, 1, 16, 128),
        ],
        out_shape=[
            jax.ShapeDtypeStruct(x.shape, BF16),
            jax.ShapeDtypeStruct((16, count, 8, 128), BF16),
            jax.ShapeDtypeStruct((8, count, 16, 128), BF16),
        ],
        scratch_shapes=[
            pltpu.VMEM((8, 512, 512), F32),
            pltpu.VMEM((512, 256), BF16),
            pltpu.VMEM((512, 256), BF16),
            pltpu.VMEM((512, 256), BF16),
            pltpu.VMEM((512, 256), F32),
        ],
        compiler_params=params(48),
        name="row_attention",
    )(core, seq_live, own, other, x, win, wo, wl, wr, live, live_col)


def outer_kernel(l_ref, r_ref, w_ref, inv_ref, plane_ref, pair_ref, wp_ref, mid_ref, tri_ref, x_ref):
    product = lax.dot_general(l_ref[...], r_ref[...], TN, preferred_element_type=F32)
    for half in range(2):
        for u in range(16):
            first = product[32 * half : 32 * half + 32, 128 * u : 128 * u + 128]
            second = product[32 * half + 64 : 32 * half + 96, 128 * u : 128 * u + 128]
            low, high = mix(first, second)
            columns = slice(128 * half, 128 * half + 128)
            x_ref[64 * u : 64 * u + 32, columns] = low.astype(BF16)
            x_ref[64 * u + 32 : 64 * u + 64, columns] = high.astype(BF16)
    update = jnp.dot(w_ref[...], x_ref[...], preferred_element_type=F32)
    for half in range(2):
        part = update[:, 128 * half : 128 * half + 128] * inv_ref[half, 0]
        before = jnp.concatenate([pair_ref[half, 0], pair_ref[half + 2, 0]], axis=0)
        mid = (before.astype(F32) + part.T).astype(BF16)
        mid_ref[half, 0] = mid[:64]
        mid_ref[half + 2, 0] = mid[64:]
        normed = layer_norm(mid).astype(BF16)
        terms = lax.dot_general(wp_ref[...], normed, NT, preferred_element_type=F32)
        plane = plane_ref[half, 0]
        tri_ref[half, 0, :128] = (jax.nn.sigmoid(terms[:128]) * terms[128:256] * plane).astype(BF16)
        tri_ref[half, 0, 128:] = (jax.nn.sigmoid(terms[256:384]) * terms[384:] * plane).astype(BF16)


def outer_update(left, right, weight, inv, plane, pairwise, wp):
    total = left.shape[0]

    def whole(a):
        return pl.BlockSpec(a.shape, lambda v: (0,) * a.ndim)

    def by_v(*dims):
        return pl.BlockSpec(dims, lambda v: (0, v) + (0,) * (len(dims) - 2))

    return pl.pallas_call(
        outer_kernel,
        grid=(8,),
        in_specs=[
            by_v(total, 128),
            whole(right),
            whole(weight),
            by_v(2, 1, 1, 128),
            by_v(2, 1, 1, 128),
            by_v(4, 1, 64, 128),
            whole(wp),
        ],
        out_specs=[by_v(4, 1, 64, 128), by_v(2, 1, 256, 128)],
        out_shape=[
            jax.ShapeDtypeStruct((4, 8, 64, 128), BF16),
            jax.ShapeDtypeStruct((2, 8, 256, 128), BF16),
        ],
        scratch_shapes=[pltpu.VMEM((1024, 256), BF16)],
        compiler_params=params(32),
        name="outer_update",
    )(left, right, weight, inv, plane, pairwise, wp)


def triangle_kernel(in_ref, out_ref, a_ref, b_ref):
    def assemble(r, carry):
        base = pl.multiple_of(r * 32, 32)
        for t, ref in ((0, a_ref), (1, b_ref)):
            for m in range(4):
                low, high = mix(
                    in_ref[r * 8 + 2 * m, t].astype(F32), in_ref[r * 8 + 2 * m + 1, t].astype(F32)
                )
                ref[pl.ds(base, 16), 128 * m : 128 * m + 128] = low.astype(BF16)
                ref[pl.ds(base + 16, 16), 128 * m : 128 * m + 128] = high.astype(BF16)
        return carry

    lax.fori_loop(0, 16, assemble, 0)

    def multiply(g, carry):
        base = pl.multiple_of(g * 128, 128)
        c = lax.dot_general(a_ref[pl.ds(base, 128), :], b_ref[...], NT, preferred_element_type=F32)
        for part in range(4):
            for m in range(4):
                columns = slice(128 * m, 128 * m + 128)
                even, odd = mix(
                    c[32 * part : 32 * part + 16, columns], c[32 * part + 16 : 32 * part + 32, columns]
                )
                out_ref[(g * 4 + part) * 8 + 2 * m] = even.astype(BF16)
                out_ref[(g * 4 + part) * 8 + 2 * m + 1] = odd.astype(BF16)
        return carry

    lax.fori_loop(0, 4, multiply, 0)


def triangle(blocks):
    return pl.pallas_call(
        triangle_kernel,
        out_shape=jax.ShapeDtypeStruct((128, 16, 128), BF16),
        scratch_shapes=[pltpu.VMEM((512, 512), BF16), pltpu.VMEM((512, 512), BF16)],
        compiler_params=params(16),
        name="triangle",
    )(blocks)


def final_kernel(tri_ref, mid_ref, wt_ref, wg_ref, out_ref):
    for u in range(16):
        combined = tri_ref[u].astype(F32)
        centered = combined - jnp.mean(combined, axis=0, keepdims=True)
        variance = jnp.mean(centered * centered, axis=0, keepdims=True)
        normed = (centered * lax.rsqrt(variance + EPS)).astype(BF16)
        update = jnp.dot(wt_ref[...], normed, preferred_element_type=F32)
        mid = jnp.concatenate([mid_ref[u], mid_ref[16 + u]], axis=0)
        gate = jax.nn.sigmoid(
            jnp.dot(layer_norm(mid).astype(BF16), wg_ref[...], preferred_element_type=F32)
        )
        out = (mid.astype(F32) + gate * update.T).astype(BF16)
        out_ref[u] = out[:64]
        out_ref[16 + u] = out[64:]


def final(tri, mid, wt, wg):
    return pl.pallas_call(
        final_kernel,
        out_shape=jax.ShapeDtypeStruct((32, 64, 128), BF16),
        compiler_params=params(16),
        name="pair_final",
    )(tri, mid, wt, wg)


def body(
    alignment,
    pairwise,
    residue_mask,
    sequence_mask,
    attention_input_weight,
    attention_output_weight,
    bias_project,
    outer_factor_weight,
    outer_output,
    tri_project,
    tri_gate,
    tri_output,
):
    row = lax.axis_index(ROW)
    col = lax.axis_index(COL)
    core = lax.axis_index("core")
    swap = [(0, 1), (1, 0)]
    res_live = residue_mask.astype(F32)
    seq_live = sequence_mask.astype(F32)
    row_live = lax.dynamic_slice_in_dim(res_live, row * 32, 32)
    col_live = lax.dynamic_slice_in_dim(res_live, col * 64, 64)
    my_seqs = lax.dynamic_slice_in_dim(seq_live, col * 80 + row * 5, 5)

    bias = pair_bias(pairwise, bias_project.T).astype(BF16).reshape(128, 128)
    bias_own = lax.all_to_all(
        jnp.broadcast_to(bias, (64, 128, 128)), CHIP, split_axis=0, concat_axis=0, tiled=True
    )
    sequences = lax.all_to_all(
        alignment.reshape(16, 5, 32, 256), ROW, split_axis=0, concat_axis=0, tiled=True
    )
    bias_other = lax.ppermute(bias_own, "core", swap)
    out_seq, left, right = attention(
        core.reshape(1),
        my_seqs,
        bias_own,
        bias_other,
        sequences,
        attention_input_weight.reshape(256, 1024),
        attention_output_weight,
        jnp.tile(outer_factor_weight[:, 0], (1, 4)),
        outer_factor_weight[:, 1].T,
        res_live.reshape(1, 512),
        jnp.broadcast_to(res_live[:, None], (512, 128)),
    )
    right_own = lax.all_to_all(
        jnp.broadcast_to(right[None], (8, 8, 5, 16, 128)).reshape(64, 80, 128),
        CHIP,
        split_axis=0,
        concat_axis=0,
        tiled=True,
    )
    left_all = lax.all_to_all(
        jnp.broadcast_to(left[:, None], (16, 8, 5, 8, 128)).reshape(128, 40, 128),
        ALL,
        split_axis=0,
        concat_axis=0,
        tiled=True,
    )
    right_other = lax.ppermute(right_own, "core", swap)
    left_all = left_all.reshape(8, 2, 320 // 8, 1024)
    left_own = lax.dynamic_index_in_dim(left_all, core, 1, keepdims=False)
    left_other = lax.dynamic_index_in_dim(left_all, 1 - core, 1, keepdims=False)
    left_cat = jnp.concatenate([left_own, left_other], axis=0).reshape(640, 1024)
    right_cat = jnp.concatenate([right_own, right_other], axis=0).reshape(640, 2048)
    alignment_output = lax.all_to_all(
        out_seq, ROW, split_axis=0, concat_axis=0, tiled=True
    ).reshape(80, 32, 256)

    plane = row_live[:, None] * col_live[None, :]
    inv = 1.0 / jnp.maximum(jnp.sum(seq_live) * plane, 1.0)

    def pairs(a):
        return a.reshape(2, 16, 64).transpose(1, 0, 2).reshape(2, 8, 1, 128)

    weight = outer_output.reshape(32, 2, 16, 128).transpose(3, 2, 1, 0).reshape(128, 1024)
    mid, tri = outer_update(
        left_cat,
        right_cat,
        weight,
        pairs(inv),
        pairs(plane),
        pairwise.reshape(4, 8, 64, 128),
        tri_project.reshape(128, 512).T,
    )
    tri = tri.reshape(16, 2, 128, 128).transpose(2, 1, 0, 3)
    blocks = lax.all_to_all(tri, ALL, split_axis=0, concat_axis=0, tiled=True)
    combined = lax.all_to_all(triangle(blocks), ALL, split_axis=0, concat_axis=0, tiled=True)
    pair_output_state = final(
        combined.transpose(1, 0, 2), mid.reshape(32, 64, 128), tri_output.T, tri_gate
    )
    return (alignment_output, pair_output_state)


def solution(mesh):
    fine = Mesh(mesh.devices.reshape(4, 2, 2, 2, 4), ALL)
    placed = (P(COL, ROW, None), P(ROW, COL, None)) + (P(),) * 10
    return jax.shard_map(
        body,
        mesh=fine,
        in_specs=placed,
        out_specs=(P(COL, ROW, None), P(ROW, COL, None)),
        check_vma=False,
    )
```

```python
import jax
import jax.numpy as jnp
from jax import lax
from jax.experimental import pallas as pl
from jax.experimental.pallas import tpu as pltpu
from jax.sharding import Mesh, PartitionSpec as P

EPS = 1e-05
BIG = 1000000000.0
F32 = jnp.float32
BF16 = jnp.bfloat16
ROW = ("x", "zl", "core")
COL = ("zh", "y")
ALL = ROW + COL
CHIP = ("x", "zl", "zh", "y")
NT = (((1,), (1,)), ((), ()))
TN = (((0,), (0,)), ((), ()))
MB = 1 << 20


def layer_norm(v):
    v = v.astype(F32)
    centered = v - jnp.mean(v, axis=-1, keepdims=True)
    variance = jnp.mean(centered * centered, axis=-1, keepdims=True)
    return centered * lax.rsqrt(variance + EPS)


def low_lanes(shape):
    return lax.broadcasted_iota(jnp.int32, shape, len(shape) - 1) < 64


def mix(first, second):
    keep = low_lanes(first.shape)
    turn = len(first.shape) - 1
    return (
        jnp.where(keep, first, pltpu.roll(second, 64, turn)),
        jnp.where(keep, pltpu.roll(first, 64, turn), second),
    )


def params(mib):
    return pltpu.CompilerParams(vmem_limit_bytes=mib * MB)


def bias_kernel(pair_ref, weight_ref, out_ref):
    heads = weight_ref.shape[0]
    for u in range(16):
        block = jnp.concatenate([pair_ref[u], pair_ref[16 + u]], axis=0)
        normed = layer_norm(block).astype(BF16)
        out_ref[:, u, :] = lax.dot_general(
            weight_ref[...], normed, NT, preferred_element_type=F32
        ).astype(out_ref.dtype)


def pair_bias(pairwise, weight):
    heads = weight.shape[0]
    return pl.pallas_call(
        bias_kernel,
        out_shape=jax.ShapeDtypeStruct((heads, 16, 128), F32),
        compiler_params=params(16),
        name="pair_bias",
    )(pairwise, weight)


def attention_kernel(
    place_ref,
    seq_ref,
    own0_ref,
    own1_ref,
    own2_ref,
    own3_ref,
    other0_ref,
    other1_ref,
    other2_ref,
    other3_ref,
    x_ref,
    win_ref,
    wo_ref,
    wl_ref,
    wr_ref,
    live_ref,
    live_col_ref,
    out_ref,
    factor_ref,
    bias_ref,
    q_ref,
    k_ref,
    v_ref,
    acc_ref,
    penalty_ref,
):
    heads = bias_ref.shape[0]
    step = pl.program_id(0)

    @pl.when(step == 0)
    def _():
        penalty = (live_ref[...] - 1.0) * BIG
        own = (own0_ref, own1_ref, own2_ref, own3_ref)
        other = (other0_ref, other1_ref, other2_ref, other3_ref)
        core, y = place_ref[0], place_ref[1]

        def assemble(pairs):
            def at_chips(xz, carry):
                for refs, side in ((own, core), (other, 1 - core)):
                    base = pl.multiple_of((xz * 2 + side) * 32, 32)
                    for even_at, odd_at in pairs:
                        y_even = lax.rem(y + 4 - even_at, 4)
                        for zh in range(2):
                            lanes = pl.ds(pl.multiple_of((zh * 2 + y_even // 2) * 128, 128), 128)
                            pen = penalty_ref[:, lanes]
                            for h in range(heads):
                                rows = slice(16 * h, 16 * h + 16)
                                low, high = mix(
                                    refs[even_at][xz * 2 + zh, rows, :].astype(F32),
                                    refs[odd_at][xz * 2 + zh, rows, :].astype(F32),
                                )
                                bias_ref[h, pl.ds(base, 16), lanes] = low + pen
                                bias_ref[h, pl.ds(base + 16, 16), lanes] = high + pen
                return carry

            lax.fori_loop(0, 8, at_chips, 0)

        penalty_ref[...] = penalty

        @pl.when(lax.rem(y, 2) == 0)
        def _():
            assemble(((0, 3), (2, 1)))

        @pl.when(lax.rem(y, 2) == 1)
        def _():
            assemble(((1, 0), (3, 2)))

    x = x_ref[:, 0].reshape(512, 256)
    normed = layer_norm(x).astype(BF16)

    def project(t):
        return jnp.dot(normed, win_ref[:, 256 * t : 256 * t + 256], preferred_element_type=F32)

    q_ref[...] = (project(0) * 32 ** (-0.5)).astype(BF16)
    k_ref[...] = project(1).astype(BF16)
    v_ref[...] = project(2).astype(BF16)
    acc_ref[...] = jnp.zeros_like(acc_ref)
    lane_head = lax.broadcasted_iota(jnp.int32, (512, 256), 1) // 32

    def head(h, carry):
        mine = lane_head == h
        k_h = jnp.where(mine, k_ref[...], jnp.zeros((), BF16))
        v_h = jnp.where(mine, v_ref[...], jnp.zeros((), BF16))
        for t in range(2):
            rows = slice(256 * t, 256 * t + 256)
            s = lax.dot_general(q_ref[rows], k_h, NT, preferred_element_type=F32)
            s = s + bias_ref[h, rows, :]
            p = jnp.exp(s - jnp.max(s, axis=-1, keepdims=True))
            total = jnp.sum(p, axis=-1, keepdims=True)
            o = jnp.dot(p.astype(BF16), v_h, preferred_element_type=F32)
            acc_ref[rows] += o * (1.0 / total)
        return carry

    lax.fori_loop(0, heads, head, 0)
    gate = jax.nn.sigmoid(project(3))
    attended = (acc_ref[...] * gate).astype(BF16)
    out = (
        x.astype(F32) + jnp.dot(attended, wo_ref[...], preferred_element_type=F32)
    ).astype(BF16)
    out_ref[:, 0] = out.reshape(16, 32, 256)
    second = layer_norm(out).astype(BF16)
    seq_live = seq_ref[step]
    left = jnp.dot(second, wl_ref[...], preferred_element_type=F32)
    left = (left * (live_col_ref[...] * seq_live)).reshape(16, 4, 8, 128)
    group = lax.broadcasted_iota(jnp.int32, (16, 8, 128), 2) // 32
    packed = left[:, 0]
    for q in range(1, 4):
        packed = jnp.where(group == q, left[:, q], packed)
    right = lax.dot_general(wr_ref[...], second, NT, preferred_element_type=F32)
    right = right * (live_ref[...] * seq_live)
    for m in range(4):
        tile = right[:, 128 * m : 128 * m + 128]
        for c, chunk in enumerate(mix(tile[:16], tile[16:])):
            for core in range(2):
                half = chunk[8 * core : 8 * core + 8]
                for xz in range(8):
                    factor_ref[xz, core, 2 * m + c, 0] = jnp.concatenate(
                        [packed[2 * xz + core], half], axis=0
                    ).astype(BF16)


def attention(place, seq_live, biases, x, win, wo, wl, wr, live, live_col):
    count = x.shape[1]
    smem = pl.BlockSpec(memory_space=pltpu.SMEM)

    def whole(a):
        return pl.BlockSpec(a.shape, lambda s: (0,) * a.ndim)

    def per_seq(*dims):
        return pl.BlockSpec(dims, lambda s: (0, s) + (0,) * (len(dims) - 2))

    return pl.pallas_call(
        attention_kernel,
        grid=(count,),
        in_specs=[
            smem,
            smem,
            *(whole(b) for b in biases),
            per_seq(16, 1, 32, 256),
            whole(win),
            whole(wo),
            whole(wl),
            whole(wr),
            whole(live),
            whole(live_col),
        ],
        out_specs=[
            per_seq(16, 1, 32, 256),
            pl.BlockSpec((8, 2, 8, 1, 16, 128), lambda s: (0, 0, 0, s, 0, 0)),
        ],
        out_shape=[
            jax.ShapeDtypeStruct(x.shape, BF16),
            jax.ShapeDtypeStruct((8, 2, 8, count, 16, 128), BF16),
        ],
        scratch_shapes=[
            pltpu.VMEM((8, 512, 512), F32),
            pltpu.VMEM((512, 256), BF16),
            pltpu.VMEM((512, 256), BF16),
            pltpu.VMEM((512, 256), BF16),
            pltpu.VMEM((512, 256), F32),
            pltpu.VMEM((1, 512), F32),
        ],
        compiler_params=params(48),
        name="row_attention",
    )(place, seq_live, *biases, x, win, wo, wl, wr, live, live_col)


def outer_kernel(core_ref, l_ref, own_ref, other_ref, w_ref, inv_ref, plane_ref, pair_ref, wp_ref, mid_ref, tri_ref, x_ref):
    for ref, core in ((own_ref, core_ref[0]), (other_ref, 1 - core_ref[0])):
        product = lax.dot_general(l_ref[...], ref[...], TN, preferred_element_type=F32)
        for half in range(2):
            columns = slice(128 * half, 128 * half + 128)
            for u in range(8):
                first = product[32 * half : 32 * half + 32, 128 * u : 128 * u + 128]
                second = product[32 * half + 64 : 32 * half + 96, 128 * u : 128 * u + 128]
                low, high = mix(first, second)
                base = pl.multiple_of(core * 512 + 64 * u, 64)
                x_ref[pl.ds(base, 32), columns] = low.astype(BF16)
                x_ref[pl.ds(base + 32, 32), columns] = high.astype(BF16)
    update = jnp.dot(w_ref[...], x_ref[...], preferred_element_type=F32)
    for half in range(2):
        part = update[:, 128 * half : 128 * half + 128] * inv_ref[half, 0]
        before = jnp.concatenate([pair_ref[half, 0], pair_ref[half + 2, 0]], axis=0)
        mid = (before.astype(F32) + part.T).astype(BF16)
        mid_ref[half, 0] = mid[:64]
        mid_ref[half + 2, 0] = mid[64:]
        normed = layer_norm(mid).astype(BF16)
        terms = lax.dot_general(wp_ref[...], normed, NT, preferred_element_type=F32)
        plane = plane_ref[half, 0]
        tri_ref[half, 0, :128] = (jax.nn.sigmoid(terms[:128]) * terms[128:256] * plane).astype(BF16)
        tri_ref[half, 0, 128:] = (jax.nn.sigmoid(terms[256:384]) * terms[384:] * plane).astype(BF16)


def outer_update(core, left, own, other, weight, inv, plane, pairwise, wp):
    total = left.shape[0]

    def whole(a):
        return pl.BlockSpec(a.shape, lambda v: (0,) * a.ndim)

    def by_v(*dims):
        return pl.BlockSpec(dims, lambda v: (0, v) + (0,) * (len(dims) - 2))

    return pl.pallas_call(
        outer_kernel,
        grid=(8,),
        in_specs=[
            pl.BlockSpec(memory_space=pltpu.SMEM),
            by_v(total, 128),
            whole(own),
            whole(other),
            whole(weight),
            by_v(2, 1, 1, 128),
            by_v(2, 1, 1, 128),
            by_v(4, 1, 64, 128),
            whole(wp),
        ],
        out_specs=[by_v(4, 1, 64, 128), by_v(2, 1, 256, 128)],
        out_shape=[
            jax.ShapeDtypeStruct((4, 8, 64, 128), BF16),
            jax.ShapeDtypeStruct((2, 8, 256, 128), BF16),
        ],
        scratch_shapes=[pltpu.VMEM((1024, 256), BF16)],
        compiler_params=params(32),
        name="outer_update",
    )(core, left, own, other, weight, inv, plane, pairwise, wp)


def triangle_kernel(in_ref, out_ref, a_ref, b_ref):
    def assemble(r, carry):
        base = pl.multiple_of(r * 32, 32)
        for t, ref in ((0, a_ref), (1, b_ref)):
            for m in range(4):
                low, high = mix(
                    in_ref[r * 8 + 2 * m, t].astype(F32), in_ref[r * 8 + 2 * m + 1, t].astype(F32)
                )
                ref[pl.ds(base, 16), 128 * m : 128 * m + 128] = low.astype(BF16)
                ref[pl.ds(base + 16, 16), 128 * m : 128 * m + 128] = high.astype(BF16)
        return carry

    lax.fori_loop(0, 16, assemble, 0)

    def multiply(g, carry):
        base = pl.multiple_of(g * 128, 128)
        c = lax.dot_general(a_ref[pl.ds(base, 128), :], b_ref[...], NT, preferred_element_type=F32)
        for part in range(4):
            for m in range(4):
                columns = slice(128 * m, 128 * m + 128)
                even, odd = mix(
                    c[32 * part : 32 * part + 16, columns], c[32 * part + 16 : 32 * part + 32, columns]
                )
                out_ref[(g * 4 + part) * 8 + 2 * m] = even.astype(BF16)
                out_ref[(g * 4 + part) * 8 + 2 * m + 1] = odd.astype(BF16)
        return carry

    lax.fori_loop(0, 4, multiply, 0)


def triangle(blocks):
    return pl.pallas_call(
        triangle_kernel,
        out_shape=jax.ShapeDtypeStruct((128, 16, 128), BF16),
        scratch_shapes=[pltpu.VMEM((512, 512), BF16), pltpu.VMEM((512, 512), BF16)],
        compiler_params=params(16),
        name="triangle",
    )(blocks)


def final_kernel(tri_ref, mid_ref, wt_ref, wg_ref, out_ref):
    for u in range(16):
        combined = tri_ref[u].astype(F32)
        centered = combined - jnp.mean(combined, axis=0, keepdims=True)
        variance = jnp.mean(centered * centered, axis=0, keepdims=True)
        normed = (centered * lax.rsqrt(variance + EPS)).astype(BF16)
        update = jnp.dot(wt_ref[...], normed, preferred_element_type=F32)
        mid = jnp.concatenate([mid_ref[u], mid_ref[16 + u]], axis=0)
        gate = jax.nn.sigmoid(
            jnp.dot(layer_norm(mid).astype(BF16), wg_ref[...], preferred_element_type=F32)
        )
        out = (mid.astype(F32) + gate * update.T).astype(BF16)
        out_ref[u] = out[:64]
        out_ref[16 + u] = out[64:]


def final(tri, mid, wt, wg):
    return pl.pallas_call(
        final_kernel,
        out_shape=jax.ShapeDtypeStruct((32, 64, 128), BF16),
        compiler_params=params(16),
        name="pair_final",
    )(tri, mid, wt, wg)


def body(
    alignment,
    pairwise,
    residue_mask,
    sequence_mask,
    attention_input_weight,
    attention_output_weight,
    bias_project,
    outer_factor_weight,
    outer_output,
    tri_project,
    tri_gate,
    tri_output,
):
    row = lax.axis_index(ROW)
    col = lax.axis_index(COL)
    core = lax.axis_index("core")
    swap = [(0, 1), (1, 0)]
    res_live = residue_mask.astype(F32)
    seq_live = sequence_mask.astype(F32)
    row_live = lax.dynamic_slice_in_dim(res_live, row * 32, 32)
    col_live = lax.dynamic_slice_in_dim(res_live, col * 64, 64)
    my_seqs = lax.dynamic_slice_in_dim(seq_live, col * 80 + row * 5, 5)

    bias = pair_bias(pairwise, bias_project.T).astype(BF16).reshape(128, 128)
    bias_plane = lax.all_to_all(
        jnp.broadcast_to(bias, (16, 128, 128)),
        ("x", "zl", "zh"),
        split_axis=0,
        concat_axis=0,
        tiled=True,
    )
    own = [bias_plane] + [
        lax.ppermute(bias_plane, "y", [(i, (i + d) % 4) for i in range(4)]) for d in (1, 2, 3)
    ]
    other = [lax.ppermute(b, "core", swap) for b in own]
    outgoing, bias_plane = lax.optimization_barrier(
        (alignment.reshape(16, 5, 32, 256), bias_plane)
    )
    sequences = lax.all_to_all(outgoing, ROW, split_axis=0, concat_axis=0, tiled=True)
    out_seq, factors = attention(
        jnp.stack([core, lax.axis_index("y")]),
        my_seqs,
        own + other,
        sequences,
        attention_input_weight.reshape(256, 1024),
        attention_output_weight,
        jnp.tile(outer_factor_weight[:, 0], (1, 4)),
        outer_factor_weight[:, 1].T,
        res_live.reshape(1, 512),
        jnp.broadcast_to(res_live[:, None], (512, 128)),
    )
    factors = lax.all_to_all(
        factors.reshape(128, 80, 128), ALL, split_axis=0, concat_axis=0, tiled=True
    )
    out_seq, factors = lax.optimization_barrier((out_seq, factors))
    factors = factors.reshape(640, 16, 128)
    right_own = factors[:, 8:].reshape(640, 1024)
    right_other = lax.ppermute(right_own, "core", swap)
    left = factors[:, :8].reshape(640, 1024)
    alignment_output = lax.all_to_all(
        out_seq, ROW, split_axis=0, concat_axis=0, tiled=True
    ).reshape(80, 32, 256)

    plane = row_live[:, None] * col_live[None, :]
    inv = 1.0 / jnp.maximum(jnp.sum(seq_live) * plane, 1.0)

    def pairs(a):
        return a.reshape(2, 16, 64).transpose(1, 0, 2).reshape(2, 8, 1, 128)

    weight = outer_output.reshape(32, 2, 16, 128).transpose(3, 2, 1, 0).reshape(128, 1024)
    mid, tri = outer_update(
        core.reshape(1),
        left,
        right_own,
        right_other,
        weight,
        pairs(inv),
        pairs(plane),
        pairwise.reshape(4, 8, 64, 128),
        tri_project.reshape(128, 512).T,
    )
    tri, alignment_output = lax.optimization_barrier((tri, alignment_output))
    tri = tri.reshape(16, 2, 128, 128).transpose(2, 1, 0, 3)
    blocks = lax.all_to_all(tri, ALL, split_axis=0, concat_axis=0, tiled=True)
    combined = lax.all_to_all(triangle(blocks), ALL, split_axis=0, concat_axis=0, tiled=True)
    pair_output_state = final(
        combined.transpose(1, 0, 2), mid.reshape(32, 64, 128), tri_output.T, tri_gate
    )
    return (alignment_output, pair_output_state)


def solution(mesh):
    fine = Mesh(mesh.devices.reshape(4, 2, 2, 2, 4), ALL)
    placed = (P(COL, ROW, None), P(ROW, COL, None)) + (P(),) * 10
    return jax.shard_map(
        body,
        mesh=fine,
        in_specs=placed,
        out_specs=(P(COL, ROW, None), P(ROW, COL, None)),
        check_vma=False,
    )
```

```python
import jax
import jax.numpy as jnp
from jax import lax
from jax.experimental import pallas as pl
from jax.experimental.pallas import tpu as pltpu
from jax.sharding import Mesh, PartitionSpec as P

EPS = 1e-05
BIG = 1000000000.0
LOG2E = 1.4426950408889634
F32 = jnp.float32
BF16 = jnp.bfloat16
ROW = ("x", "zl", "core")
COL = ("zh", "y")
ALL = ROW + COL
CHIP = ("x", "zl", "zh", "y")
NT = (((1,), (1,)), ((), ()))
TN = (((0,), (0,)), ((), ()))
MB = 1 << 20


def layer_norm(v):
    v = v.astype(F32)
    centered = v - jnp.mean(v, axis=-1, keepdims=True)
    variance = jnp.mean(centered * centered, axis=-1, keepdims=True)
    return centered * lax.rsqrt(variance + EPS)


def low_lanes(shape):
    return lax.broadcasted_iota(jnp.int32, shape, len(shape) - 1) < 64


def mix(first, second):
    keep = low_lanes(first.shape)
    turn = len(first.shape) - 1
    return (
        jnp.where(keep, first, pltpu.roll(second, 64, turn)),
        jnp.where(keep, pltpu.roll(first, 64, turn), second),
    )


def params(mib):
    return pltpu.CompilerParams(vmem_limit_bytes=mib * MB)


def bias_kernel(pair_ref, weight_ref, out_ref, normed_ref, bias_ref):
    normed_ref[...] = layer_norm(pair_ref[...])
    for w in range(16):
        block = jnp.concatenate([normed_ref[:, jq * 16 + w, :] for jq in range(4)], axis=0)
        bias_ref[:, w, :] = lax.dot_general(
            weight_ref[...], block.astype(BF16), NT, preferred_element_type=F32
        )
    for core in range(2):
        chunk = bias_ref[4 * core : 4 * core + 4].reshape(64, 128).astype(BF16)
        for xz in range(8):
            for zh in range(2):
                out_ref[xz, core, zh] = chunk


def pair_bias(pairwise, weight):
    return pl.pallas_call(
        bias_kernel,
        out_shape=jax.ShapeDtypeStruct((8, 2, 2, 64, 128), BF16),
        scratch_shapes=[pltpu.VMEM((32, 64, 128), F32), pltpu.VMEM((8, 16, 128), F32)],
        compiler_params=params(16),
        name="pair_bias",
    )(pairwise, weight)


def plane_kernel(in_ref, out_ref):
    group = lax.broadcasted_iota(jnp.int32, (16, 128), 1) // 32
    for zh in range(2):
        for hh in range(4):
            for x in range(4):
                parts = [
                    in_ref[(x * 4 + g) * 2 + zh, 16 * hh : 16 * hh + 16, :].astype(F32)
                    for g in range(4)
                ]
                for jq in range(4):
                    turned = [
                        part if g == jq else pltpu.roll(part, 32 * ((g - jq) % 4), 1)
                        for g, part in enumerate(parts)
                    ]
                    row = jnp.where(
                        group < 2,
                        jnp.where(group == 0, turned[0], turned[1]),
                        jnp.where(group == 2, turned[2], turned[3]),
                    )
                    base = 64 * zh + 16 * jq
                    out_ref[hh, base : base + 16, 128 * x : 128 * x + 128] = row.astype(BF16)


def plane(blocks):
    return pl.pallas_call(
        plane_kernel,
        out_shape=jax.ShapeDtypeStruct((4, 128, 512), BF16),
        compiler_params=params(8),
        name="bias_plane",
    )(blocks)


def attention_kernel(
    place_ref,
    seq_ref,
    own0_ref,
    own1_ref,
    own2_ref,
    own3_ref,
    other0_ref,
    other1_ref,
    other2_ref,
    other3_ref,
    x_ref,
    win_ref,
    wo_ref,
    wl_ref,
    wr_ref,
    live_ref,
    live_col_ref,
    out_ref,
    factor_ref,
    bias_ref,
    qt_ref,
    k_ref,
    vt_ref,
    acc_ref,
):
    heads = bias_ref.shape[0]
    step = pl.program_id(0)

    @pl.when(step == 0)
    def _():
        core, y = place_ref[0], place_ref[1]
        own = (own0_ref, own1_ref, own2_ref, own3_ref)
        other = (other0_ref, other1_ref, other2_ref, other3_ref)
        for refs, side in ((own, core), (other, 1 - core)):
            for d in range(4):
                source = lax.rem(y + 4 - d, 4)
                for zh in range(2):
                    rows = pl.ds(pl.multiple_of(256 * zh + 64 * source, 64), 64)
                    penalty = (live_col_ref[rows, :] - 1.0) * BIG
                    for m in range(4):
                        lanes = slice(128 * m, 128 * m + 128)
                        for hh in range(4):
                            bias_ref[4 * side + hh, rows, lanes] = (
                                refs[d][hh, 64 * zh : 64 * zh + 64, lanes].astype(F32) * LOG2E
                                + penalty
                            )

    x = x_ref[:, 0].reshape(512, 256)
    normed = layer_norm(x).astype(BF16)

    def project(t):
        return lax.dot_general(
            win_ref[256 * t : 256 * t + 256], normed, NT, preferred_element_type=F32
        )

    qt_ref[...] = (project(0) * (32 ** (-0.5) * LOG2E)).astype(BF16)
    k_ref[...] = lax.dot_general(
        normed, win_ref[256:512], NT, preferred_element_type=F32
    ).astype(BF16)
    vt_ref[:, :32] = project(2).astype(BF16).reshape(heads, 32, 512)
    vt_ref[:, 32:] = jnp.ones((heads, 16, 512), BF16)
    row_head = lax.broadcasted_iota(jnp.int32, (128, 512), 0) // 32
    for h in range(heads):
        lanes = slice(128 * (h // 4), 128 * (h // 4) + 128)
        q_h = jnp.where(row_head == h % 4, qt_ref[lanes, :], jnp.zeros((), BF16))
        s = jnp.dot(k_ref[:, lanes], q_h, preferred_element_type=F32) + bias_ref[h]
        p = jnp.exp2(s - jnp.max(s, axis=0, keepdims=True)).astype(BF16)
        o = jnp.dot(vt_ref[h], p, preferred_element_type=F32)
        acc_ref[32 * h : 32 * h + 32, :] = o[:32] / o[32:33]
    attended = (acc_ref[...] * jax.nn.sigmoid(project(3))).T.astype(BF16)
    out = (
        x.astype(F32) + jnp.dot(attended, wo_ref[...], preferred_element_type=F32)
    ).astype(BF16)
    out_ref[:, 0] = out.reshape(16, 32, 256)
    second = layer_norm(out).astype(BF16)
    seq_live = seq_ref[step]
    left = jnp.dot(second, wl_ref[...], preferred_element_type=F32)
    left = (left * (live_col_ref[...] * seq_live)).reshape(16, 4, 8, 128)
    group = lax.broadcasted_iota(jnp.int32, (16, 8, 128), 2) // 32
    packed = left[:, 0]
    for q in range(1, 4):
        packed = jnp.where(group == q, left[:, q], packed)
    right = lax.dot_general(wr_ref[...], second, NT, preferred_element_type=F32)
    right = right * (live_ref[...] * seq_live)
    for m in range(4):
        tile = right[:, 128 * m : 128 * m + 128]
        for c, chunk in enumerate(mix(tile[:16], tile[16:])):
            for core in range(2):
                half = chunk[8 * core : 8 * core + 8]
                for xz in range(8):
                    factor_ref[xz, core, 2 * m + c, 0] = jnp.concatenate(
                        [packed[2 * xz + core], half], axis=0
                    ).astype(BF16)


def attention(place, seq_live, biases, x, win, wo, wl, wr, live, live_col):
    count = x.shape[1]
    smem = pl.BlockSpec(memory_space=pltpu.SMEM)

    def whole(a):
        return pl.BlockSpec(a.shape, lambda s: (0,) * a.ndim)

    def per_seq(*dims):
        return pl.BlockSpec(dims, lambda s: (0, s) + (0,) * (len(dims) - 2))

    return pl.pallas_call(
        attention_kernel,
        grid=(count,),
        in_specs=[
            smem,
            smem,
            *(whole(b) for b in biases),
            per_seq(16, 1, 32, 256),
            whole(win),
            whole(wo),
            whole(wl),
            whole(wr),
            whole(live),
            whole(live_col),
        ],
        out_specs=[
            per_seq(16, 1, 32, 256),
            pl.BlockSpec((8, 2, 8, 1, 16, 128), lambda s: (0, 0, 0, s, 0, 0)),
        ],
        out_shape=[
            jax.ShapeDtypeStruct(x.shape, BF16),
            jax.ShapeDtypeStruct((8, 2, 8, count, 16, 128), BF16),
        ],
        scratch_shapes=[
            pltpu.VMEM((8, 512, 512), F32),
            pltpu.VMEM((256, 512), BF16),
            pltpu.VMEM((512, 256), BF16),
            pltpu.VMEM((8, 48, 512), BF16),
            pltpu.VMEM((256, 512), F32),
        ],
        compiler_params=params(48),
        name="row_attention",
    )(place, seq_live, *biases, x, win, wo, wl, wr, live, live_col)


def outer_kernel(
    core_ref,
    l_ref,
    own_ref,
    other_ref,
    w_ref,
    inv_ref,
    plane_ref,
    pair_ref,
    wp_ref,
    mid_ref,
    tri_ref,
    lt_ref,
    x_ref,
):
    step = pl.program_id(0)

    @pl.when(step == 0)
    def _():
        for v in range(8):
            rows = slice(128 * v, 128 * v + 128)
            lt_ref[rows, :] = l_ref[:, rows].astype(F32).T.astype(BF16)
        for ref, core in ((own_ref, core_ref[0]), (other_ref, 1 - core_ref[0])):

            def some(n, carry):
                lanes = pl.ds(pl.multiple_of(n * 256, 256), 256)
                product = jnp.dot(lt_ref[...], ref[:, lanes], preferred_element_type=F32)
                for k in range(2):
                    base = pl.multiple_of(core * 512 + n * 128 + 64 * k, 64)
                    for v in range(8):
                        for half in range(2):
                            at = 128 * v + 32 * half
                            low, high = mix(
                                product[at : at + 32, 128 * k : 128 * k + 128],
                                product[at + 64 : at + 96, 128 * k : 128 * k + 128],
                            )
                            columns = slice(128 * half, 128 * half + 128)
                            x_ref[v, pl.ds(base, 32), columns] = low.astype(BF16)
                            x_ref[v, pl.ds(base + 32, 32), columns] = high.astype(BF16)
                return carry

            lax.fori_loop(0, 4, some, 0)

    update = jnp.dot(w_ref[...], x_ref[step], preferred_element_type=F32)
    for half in range(2):
        part = update[:, 128 * half : 128 * half + 128] * inv_ref[half, 0]
        before = jnp.concatenate([pair_ref[half, 0], pair_ref[half + 2, 0]], axis=0)
        mid = (before.astype(F32) + part.T).astype(BF16)
        mid_ref[half, 0] = mid[:64]
        mid_ref[half + 2, 0] = mid[64:]
        normed = layer_norm(mid).astype(BF16)
        terms = lax.dot_general(wp_ref[...], normed, NT, preferred_element_type=F32)
        plane = plane_ref[half, 0]
        tri_ref[half, 0, :128] = (jax.nn.sigmoid(terms[:128]) * terms[128:256] * plane).astype(BF16)
        tri_ref[half, 0, 128:] = (jax.nn.sigmoid(terms[256:384]) * terms[384:] * plane).astype(BF16)


def outer_update(core, left, own, other, weight, inv, plane, pairwise, wp):
    total = left.shape[0]

    def whole(a):
        return pl.BlockSpec(a.shape, lambda v: (0,) * a.ndim)

    def by_v(*dims):
        return pl.BlockSpec(dims, lambda v: (0, v) + (0,) * (len(dims) - 2))

    return pl.pallas_call(
        outer_kernel,
        grid=(8,),
        in_specs=[
            pl.BlockSpec(memory_space=pltpu.SMEM),
            whole(left),
            whole(own),
            whole(other),
            whole(weight),
            by_v(2, 1, 1, 128),
            by_v(2, 1, 1, 128),
            by_v(4, 1, 64, 128),
            whole(wp),
        ],
        out_specs=[by_v(4, 1, 64, 128), by_v(2, 1, 256, 128)],
        out_shape=[
            jax.ShapeDtypeStruct((4, 8, 64, 128), BF16),
            jax.ShapeDtypeStruct((2, 8, 256, 128), BF16),
        ],
        scratch_shapes=[pltpu.VMEM((1024, total), BF16), pltpu.VMEM((8, 1024, 256), BF16)],
        compiler_params=params(32),
        name="outer_update",
    )(core, left, own, other, weight, inv, plane, pairwise, wp)


def triangle_kernel(in_ref, out_ref, a_ref, b_ref):
    def assemble(r, carry):
        base = pl.multiple_of(r * 32, 32)
        for t, ref in ((0, a_ref), (1, b_ref)):
            for m in range(4):
                low, high = mix(
                    in_ref[r * 8 + 2 * m, t].astype(F32), in_ref[r * 8 + 2 * m + 1, t].astype(F32)
                )
                ref[pl.ds(base, 16), 128 * m : 128 * m + 128] = low.astype(BF16)
                ref[pl.ds(base + 16, 16), 128 * m : 128 * m + 128] = high.astype(BF16)
        return carry

    lax.fori_loop(0, 16, assemble, 0)

    def multiply(g, carry):
        base = pl.multiple_of(g * 128, 128)
        c = lax.dot_general(a_ref[pl.ds(base, 128), :], b_ref[...], NT, preferred_element_type=F32)
        for part in range(4):
            for m in range(4):
                columns = slice(128 * m, 128 * m + 128)
                even, odd = mix(
                    c[32 * part : 32 * part + 16, columns], c[32 * part + 16 : 32 * part + 32, columns]
                )
                out_ref[(g * 4 + part) * 8 + 2 * m] = even.astype(BF16)
                out_ref[(g * 4 + part) * 8 + 2 * m + 1] = odd.astype(BF16)
        return carry

    lax.fori_loop(0, 4, multiply, 0)


def triangle(blocks):
    return pl.pallas_call(
        triangle_kernel,
        out_shape=jax.ShapeDtypeStruct((128, 16, 128), BF16),
        scratch_shapes=[pltpu.VMEM((512, 512), BF16), pltpu.VMEM((512, 512), BF16)],
        compiler_params=params(16),
        name="triangle",
    )(blocks)


def final_kernel(tri_ref, mid_ref, wt_ref, wg_ref, out_ref):
    for u in range(16):
        combined = tri_ref[u].astype(F32)
        centered = combined - jnp.mean(combined, axis=0, keepdims=True)
        variance = jnp.mean(centered * centered, axis=0, keepdims=True)
        normed = (centered * lax.rsqrt(variance + EPS)).astype(BF16)
        update = jnp.dot(wt_ref[...], normed, preferred_element_type=F32)
        mid = jnp.concatenate([mid_ref[u], mid_ref[16 + u]], axis=0)
        gate = jax.nn.sigmoid(
            jnp.dot(layer_norm(mid).astype(BF16), wg_ref[...], preferred_element_type=F32)
        )
        out = (mid.astype(F32) + gate * update.T).astype(BF16)
        out_ref[u] = out[:64]
        out_ref[16 + u] = out[64:]


def final(tri, mid, wt, wg):
    return pl.pallas_call(
        final_kernel,
        out_shape=jax.ShapeDtypeStruct((32, 64, 128), BF16),
        compiler_params=params(16),
        name="pair_final",
    )(tri, mid, wt, wg)


def copy_kernel(in_ref, out_ref):
    out_ref[...] = in_ref[...]


def copied(a):
    return pl.pallas_call(
        copy_kernel,
        out_shape=jax.ShapeDtypeStruct(a.shape, a.dtype),
        compiler_params=params(8),
        name="copied",
    )(a)


def body(
    alignment,
    pairwise,
    residue_mask,
    sequence_mask,
    attention_input_weight,
    attention_output_weight,
    bias_project,
    outer_factor_weight,
    outer_output,
    tri_project,
    tri_gate,
    tri_output,
):
    row = lax.axis_index(ROW)
    col = lax.axis_index(COL)
    core = lax.axis_index("core")
    swap = [(0, 1), (1, 0)]
    res_live = residue_mask.astype(F32)
    seq_live = sequence_mask.astype(F32)
    row_live = lax.dynamic_slice_in_dim(res_live, row * 32, 32)
    col_live = lax.dynamic_slice_in_dim(res_live, col * 64, 64)
    my_seqs = lax.dynamic_slice_in_dim(seq_live, col * 80 + row * 5, 5)

    blocks = lax.all_to_all(
        pair_bias(pairwise, bias_project.T).reshape(32, 64, 128),
        ROW + ("zh",),
        split_axis=0,
        concat_axis=0,
        tiled=True,
    )
    outgoing, blocks = lax.optimization_barrier((alignment.reshape(16, 5, 32, 256), blocks))
    bias_plane = plane(blocks)
    own = [bias_plane] + [
        lax.ppermute(bias_plane, "y", [(i, (i + d) % 4) for i in range(4)]) for d in (1, 2, 3)
    ]
    other = [lax.ppermute(b, "core", swap) for b in own]
    sequences = lax.all_to_all(outgoing, ROW, split_axis=0, concat_axis=0, tiled=True)
    live_plane = row_live[:, None] * col_live[None, :]
    inv = 1.0 / jnp.maximum(jnp.sum(seq_live) * live_plane, 1.0)

    def pairs(a):
        return a.reshape(2, 16, 64).transpose(1, 0, 2).reshape(2, 8, 1, 128)

    weight = outer_output.reshape(32, 2, 16, 128).transpose(3, 2, 1, 0).reshape(128, 1024)
    win = attention_input_weight.reshape(256, 1024).T
    wp = tri_project.reshape(128, 512).T
    wt = tri_output.T
    sequences, weight, wp, wt, inv, live_plane, win = lax.optimization_barrier(
        (sequences, weight, wp, wt, pairs(inv), pairs(live_plane), win)
    )
    out_seq, factors = attention(
        jnp.stack([core, lax.axis_index("y")]),
        my_seqs,
        own + other,
        sequences,
        win,
        attention_output_weight,
        jnp.tile(outer_factor_weight[:, 0], (1, 4)),
        outer_factor_weight[:, 1].T,
        res_live.reshape(1, 512),
        jnp.broadcast_to(res_live[:, None], (512, 128)),
    )
    factors = lax.all_to_all(
        factors.reshape(128, 80, 128), ALL, split_axis=0, concat_axis=0, tiled=True
    )
    out_seq, factors = lax.optimization_barrier((out_seq, factors))
    factors = factors.reshape(640, 16, 128)
    right_own = factors[:, 8:].reshape(640, 1024)
    right_other = lax.ppermute(right_own, "core", swap)
    left = factors[:, :8].reshape(640, 1024)
    alignment_output = lax.all_to_all(
        out_seq, ROW, split_axis=0, concat_axis=0, tiled=True
    ).reshape(80, 32, 256)

    mid, tri = outer_update(
        core.reshape(1),
        left,
        right_own,
        right_other,
        weight,
        inv,
        live_plane,
        pairwise.reshape(4, 8, 64, 128),
        wp,
    )
    tri, alignment_output = lax.optimization_barrier((tri, alignment_output))
    alignment_output = copied(alignment_output)
    tri = tri.reshape(16, 2, 128, 128).transpose(2, 1, 0, 3)
    blocks = lax.all_to_all(tri, ALL, split_axis=0, concat_axis=0, tiled=True)
    combined = lax.all_to_all(triangle(blocks), ALL, split_axis=0, concat_axis=0, tiled=True)
    pair_output_state = final(
        combined.transpose(1, 0, 2), mid.reshape(32, 64, 128), wt, tri_gate
    )
    return (alignment_output, pair_output_state)


def solution(mesh):
    fine = Mesh(mesh.devices.reshape(4, 2, 2, 2, 4), ALL)
    placed = (P(COL, ROW, None), P(ROW, COL, None)) + (P(),) * 10
    return jax.shard_map(
        body,
        mesh=fine,
        in_specs=placed,
        out_specs=(P(COL, ROW, None), P(ROW, COL, None)),
        check_vma=False,
    )
```

```python
import jax
import jax.numpy as jnp
from jax import lax
from jax.experimental import pallas as pl
from jax.experimental.pallas import tpu as pltpu
from jax.sharding import Mesh, PartitionSpec as P

EPS = 1e-05
BIG = 1000000000.0
LOG2E = 1.4426950408889634
F32 = jnp.float32
BF16 = jnp.bfloat16
ROW = ("x", "zl", "core")
COL = ("zh", "y")
ALL = ROW + COL
CHIP = ("x", "zl", "zh", "y")
NT = (((1,), (1,)), ((), ()))
TN = (((0,), (0,)), ((), ()))
MB = 1 << 20


def layer_norm(v):
    v = v.astype(F32)
    centered = v - jnp.mean(v, axis=-1, keepdims=True)
    variance = jnp.mean(centered * centered, axis=-1, keepdims=True)
    return centered * lax.rsqrt(variance + EPS)


def low_lanes(shape):
    return lax.broadcasted_iota(jnp.int32, shape, len(shape) - 1) < 64


def mix(first, second):
    keep = low_lanes(first.shape)
    turn = len(first.shape) - 1
    return (
        jnp.where(keep, first, pltpu.roll(second, 64, turn)),
        jnp.where(keep, pltpu.roll(first, 64, turn), second),
    )


def params(mib):
    return pltpu.CompilerParams(vmem_limit_bytes=mib * MB)


def bias_kernel(core_ref, pair_ref, weight_ref, own_ref, other_ref, normed_ref, bias_ref):
    normed_ref[...] = layer_norm(pair_ref[...])
    for w in range(16):
        block = jnp.concatenate([normed_ref[:, jq * 16 + w, :] for jq in range(4)], axis=0)
        bias_ref[:, w, :] = lax.dot_general(
            weight_ref[...], block.astype(BF16), NT, preferred_element_type=F32
        )
    core = core_ref[0]
    own_ref[...] = bias_ref[pl.ds(4 * core, 4)].reshape(64, 128).astype(BF16)
    other_ref[...] = bias_ref[pl.ds(4 - 4 * core, 4)].reshape(64, 128).astype(BF16)


def pair_bias(core, pairwise, weight):
    return pl.pallas_call(
        bias_kernel,
        in_specs=[
            pl.BlockSpec(memory_space=pltpu.SMEM),
            pl.BlockSpec(memory_space=pltpu.VMEM),
            pl.BlockSpec(memory_space=pltpu.VMEM),
        ],
        out_shape=[jax.ShapeDtypeStruct((64, 128), BF16)] * 2,
        scratch_shapes=[pltpu.VMEM((32, 64, 128), F32), pltpu.VMEM((8, 16, 128), F32)],
        compiler_params=params(16),
        name="pair_bias",
    )(core, pairwise, weight)


def plane_kernel(place_ref, d0_ref, d1_ref, d2_ref, d3_ref, out_ref):
    group = lax.broadcasted_iota(jnp.int32, (16, 128), 1) // 32
    x, zl, core, zh = (place_ref[k] for k in range(4))
    for d, ref in enumerate((d0_ref, d1_ref, d2_ref, d3_ref)):
        lanes = pl.ds(pl.multiple_of(lax.rem(x + 4 - d, 4) * 128, 128), 128)
        for at in range(2):
            for hh in range(4):
                parts = []
                for g in range(4):
                    far_zl = jnp.where(zl == g // 2, 0, 1)
                    far_core = jnp.where(core == g % 2, 0, 1)
                    far_zh = jnp.where(zh == at, 0, 1)
                    block = (far_zl * 2 + far_zh) * 2 + far_core
                    parts.append(ref[block, 16 * hh : 16 * hh + 16, :].astype(F32))
                for jq in range(4):
                    turned = [
                        part if g == jq else pltpu.roll(part, 32 * ((g - jq) % 4), 1)
                        for g, part in enumerate(parts)
                    ]
                    row = jnp.where(
                        group < 2,
                        jnp.where(group == 0, turned[0], turned[1]),
                        jnp.where(group == 2, turned[2], turned[3]),
                    )
                    base = 64 * at + 16 * jq
                    out_ref[hh, base : base + 16, lanes] = row.astype(BF16)


def plane(place, blocks):
    vmem = pl.BlockSpec(memory_space=pltpu.VMEM)
    return pl.pallas_call(
        plane_kernel,
        in_specs=[pl.BlockSpec(memory_space=pltpu.SMEM)] + [vmem] * 4,
        out_shape=jax.ShapeDtypeStruct((4, 128, 512), BF16),
        compiler_params=params(8),
        name="bias_plane",
    )(place, *blocks)


def project_kernel(x_ref, win_ref, qt_ref, k_ref, vt_ref, gate_ref):
    normed = layer_norm(x_ref[:, 0].reshape(512, 256)).astype(BF16)

    def project(t):
        return lax.dot_general(
            win_ref[256 * t : 256 * t + 256], normed, NT, preferred_element_type=F32
        )

    heads = vt_ref.shape[1]
    qt_ref[0] = (project(0) * (32 ** (-0.5) * LOG2E)).astype(BF16)
    k_ref[0] = lax.dot_general(normed, win_ref[256:512], NT, preferred_element_type=F32).astype(
        BF16
    )
    vt_ref[0, :, :32] = project(2).astype(BF16).reshape(heads, 32, 512)
    vt_ref[0, :, 32:] = jnp.ones((heads, 16, 512), BF16)
    gate_ref[0] = jax.nn.sigmoid(project(3))


def projections(x, win):
    count = x.shape[1]
    shapes = ((256, 512), (512, 256), (8, 48, 512), (256, 512))
    types = (BF16, BF16, BF16, F32)
    return pl.pallas_call(
        project_kernel,
        grid=(count,),
        in_specs=[
            pl.BlockSpec((16, 1, 32, 256), lambda s: (0, s, 0, 0)),
            pl.BlockSpec(win.shape, lambda s: (0, 0)),
        ],
        out_specs=[
            pl.BlockSpec((1,) + dims, lambda s, n=len(dims): (s,) + (0,) * n) for dims in shapes
        ],
        out_shape=[
            jax.ShapeDtypeStruct((count,) + dims, t) for dims, t in zip(shapes, types)
        ],
        compiler_params=params(24),
        name="projections",
    )(x, win)


def attention_kernel(
    place_ref,
    seq_ref,
    own0_ref,
    own1_ref,
    own2_ref,
    own3_ref,
    other0_ref,
    other1_ref,
    other2_ref,
    other3_ref,
    x_ref,
    qt_ref,
    k_ref,
    vt_ref,
    gate_ref,
    wo_ref,
    wl_ref,
    wr_ref,
    live_ref,
    live_col_ref,
    out_ref,
    factor_ref,
    bias_ref,
    acc_ref,
):
    heads = bias_ref.shape[0]
    step = pl.program_id(0)

    @pl.when(step == 0)
    def _():
        core, y = place_ref[0], place_ref[1]
        own = (own0_ref, own1_ref, own2_ref, own3_ref)
        other = (other0_ref, other1_ref, other2_ref, other3_ref)
        for refs, side in ((own, core), (other, 1 - core)):
            for d in range(4):
                source = lax.rem(y + 4 - d, 4)
                for zh in range(2):
                    rows = pl.ds(pl.multiple_of(256 * zh + 64 * source, 64), 64)
                    penalty = (live_col_ref[rows, :] - 1.0) * BIG
                    for m in range(4):
                        lanes = slice(128 * m, 128 * m + 128)
                        for hh in range(4):
                            bias_ref[4 * side + hh, rows, lanes] = (
                                refs[d][hh, 64 * zh : 64 * zh + 64, lanes].astype(F32) * LOG2E
                                + penalty
                            )

    x = x_ref[:, 0].reshape(512, 256)
    row_head = lax.broadcasted_iota(jnp.int32, (128, 512), 0) // 32
    for h in range(heads):
        lanes = slice(128 * (h // 4), 128 * (h // 4) + 128)
        q_h = jnp.where(row_head == h % 4, qt_ref[0, lanes, :], jnp.zeros((), BF16))
        s = jnp.dot(k_ref[0, :, lanes], q_h, preferred_element_type=F32) + bias_ref[h]
        p = jnp.exp2(s - jnp.max(s, axis=0, keepdims=True)).astype(BF16)
        o = jnp.dot(vt_ref[0, h], p, preferred_element_type=F32)
        acc_ref[32 * h : 32 * h + 32, :] = o[:32] / o[32:33]
    attended = (acc_ref[...] * gate_ref[0]).T.astype(BF16)
    out = (
        x.astype(F32) + jnp.dot(attended, wo_ref[...], preferred_element_type=F32)
    ).astype(BF16)
    out_ref[:, 0] = out.reshape(16, 32, 256)
    second = layer_norm(out).astype(BF16)
    seq_live = seq_ref[step]
    left = jnp.dot(second, wl_ref[...], preferred_element_type=F32)
    left = (left * (live_col_ref[...] * seq_live)).reshape(16, 4, 8, 128)
    group = lax.broadcasted_iota(jnp.int32, (16, 8, 128), 2) // 32
    packed = left[:, 0]
    for q in range(1, 4):
        packed = jnp.where(group == q, left[:, q], packed)
    right = lax.dot_general(wr_ref[...], second, NT, preferred_element_type=F32)
    right = right * (live_ref[...] * seq_live)
    for m in range(4):
        tile = right[:, 128 * m : 128 * m + 128]
        for c, chunk in enumerate(mix(tile[:16], tile[16:])):
            for core in range(2):
                half = chunk[8 * core : 8 * core + 8]
                for xz in range(8):
                    factor_ref[xz, core, 2 * m + c, 0] = jnp.concatenate(
                        [packed[2 * xz + core], half], axis=0
                    ).astype(BF16)


def attention(place, seq_live, biases, x, projected, wo, wl, wr, live, live_col):
    count = x.shape[1]
    smem = pl.BlockSpec(memory_space=pltpu.SMEM)

    def whole(a):
        return pl.BlockSpec(a.shape, lambda s: (0,) * a.ndim)

    def per_seq(*dims):
        return pl.BlockSpec(dims, lambda s: (0, s) + (0,) * (len(dims) - 2))

    return pl.pallas_call(
        attention_kernel,
        grid=(count,),
        in_specs=[
            smem,
            smem,
            *(whole(b) for b in biases),
            per_seq(16, 1, 32, 256),
            *(
                pl.BlockSpec((1,) + a.shape[1:], lambda s, n=a.ndim: (s,) + (0,) * (n - 1))
                for a in projected
            ),
            whole(wo),
            whole(wl),
            whole(wr),
            whole(live),
            whole(live_col),
        ],
        out_specs=[
            per_seq(16, 1, 32, 256),
            pl.BlockSpec((8, 2, 8, 1, 16, 128), lambda s: (0, 0, 0, s, 0, 0)),
        ],
        out_shape=[
            jax.ShapeDtypeStruct(x.shape, BF16),
            jax.ShapeDtypeStruct((8, 2, 8, count, 16, 128), BF16),
        ],
        scratch_shapes=[
            pltpu.VMEM((8, 512, 512), F32),
            pltpu.VMEM((256, 512), F32),
        ],
        compiler_params=params(48),
        name="row_attention",
    )(place, seq_live, *biases, x, *projected, wo, wl, wr, live, live_col)


def outer_kernel(
    core_ref,
    l_ref,
    own_ref,
    other_ref,
    w_ref,
    inv_ref,
    plane_ref,
    pair_ref,
    wp_ref,
    mid_ref,
    tri_ref,
    lt_ref,
    x_ref,
):
    step = pl.program_id(0)

    @pl.when(step == 0)
    def _():
        for v in range(8):
            rows = slice(128 * v, 128 * v + 128)
            lt_ref[rows, :] = l_ref[:, rows].astype(F32).T.astype(BF16)
        for ref, core in ((own_ref, core_ref[0]), (other_ref, 1 - core_ref[0])):

            def some(n, carry):
                lanes = pl.ds(pl.multiple_of(n * 256, 256), 256)
                product = jnp.dot(lt_ref[...], ref[:, lanes], preferred_element_type=F32)
                for k in range(2):
                    base = pl.multiple_of(core * 512 + n * 128 + 64 * k, 64)
                    for v in range(8):
                        for half in range(2):
                            at = 128 * v + 32 * half
                            low, high = mix(
                                product[at : at + 32, 128 * k : 128 * k + 128],
                                product[at + 64 : at + 96, 128 * k : 128 * k + 128],
                            )
                            columns = slice(128 * half, 128 * half + 128)
                            x_ref[v, pl.ds(base, 32), columns] = low.astype(BF16)
                            x_ref[v, pl.ds(base + 32, 32), columns] = high.astype(BF16)
                return carry

            lax.fori_loop(0, 4, some, 0)

    update = jnp.dot(w_ref[...], x_ref[step], preferred_element_type=F32)
    for half in range(2):
        part = update[:, 128 * half : 128 * half + 128] * inv_ref[half, 0]
        before = jnp.concatenate([pair_ref[half, 0], pair_ref[half + 2, 0]], axis=0)
        mid = (before.astype(F32) + part.T).astype(BF16)
        mid_ref[half, 0] = mid[:64]
        mid_ref[half + 2, 0] = mid[64:]
        normed = layer_norm(mid).astype(BF16)
        terms = lax.dot_general(wp_ref[...], normed, NT, preferred_element_type=F32)
        plane = plane_ref[half, 0]
        tri_ref[half, 0, :128] = (jax.nn.sigmoid(terms[:128]) * terms[128:256] * plane).astype(BF16)
        tri_ref[half, 0, 128:] = (jax.nn.sigmoid(terms[256:384]) * terms[384:] * plane).astype(BF16)


def outer_update(core, left, own, other, weight, inv, plane, pairwise, wp):
    total = left.shape[0]

    def whole(a):
        return pl.BlockSpec(a.shape, lambda v: (0,) * a.ndim)

    def by_v(*dims):
        return pl.BlockSpec(dims, lambda v: (0, v) + (0,) * (len(dims) - 2))

    return pl.pallas_call(
        outer_kernel,
        grid=(8,),
        in_specs=[
            pl.BlockSpec(memory_space=pltpu.SMEM),
            whole(left),
            whole(own),
            whole(other),
            whole(weight),
            by_v(2, 1, 1, 128),
            by_v(2, 1, 1, 128),
            by_v(4, 1, 64, 128),
            whole(wp),
        ],
        out_specs=[by_v(4, 1, 64, 128), by_v(2, 1, 256, 128)],
        out_shape=[
            jax.ShapeDtypeStruct((4, 8, 64, 128), BF16),
            jax.ShapeDtypeStruct((2, 8, 256, 128), BF16),
        ],
        scratch_shapes=[pltpu.VMEM((1024, total), BF16), pltpu.VMEM((8, 1024, 256), BF16)],
        compiler_params=params(32),
        name="outer_update",
    )(core, left, own, other, weight, inv, plane, pairwise, wp)


def triangle_kernel(in_ref, out_ref, a_ref, b_ref):
    def assemble(r, carry):
        base = pl.multiple_of(r * 32, 32)
        for t, ref in ((0, a_ref), (1, b_ref)):
            for m in range(4):
                low, high = mix(
                    in_ref[r * 8 + 2 * m, t].astype(F32), in_ref[r * 8 + 2 * m + 1, t].astype(F32)
                )
                ref[pl.ds(base, 16), 128 * m : 128 * m + 128] = low.astype(BF16)
                ref[pl.ds(base + 16, 16), 128 * m : 128 * m + 128] = high.astype(BF16)
        return carry

    lax.fori_loop(0, 16, assemble, 0)

    def multiply(g, carry):
        base = pl.multiple_of(g * 128, 128)
        c = lax.dot_general(a_ref[pl.ds(base, 128), :], b_ref[...], NT, preferred_element_type=F32)
        for part in range(4):
            for m in range(4):
                columns = slice(128 * m, 128 * m + 128)
                even, odd = mix(
                    c[32 * part : 32 * part + 16, columns], c[32 * part + 16 : 32 * part + 32, columns]
                )
                out_ref[(g * 4 + part) * 8 + 2 * m] = even.astype(BF16)
                out_ref[(g * 4 + part) * 8 + 2 * m + 1] = odd.astype(BF16)
        return carry

    lax.fori_loop(0, 4, multiply, 0)


def triangle(blocks):
    return pl.pallas_call(
        triangle_kernel,
        out_shape=jax.ShapeDtypeStruct((128, 16, 128), BF16),
        scratch_shapes=[pltpu.VMEM((512, 512), BF16), pltpu.VMEM((512, 512), BF16)],
        compiler_params=params(16),
        name="triangle",
    )(blocks)


def final_kernel(tri_ref, mid_ref, wt_ref, wg_ref, out_ref):
    for u in range(16):
        combined = tri_ref[u].astype(F32)
        centered = combined - jnp.mean(combined, axis=0, keepdims=True)
        variance = jnp.mean(centered * centered, axis=0, keepdims=True)
        normed = (centered * lax.rsqrt(variance + EPS)).astype(BF16)
        update = jnp.dot(wt_ref[...], normed, preferred_element_type=F32)
        mid = jnp.concatenate([mid_ref[u], mid_ref[16 + u]], axis=0)
        gate = jax.nn.sigmoid(
            jnp.dot(layer_norm(mid).astype(BF16), wg_ref[...], preferred_element_type=F32)
        )
        out = (mid.astype(F32) + gate * update.T).astype(BF16)
        out_ref[u] = out[:64]
        out_ref[16 + u] = out[64:]


def final(tri, mid, wt, wg):
    return pl.pallas_call(
        final_kernel,
        out_shape=jax.ShapeDtypeStruct((32, 64, 128), BF16),
        compiler_params=params(16),
        name="pair_final",
    )(tri, mid, wt, wg)


def copy_kernel(in_ref, out_ref):
    out_ref[...] = in_ref[...]


def copied(a):
    return pl.pallas_call(
        copy_kernel,
        out_shape=jax.ShapeDtypeStruct(a.shape, a.dtype),
        compiler_params=params(8),
        name="copied",
    )(a)


def body(
    alignment,
    pairwise,
    residue_mask,
    sequence_mask,
    attention_input_weight,
    attention_output_weight,
    bias_project,
    outer_factor_weight,
    outer_output,
    tri_project,
    tri_gate,
    tri_output,
):
    row = lax.axis_index(ROW)
    col = lax.axis_index(COL)
    core = lax.axis_index("core")
    swap = [(0, 1), (1, 0)]
    res_live = residue_mask.astype(F32)
    seq_live = sequence_mask.astype(F32)
    row_live = lax.dynamic_slice_in_dim(res_live, row * 32, 32)
    col_live = lax.dynamic_slice_in_dim(res_live, col * 64, 64)
    my_seqs = lax.dynamic_slice_in_dim(seq_live, col * 80 + row * 5, 5)

    def gather(a, perms):
        return [a] + [lax.ppermute(a, axes, perm) for axes, perm in perms]

    def ring(axis):
        return [(axis, [(i, (i + d) % 4) for i in range(4)]) for d in (1, 2, 3)]

    z = ("zl", "zh")
    near = [(z, [(i, i ^ d) for i in range(4)]) for d in (1, 2, 3)]
    half, rest = pair_bias(core.reshape(1), pairwise, bias_project.T)
    outgoing, half, rest = lax.optimization_barrier(
        (alignment.reshape(16, 5, 32, 256), half, rest)
    )
    both = jnp.stack([half, lax.ppermute(rest, "core", swap)])
    blocks = jnp.concatenate(gather(both, near), axis=0)
    place = jnp.stack([lax.axis_index(name) for name in ("x", "zl", "core", "zh", "y")])
    bias_plane = plane(place, gather(blocks, ring("x")))
    own = gather(bias_plane, ring("y"))
    sequences = lax.all_to_all(outgoing, ROW, split_axis=0, concat_axis=0, tiled=True)
    live_plane = row_live[:, None] * col_live[None, :]
    inv = 1.0 / jnp.maximum(jnp.sum(seq_live) * live_plane, 1.0)

    def pairs(a):
        return a.reshape(2, 16, 64).transpose(1, 0, 2).reshape(2, 8, 1, 128)

    weight = outer_output.reshape(32, 2, 16, 128).transpose(3, 2, 1, 0).reshape(128, 1024)
    win = attention_input_weight.reshape(256, 1024).T
    wp = tri_project.reshape(128, 512).T
    wt = tri_output.T
    wl = jnp.tile(outer_factor_weight[:, 0], (1, 4))
    wr = outer_factor_weight[:, 1].T
    live_cols = jnp.broadcast_to(res_live[:, None], (512, 128))
    sequences, _, weight, wp, wt, inv, live_plane, win, wl, wr, live_cols, my_seqs = (
        lax.optimization_barrier(
            (
                sequences,
                bias_plane,
                weight,
                wp,
                wt,
                pairs(inv),
                pairs(live_plane),
                win,
                wl,
                wr,
                live_cols,
                my_seqs,
            )
        )
    )
    projected = projections(sequences, win)
    own, projected = lax.optimization_barrier((own, projected))
    other = [lax.ppermute(b, "core", swap) for b in own]
    out_seq, factors = attention(
        jnp.stack([core, lax.axis_index("y")]),
        my_seqs,
        own + other,
        sequences,
        projected,
        attention_output_weight,
        wl,
        wr,
        res_live.reshape(1, 512),
        live_cols,
    )
    factors = lax.all_to_all(
        factors.reshape(128, 80, 128), ALL, split_axis=0, concat_axis=0, tiled=True
    )
    out_seq, factors = lax.optimization_barrier((out_seq, factors))
    factors = factors.reshape(640, 16, 128)
    right_own = factors[:, 8:].reshape(640, 1024)
    right_other = lax.ppermute(right_own, "core", swap)
    left = factors[:, :8].reshape(640, 1024)
    alignment_output = lax.all_to_all(
        out_seq, ROW, split_axis=0, concat_axis=0, tiled=True
    ).reshape(80, 32, 256)

    mid, tri = outer_update(
        core.reshape(1),
        left,
        right_own,
        right_other,
        weight,
        inv,
        live_plane,
        pairwise.reshape(4, 8, 64, 128),
        wp,
    )
    tri, alignment_output = lax.optimization_barrier((tri, alignment_output))
    alignment_output = copied(alignment_output)
    tri = tri.reshape(16, 2, 128, 128).transpose(2, 1, 0, 3)
    blocks = lax.all_to_all(tri, ALL, split_axis=0, concat_axis=0, tiled=True)
    combined = lax.all_to_all(triangle(blocks), ALL, split_axis=0, concat_axis=0, tiled=True)
    pair_output_state = final(
        combined.transpose(1, 0, 2), mid.reshape(32, 64, 128), wt, tri_gate
    )
    return (alignment_output, pair_output_state)


def solution(mesh):
    fine = Mesh(mesh.devices.reshape(4, 2, 2, 2, 4), ALL)
    placed = (P(COL, ROW, None), P(ROW, COL, None)) + (P(),) * 10
    return jax.shard_map(
        body,
        mesh=fine,
        in_specs=placed,
        out_specs=(P(COL, ROW, None), P(ROW, COL, None)),
        check_vma=False,
    )
```

```python
import jax
import jax.numpy as jnp
from jax import lax
from jax.experimental import pallas as pl
from jax.experimental.pallas import tpu as pltpu
from jax.sharding import Mesh, PartitionSpec as P

EPS = 1e-05
BIG = 1000000000.0
LOG2E = 1.4426950408889634
F32 = jnp.float32
BF16 = jnp.bfloat16
ROW = ("x", "zl", "core")
COL = ("zh", "y")
ALL = ROW + COL
CHIP = ("x", "zl", "zh", "y")
NT = (((1,), (1,)), ((), ()))
TN = (((0,), (0,)), ((), ()))
MB = 1 << 20


def layer_norm(v):
    v = v.astype(F32)
    centered = v - jnp.mean(v, axis=-1, keepdims=True)
    variance = jnp.mean(centered * centered, axis=-1, keepdims=True)
    return centered * lax.rsqrt(variance + EPS)


def low_lanes(shape):
    return lax.broadcasted_iota(jnp.int32, shape, len(shape) - 1) < 64


def mix(first, second):
    keep = low_lanes(first.shape)
    turn = len(first.shape) - 1
    return (
        jnp.where(keep, first, pltpu.roll(second, 64, turn)),
        jnp.where(keep, pltpu.roll(first, 64, turn), second),
    )


def params(mib):
    return pltpu.CompilerParams(vmem_limit_bytes=mib * MB)


def bias_kernel(pair_ref, weight_ref, out_ref, normed_ref, bias_ref):
    normed_ref[...] = layer_norm(pair_ref[...])
    for w in range(16):
        block = jnp.concatenate([normed_ref[:, jq * 16 + w, :] for jq in range(4)], axis=0)
        bias_ref[:, w, :] = lax.dot_general(
            weight_ref[...], block.astype(BF16), NT, preferred_element_type=F32
        )
    for core in range(2):
        chunk = bias_ref[4 * core : 4 * core + 4].reshape(64, 128).astype(BF16)
        for xz in range(8):
            for zh in range(2):
                out_ref[xz, core, zh] = chunk


def pair_bias(pairwise, weight):
    return pl.pallas_call(
        bias_kernel,
        out_shape=jax.ShapeDtypeStruct((8, 2, 2, 64, 128), BF16),
        scratch_shapes=[pltpu.VMEM((32, 64, 128), F32), pltpu.VMEM((8, 16, 128), F32)],
        compiler_params=params(16),
        name="pair_bias",
    )(pairwise, weight)


def plane_kernel(in_ref, out_ref):
    group = lax.broadcasted_iota(jnp.int32, (16, 128), 1) // 32
    for zh in range(2):
        for hh in range(4):
            for x in range(4):
                parts = [
                    in_ref[(x * 4 + g) * 2 + zh, 16 * hh : 16 * hh + 16, :].astype(F32)
                    for g in range(4)
                ]
                for jq in range(4):
                    turned = [
                        part if g == jq else pltpu.roll(part, 32 * ((g - jq) % 4), 1)
                        for g, part in enumerate(parts)
                    ]
                    row = jnp.where(
                        group < 2,
                        jnp.where(group == 0, turned[0], turned[1]),
                        jnp.where(group == 2, turned[2], turned[3]),
                    )
                    base = 64 * zh + 16 * jq
                    out_ref[hh, base : base + 16, 128 * x : 128 * x + 128] = row.astype(BF16)


def plane(blocks):
    return pl.pallas_call(
        plane_kernel,
        out_shape=jax.ShapeDtypeStruct((4, 128, 512), BF16),
        compiler_params=params(8),
        name="bias_plane",
    )(blocks)


def attention_kernel(
    place_ref,
    seq_ref,
    own0_ref,
    own1_ref,
    own2_ref,
    own3_ref,
    other0_ref,
    other1_ref,
    other2_ref,
    other3_ref,
    x_ref,
    win_ref,
    wo_ref,
    wl_ref,
    wr_ref,
    live_ref,
    live_col_ref,
    out_ref,
    factor_ref,
    bias_ref,
    qt_ref,
    k_ref,
    vt_ref,
    acc_ref,
):
    heads = bias_ref.shape[0]
    step = pl.program_id(0)

    @pl.when(step == 0)
    def _():
        core, y = place_ref[0], place_ref[1]
        own = (own0_ref, own1_ref, own2_ref, own3_ref)
        other = (other0_ref, other1_ref, other2_ref, other3_ref)
        for refs, side in ((own, core), (other, 1 - core)):
            for d in range(4):
                source = lax.rem(y + 4 - d, 4)
                for zh in range(2):
                    rows = pl.ds(pl.multiple_of(256 * zh + 64 * source, 64), 64)
                    penalty = (live_col_ref[rows, :] - 1.0) * BIG
                    for m in range(4):
                        lanes = slice(128 * m, 128 * m + 128)
                        for hh in range(4):
                            bias_ref[4 * side + hh, rows, lanes] = (
                                refs[d][hh, 64 * zh : 64 * zh + 64, lanes].astype(F32) * LOG2E
                                + penalty
                            )

    x = x_ref[:, 0].reshape(512, 256)
    normed = layer_norm(x).astype(BF16)

    def project(t):
        return lax.dot_general(
            win_ref[256 * t : 256 * t + 256], normed, NT, preferred_element_type=F32
        )

    qt_ref[...] = (project(0) * (32 ** (-0.5) * LOG2E)).astype(BF16)
    k_ref[...] = lax.dot_general(
        normed, win_ref[256:512], NT, preferred_element_type=F32
    ).astype(BF16)
    vt_ref[:, :32] = project(2).astype(BF16).reshape(heads, 32, 512)
    vt_ref[:, 32:] = jnp.ones((heads, 16, 512), BF16)
    row_head = lax.broadcasted_iota(jnp.int32, (128, 512), 0) // 32

    def scores(h):
        lanes = slice(128 * (h // 4), 128 * (h // 4) + 128)
        q_h = jnp.where(row_head == h % 4, qt_ref[lanes, :], jnp.zeros((), BF16))
        s = jnp.dot(k_ref[:, lanes], q_h, preferred_element_type=F32) + bias_ref[h]
        return s, jnp.max(s, axis=0, keepdims=True)

    def values(h, p):
        o = jnp.dot(vt_ref[h], p, preferred_element_type=F32)
        acc_ref[32 * h : 32 * h + 32, :] = o[:32] / o[32:33]

    s, top = scores(0)
    p = None
    for h in range(heads):
        ahead = scores(h + 1) if h + 1 < heads else None
        if p is not None:
            values(h - 1, p)
        p = jnp.exp2(s - top).astype(BF16)
        if ahead is not None:
            s, top = ahead
    values(heads - 1, p)
    attended = (acc_ref[...] * jax.nn.sigmoid(project(3))).T.astype(BF16)
    out = (
        x.astype(F32) + jnp.dot(attended, wo_ref[...], preferred_element_type=F32)
    ).astype(BF16)
    out_ref[:, 0] = out.reshape(16, 32, 256)
    second = layer_norm(out).astype(BF16)
    seq_live = seq_ref[step]
    left = jnp.dot(second, wl_ref[...], preferred_element_type=F32)
    left = (left * (live_col_ref[...] * seq_live)).reshape(16, 4, 8, 128)
    group = lax.broadcasted_iota(jnp.int32, (16, 8, 128), 2) // 32
    packed = left[:, 0]
    for q in range(1, 4):
        packed = jnp.where(group == q, left[:, q], packed)
    right = lax.dot_general(wr_ref[...], second, NT, preferred_element_type=F32)
    right = right * (live_ref[...] * seq_live)
    for m in range(4):
        tile = right[:, 128 * m : 128 * m + 128]
        for c, chunk in enumerate(mix(tile[:16], tile[16:])):
            for core in range(2):
                half = chunk[8 * core : 8 * core + 8]
                for xz in range(8):
                    factor_ref[xz, core, 2 * m + c, 0] = jnp.concatenate(
                        [packed[2 * xz + core], half], axis=0
                    ).astype(BF16)


def attention(place, seq_live, biases, x, win, wo, wl, wr, live, live_col):
    count = x.shape[1]
    smem = pl.BlockSpec(memory_space=pltpu.SMEM)

    def whole(a):
        return pl.BlockSpec(a.shape, lambda s: (0,) * a.ndim)

    def per_seq(*dims):
        return pl.BlockSpec(dims, lambda s: (0, s) + (0,) * (len(dims) - 2))

    return pl.pallas_call(
        attention_kernel,
        grid=(count,),
        in_specs=[
            smem,
            smem,
            *(whole(b) for b in biases),
            per_seq(16, 1, 32, 256),
            whole(win),
            whole(wo),
            whole(wl),
            whole(wr),
            whole(live),
            whole(live_col),
        ],
        out_specs=[
            per_seq(16, 1, 32, 256),
            pl.BlockSpec((8, 2, 8, 1, 16, 128), lambda s: (0, 0, 0, s, 0, 0)),
        ],
        out_shape=[
            jax.ShapeDtypeStruct(x.shape, BF16),
            jax.ShapeDtypeStruct((8, 2, 8, count, 16, 128), BF16),
        ],
        scratch_shapes=[
            pltpu.VMEM((8, 512, 512), F32),
            pltpu.VMEM((256, 512), BF16),
            pltpu.VMEM((512, 256), BF16),
            pltpu.VMEM((8, 48, 512), BF16),
            pltpu.VMEM((256, 512), F32),
        ],
        compiler_params=params(32),
        name="row_attention",
    )(place, seq_live, *biases, x, win, wo, wl, wr, live, live_col)


def outer_kernel(
    core_ref,
    l_ref,
    own_ref,
    other_ref,
    w_ref,
    inv_ref,
    plane_ref,
    pair_ref,
    wp_ref,
    mid_ref,
    tri_ref,
    lt_ref,
    x_ref,
):
    for v in range(8):
        rows = slice(128 * v, 128 * v + 128)
        lt_ref[rows, :] = l_ref[:, rows].astype(F32).T.astype(BF16)
    for ref, core in ((own_ref, core_ref[0]), (other_ref, 1 - core_ref[0])):

        def some(n, carry):
            lanes = pl.ds(pl.multiple_of(n * 256, 256), 256)
            product = jnp.dot(lt_ref[...], ref[:, lanes], preferred_element_type=F32)
            for k in range(2):
                base = pl.multiple_of(core * 512 + n * 128 + 64 * k, 64)
                for v in range(8):
                    for half in range(2):
                        at = 128 * v + 32 * half
                        low, high = mix(
                            product[at : at + 32, 128 * k : 128 * k + 128],
                            product[at + 64 : at + 96, 128 * k : 128 * k + 128],
                        )
                        place = (v % 2) * 256 + 128 * half
                        columns = slice(place, place + 128)
                        x_ref[v // 2, pl.ds(base, 32), columns] = low.astype(BF16)
                        x_ref[v // 2, pl.ds(base + 32, 32), columns] = high.astype(BF16)
            return carry

        lax.fori_loop(0, 4, some, 0, unroll=2)

    def finish(g, carry):
        update = jnp.dot(w_ref[...], x_ref[g], preferred_element_type=F32)
        places = [(half, 2 * g + e) for e in range(2) for half in range(2)]
        inv = jnp.concatenate([inv_ref[half, v] for half, v in places], axis=1)
        live = jnp.concatenate([plane_ref[half, v] for half, v in places], axis=1)
        before = jnp.concatenate(
            [pair_ref[half + 2 * k, v] for half, v in places for k in range(2)], axis=0
        )
        mid = (before.astype(F32) + (update * inv).T).astype(BF16)
        normed = layer_norm(mid).astype(BF16)
        terms = lax.dot_general(wp_ref[...], normed, NT, preferred_element_type=F32)
        ta = (jax.nn.sigmoid(terms[:128]) * terms[128:256] * live).astype(BF16)
        tb = (jax.nn.sigmoid(terms[256:384]) * terms[384:] * live).astype(BF16)
        for n, (half, v) in enumerate(places):
            for k in range(2):
                mid_ref[half + 2 * k, v] = mid[128 * n + 64 * k : 128 * n + 64 * k + 64]
            tri_ref[half, v, :128] = ta[:, 128 * n : 128 * n + 128]
            tri_ref[half, v, 128:] = tb[:, 128 * n : 128 * n + 128]
        return carry

    lax.fori_loop(0, 4, finish, 0, unroll=True)


def outer_update(core, left, own, other, weight, inv, live_plane, pairwise, wp):
    total = left.shape[0]
    vmem = pl.BlockSpec(memory_space=pltpu.VMEM)
    return pl.pallas_call(
        outer_kernel,
        in_specs=[pl.BlockSpec(memory_space=pltpu.SMEM)] + [vmem] * 8,
        out_shape=[
            jax.ShapeDtypeStruct((4, 8, 64, 128), BF16),
            jax.ShapeDtypeStruct((2, 8, 256, 128), BF16),
        ],
        scratch_shapes=[pltpu.VMEM((1024, total), BF16), pltpu.VMEM((4, 1024, 512), BF16)],
        compiler_params=params(32),
        name="outer_update",
    )(core, left, own, other, weight, inv, live_plane, pairwise, wp)


def triangle_kernel(in_ref, out_ref, a_ref, b_ref):
    def assemble(r, carry):
        base = pl.multiple_of(r * 32, 32)
        for t, ref in ((0, a_ref), (1, b_ref)):
            for m in range(4):
                low, high = mix(
                    in_ref[r * 8 + 2 * m, t].astype(F32), in_ref[r * 8 + 2 * m + 1, t].astype(F32)
                )
                ref[pl.ds(base, 16), 128 * m : 128 * m + 128] = low.astype(BF16)
                ref[pl.ds(base + 16, 16), 128 * m : 128 * m + 128] = high.astype(BF16)
        return carry

    lax.fori_loop(0, 16, assemble, 0)

    def multiply(g, carry):
        base = pl.multiple_of(g * 128, 128)
        c = lax.dot_general(a_ref[pl.ds(base, 128), :], b_ref[...], NT, preferred_element_type=F32)
        for part in range(4):
            for m in range(4):
                columns = slice(128 * m, 128 * m + 128)
                even, odd = mix(
                    c[32 * part : 32 * part + 16, columns], c[32 * part + 16 : 32 * part + 32, columns]
                )
                out_ref[(g * 4 + part) * 8 + 2 * m] = even.astype(BF16)
                out_ref[(g * 4 + part) * 8 + 2 * m + 1] = odd.astype(BF16)
        return carry

    lax.fori_loop(0, 4, multiply, 0)


def triangle(blocks):
    return pl.pallas_call(
        triangle_kernel,
        out_shape=jax.ShapeDtypeStruct((128, 16, 128), BF16),
        scratch_shapes=[pltpu.VMEM((512, 512), BF16), pltpu.VMEM((512, 512), BF16)],
        compiler_params=params(16),
        name="triangle",
    )(blocks)


def gate_kernel(mid_ref, wg_ref, out_ref):
    for u in range(16):
        mid = jnp.concatenate([mid_ref[u], mid_ref[16 + u]], axis=0)
        out_ref[u] = jax.nn.sigmoid(
            jnp.dot(layer_norm(mid).astype(BF16), wg_ref[...], preferred_element_type=F32)
        )


def gates(mid, wg):
    return pl.pallas_call(
        gate_kernel,
        out_shape=jax.ShapeDtypeStruct((16, 128, 128), F32),
        compiler_params=params(16),
        name="pair_gate",
    )(mid, wg)


def final_kernel(tri_ref, mid_ref, wt_ref, gate_ref, out_ref):
    for u in range(16):
        combined = tri_ref[u].astype(F32)
        centered = combined - jnp.mean(combined, axis=0, keepdims=True)
        variance = jnp.mean(centered * centered, axis=0, keepdims=True)
        normed = (centered * lax.rsqrt(variance + EPS)).astype(BF16)
        update = jnp.dot(wt_ref[...], normed, preferred_element_type=F32)
        mid = jnp.concatenate([mid_ref[u], mid_ref[16 + u]], axis=0)
        out = (mid.astype(F32) + gate_ref[u] * update.T).astype(BF16)
        out_ref[u] = out[:64]
        out_ref[16 + u] = out[64:]


def final(tri, mid, wt, gate):
    return pl.pallas_call(
        final_kernel,
        out_shape=jax.ShapeDtypeStruct((32, 64, 128), BF16),
        compiler_params=params(16),
        name="pair_final",
    )(tri, mid, wt, gate)


def copy_kernel(in_ref, out_ref):
    out_ref[...] = in_ref[...]


def copied(a):
    return pl.pallas_call(
        copy_kernel,
        out_shape=jax.ShapeDtypeStruct(a.shape, a.dtype),
        compiler_params=params(8),
        name="copied",
    )(a)


def body(
    alignment,
    pairwise,
    residue_mask,
    sequence_mask,
    attention_input_weight,
    attention_output_weight,
    bias_project,
    outer_factor_weight,
    outer_output,
    tri_project,
    tri_gate,
    tri_output,
):
    row = lax.axis_index(ROW)
    col = lax.axis_index(COL)
    core = lax.axis_index("core")
    swap = [(0, 1), (1, 0)]
    res_live = residue_mask.astype(F32)
    seq_live = sequence_mask.astype(F32)
    row_live = lax.dynamic_slice_in_dim(res_live, row * 32, 32)
    col_live = lax.dynamic_slice_in_dim(res_live, col * 64, 64)
    my_seqs = lax.dynamic_slice_in_dim(seq_live, col * 80 + row * 5, 5)

    blocks = lax.all_to_all(
        pair_bias(pairwise, bias_project.T).reshape(32, 64, 128),
        ROW + ("zh",),
        split_axis=0,
        concat_axis=0,
        tiled=True,
    )
    live_plane = row_live[:, None] * col_live[None, :]
    inv = 1.0 / jnp.maximum(jnp.sum(seq_live) * live_plane, 1.0)

    def pairs(a):
        return a.reshape(2, 16, 64).transpose(1, 0, 2).reshape(2, 8, 1, 128)

    weight = outer_output.reshape(32, 2, 16, 128).transpose(3, 2, 1, 0).reshape(128, 1024)
    win = attention_input_weight.reshape(256, 1024).T
    wp = tri_project.reshape(128, 512).T
    wt = tri_output.T
    wl = jnp.tile(outer_factor_weight[:, 0], (1, 4))
    wr = outer_factor_weight[:, 1].T
    live_cols = jnp.broadcast_to(res_live[:, None], (512, 128))
    blocks, weight, wp, wt, inv, live_plane, win, wl, wr, live_cols, my_seqs = (
        lax.optimization_barrier(
            (
                blocks,
                weight,
                wp,
                wt,
                pairs(inv),
                pairs(live_plane),
                win,
                wl,
                wr,
                live_cols,
                my_seqs,
            )
        )
    )
    outgoing, blocks = lax.optimization_barrier((alignment.reshape(16, 5, 32, 256), blocks))
    bias_plane = plane(blocks)
    own = [bias_plane] + [
        lax.ppermute(bias_plane, "y", [(i, (i + d) % 4) for i in range(4)]) for d in (1, 2, 3)
    ]
    other = [lax.ppermute(b, "core", swap) for b in own]
    sequences = lax.all_to_all(outgoing, ROW, split_axis=0, concat_axis=0, tiled=True)
    out_seq, factors = attention(
        jnp.stack([core, lax.axis_index("y")]),
        my_seqs,
        own + other,
        sequences,
        win,
        attention_output_weight,
        wl,
        wr,
        res_live.reshape(1, 512),
        live_cols,
    )
    factors = lax.all_to_all(
        factors.reshape(128, 80, 128), ALL, split_axis=0, concat_axis=0, tiled=True
    )
    out_seq, factors = lax.optimization_barrier((out_seq, factors))
    factors = factors.reshape(640, 16, 128)
    right_own = factors[:, 8:].reshape(640, 1024)
    right_other = lax.ppermute(right_own, "core", swap)
    left = factors[:, :8].reshape(640, 1024)
    alignment_output = lax.all_to_all(
        out_seq, ROW, split_axis=0, concat_axis=0, tiled=True
    ).reshape(80, 32, 256)

    mid, tri = outer_update(
        core.reshape(1),
        left,
        right_own,
        right_other,
        weight,
        inv,
        live_plane,
        pairwise.reshape(4, 8, 64, 128),
        wp,
    )
    tri, alignment_output = lax.optimization_barrier((tri, alignment_output))
    alignment_output = copied(alignment_output)
    tri = tri.reshape(16, 2, 128, 128).transpose(2, 1, 0, 3)
    blocks = lax.all_to_all(tri, ALL, split_axis=0, concat_axis=0, tiled=True)
    product, mid = lax.optimization_barrier((triangle(blocks), mid.reshape(32, 64, 128)))
    combined = lax.all_to_all(product, ALL, split_axis=0, concat_axis=0, tiled=True)
    pair_output_state = final(combined.transpose(1, 0, 2), mid, wt, gates(mid, tri_gate))
    return (alignment_output, pair_output_state)


def solution(mesh):
    fine = Mesh(mesh.devices.reshape(4, 2, 2, 2, 4), ALL)
    placed = (P(COL, ROW, None), P(ROW, COL, None)) + (P(),) * 10
    return jax.shard_map(
        body,
        mesh=fine,
        in_specs=placed,
        out_specs=(P(COL, ROW, None), P(ROW, COL, None)),
        check_vma=False,
    )
```

```python
import jax
import jax.numpy as jnp
from jax import lax
from jax.experimental import pallas as pl
from jax.experimental.pallas import tpu as pltpu
from jax.sharding import Mesh, PartitionSpec as P

EPS = 1e-05
BIG = 1000000000.0
LOG2E = 1.4426950408889634
F32 = jnp.float32
BF16 = jnp.bfloat16
ROW = ("x", "zl", "core")
COL = ("zh", "y")
ALL = ROW + COL
CHIP = ("x", "zl", "zh", "y")
NT = (((1,), (1,)), ((), ()))
TN = (((0,), (0,)), ((), ()))
MB = 1 << 20


def layer_norm(v):
    v = v.astype(F32)
    centered = v - jnp.mean(v, axis=-1, keepdims=True)
    variance = jnp.mean(centered * centered, axis=-1, keepdims=True)
    return centered * lax.rsqrt(variance + EPS)


def low_lanes(shape):
    return lax.broadcasted_iota(jnp.int32, shape, len(shape) - 1) < 64


def mix(first, second):
    keep = low_lanes(first.shape)
    turn = len(first.shape) - 1
    return (
        jnp.where(keep, first, pltpu.roll(second, 64, turn)),
        jnp.where(keep, pltpu.roll(first, 64, turn), second),
    )


def params(mib):
    return pltpu.CompilerParams(vmem_limit_bytes=mib * MB)


def bias_kernel(pair_ref, weight_ref, out_ref, normed_ref, bias_ref):
    normed_ref[...] = layer_norm(pair_ref[...])
    for w in range(16):
        block = jnp.concatenate([normed_ref[:, jq * 16 + w, :] for jq in range(4)], axis=0)
        bias_ref[:, w, :] = lax.dot_general(
            weight_ref[...], block.astype(BF16), NT, preferred_element_type=F32
        )
    for core in range(2):
        chunk = bias_ref[4 * core : 4 * core + 4].reshape(64, 128).astype(BF16)
        for xz in range(8):
            for zh in range(2):
                out_ref[xz, core, zh] = chunk


def pair_bias(pairwise, weight):
    return pl.pallas_call(
        bias_kernel,
        out_shape=jax.ShapeDtypeStruct((8, 2, 2, 64, 128), BF16),
        scratch_shapes=[pltpu.VMEM((32, 64, 128), F32), pltpu.VMEM((8, 16, 128), F32)],
        compiler_params=params(16),
        name="pair_bias",
    )(pairwise, weight)


def plane_kernel(in_ref, out_ref):
    group = lax.broadcasted_iota(jnp.int32, (16, 128), 1) // 32
    for zh in range(2):
        for hh in range(4):
            for x in range(4):
                parts = [
                    in_ref[(x * 4 + g) * 2 + zh, 16 * hh : 16 * hh + 16, :].astype(F32)
                    for g in range(4)
                ]
                for jq in range(4):
                    turned = [
                        part if g == jq else pltpu.roll(part, 32 * ((g - jq) % 4), 1)
                        for g, part in enumerate(parts)
                    ]
                    row = jnp.where(
                        group < 2,
                        jnp.where(group == 0, turned[0], turned[1]),
                        jnp.where(group == 2, turned[2], turned[3]),
                    )
                    base = 64 * zh + 16 * jq
                    out_ref[hh, base : base + 16, 128 * x : 128 * x + 128] = row.astype(BF16)


def plane(blocks):
    return pl.pallas_call(
        plane_kernel,
        out_shape=jax.ShapeDtypeStruct((4, 128, 512), BF16),
        compiler_params=params(8),
        name="bias_plane",
    )(blocks)


def attention_kernel(
    place_ref,
    seq_ref,
    own0_ref,
    own1_ref,
    own2_ref,
    own3_ref,
    other0_ref,
    other1_ref,
    other2_ref,
    other3_ref,
    x_ref,
    win_ref,
    wo_ref,
    wl_ref,
    wr_ref,
    live_ref,
    live_col_ref,
    out_ref,
    factor_ref,
    bias_ref,
    qt_ref,
    k_ref,
    vt_ref,
    acc_ref,
):
    heads = bias_ref.shape[0]
    step = pl.program_id(0)

    @pl.when(step == 0)
    def _():
        core, y = place_ref[0], place_ref[1]
        own = (own0_ref, own1_ref, own2_ref, own3_ref)
        other = (other0_ref, other1_ref, other2_ref, other3_ref)
        for refs, side in ((own, core), (other, 1 - core)):
            for d in range(4):
                source = lax.rem(y + 4 - d, 4)
                for zh in range(2):
                    rows = pl.ds(pl.multiple_of(256 * zh + 64 * source, 64), 64)
                    penalty = (live_col_ref[rows, :] - 1.0) * BIG
                    for m in range(4):
                        lanes = slice(128 * m, 128 * m + 128)
                        for hh in range(4):
                            bias_ref[4 * side + hh, rows, lanes] = (
                                refs[d][hh, 64 * zh : 64 * zh + 64, lanes].astype(F32) * LOG2E
                                + penalty
                            )

    x = x_ref[:, 0].reshape(512, 256)
    normed = layer_norm(x).astype(BF16)

    def project(t):
        return lax.dot_general(
            win_ref[256 * t : 256 * t + 256], normed, NT, preferred_element_type=F32
        )

    qt_ref[...] = (project(0) * (32 ** (-0.5) * LOG2E)).astype(BF16)
    k_ref[...] = lax.dot_general(
        normed, win_ref[256:512], NT, preferred_element_type=F32
    ).astype(BF16)
    vt_ref[:, :32] = project(2).astype(BF16).reshape(heads, 32, 512)
    vt_ref[:, 32:] = jnp.ones((heads, 16, 512), BF16)
    row_head = lax.broadcasted_iota(jnp.int32, (128, 512), 0) // 32

    def scores(h):
        lanes = slice(128 * (h // 4), 128 * (h // 4) + 128)
        q_h = jnp.where(row_head == h % 4, qt_ref[lanes, :], jnp.zeros((), BF16))
        s = jnp.dot(k_ref[:, lanes], q_h, preferred_element_type=F32) + bias_ref[h]
        return s, jnp.max(s, axis=0, keepdims=True)

    def values(h, p):
        o = jnp.dot(vt_ref[h], p, preferred_element_type=F32)
        acc_ref[32 * h : 32 * h + 32, :] = o[:32] / o[32:33]

    s, top = scores(0)
    p = None
    for h in range(heads):
        ahead = scores(h + 1) if h + 1 < heads else None
        if p is not None:
            values(h - 1, p)
        p = jnp.exp2(s - top).astype(BF16)
        if ahead is not None:
            s, top = ahead
    values(heads - 1, p)
    attended = (acc_ref[...] * jax.nn.sigmoid(project(3))).T.astype(BF16)
    out = (
        x.astype(F32) + jnp.dot(attended, wo_ref[...], preferred_element_type=F32)
    ).astype(BF16)
    out_ref[:, 0] = out.reshape(16, 32, 256)
    second = layer_norm(out).astype(BF16)
    seq_live = seq_ref[step]
    left = jnp.dot(second, wl_ref[...], preferred_element_type=F32)
    left = (left * (live_col_ref[...] * seq_live)).reshape(16, 4, 8, 128)
    group = lax.broadcasted_iota(jnp.int32, (16, 8, 128), 2) // 32
    packed = left[:, 0]
    for q in range(1, 4):
        packed = jnp.where(group == q, left[:, q], packed)
    right = lax.dot_general(wr_ref[...], second, NT, preferred_element_type=F32)
    right = right * (live_ref[...] * seq_live)
    for m in range(4):
        tile = right[:, 128 * m : 128 * m + 128]
        for c, chunk in enumerate(mix(tile[:16], tile[16:])):
            for core in range(2):
                half = chunk[8 * core : 8 * core + 8]
                for xz in range(8):
                    factor_ref[xz, core, 2 * m + c, 0] = jnp.concatenate(
                        [packed[2 * xz + core], half], axis=0
                    ).astype(BF16)


def attention(place, seq_live, biases, x, win, wo, wl, wr, live, live_col):
    count = x.shape[1]
    smem = pl.BlockSpec(memory_space=pltpu.SMEM)

    def whole(a):
        return pl.BlockSpec(a.shape, lambda s: (0,) * a.ndim)

    def per_seq(*dims):
        return pl.BlockSpec(dims, lambda s: (0, s) + (0,) * (len(dims) - 2))

    return pl.pallas_call(
        attention_kernel,
        grid=(count,),
        in_specs=[
            smem,
            smem,
            *(whole(b) for b in biases),
            per_seq(16, 1, 32, 256),
            whole(win),
            whole(wo),
            whole(wl),
            whole(wr),
            whole(live),
            whole(live_col),
        ],
        out_specs=[
            per_seq(16, 1, 32, 256),
            pl.BlockSpec((8, 2, 8, 1, 16, 128), lambda s: (0, 0, 0, s, 0, 0)),
        ],
        out_shape=[
            jax.ShapeDtypeStruct(x.shape, BF16),
            jax.ShapeDtypeStruct((8, 2, 8, count, 16, 128), BF16),
        ],
        scratch_shapes=[
            pltpu.VMEM((8, 512, 512), F32),
            pltpu.VMEM((256, 512), BF16),
            pltpu.VMEM((512, 256), BF16),
            pltpu.VMEM((8, 48, 512), BF16),
            pltpu.VMEM((256, 512), F32),
        ],
        compiler_params=params(32),
        name="row_attention",
    )(place, seq_live, *biases, x, win, wo, wl, wr, live, live_col)


def outer_kernel(
    core_ref,
    l_ref,
    own_ref,
    other_ref,
    w_ref,
    inv_ref,
    plane_ref,
    pair_ref,
    wp_ref,
    mid_ref,
    tri_ref,
    lt_ref,
    x_ref,
):
    for v in range(8):
        rows = slice(128 * v, 128 * v + 128)
        lt_ref[rows, :] = l_ref[:, rows].astype(F32).T.astype(BF16)
    for ref, core in ((own_ref, core_ref[0]), (other_ref, 1 - core_ref[0])):

        def some(n, carry):
            lanes = pl.ds(pl.multiple_of(n * 256, 256), 256)
            product = jnp.dot(lt_ref[...], ref[:, lanes], preferred_element_type=F32)
            for k in range(2):
                base = pl.multiple_of(core * 512 + n * 128 + 64 * k, 64)
                for v in range(8):
                    for half in range(2):
                        at = 128 * v + 32 * half
                        low, high = mix(
                            product[at : at + 32, 128 * k : 128 * k + 128],
                            product[at + 64 : at + 96, 128 * k : 128 * k + 128],
                        )
                        place = (v % 2) * 256 + 128 * half
                        columns = slice(place, place + 128)
                        x_ref[v // 2, pl.ds(base, 32), columns] = low.astype(BF16)
                        x_ref[v // 2, pl.ds(base + 32, 32), columns] = high.astype(BF16)
            return carry

        lax.fori_loop(0, 4, some, 0, unroll=2)

    def finish(g, carry):
        update = jnp.dot(w_ref[...], x_ref[g], preferred_element_type=F32)
        places = [(half, 2 * g + e) for e in range(2) for half in range(2)]
        inv = jnp.concatenate([inv_ref[half, v] for half, v in places], axis=1)
        live = jnp.concatenate([plane_ref[half, v] for half, v in places], axis=1)
        before = jnp.concatenate(
            [pair_ref[half + 2 * k, v] for half, v in places for k in range(2)], axis=0
        )
        mid = (before.astype(F32) + (update * inv).T).astype(BF16)
        normed = layer_norm(mid).astype(BF16)
        terms = lax.dot_general(wp_ref[...], normed, NT, preferred_element_type=F32)
        ta = (jax.nn.sigmoid(terms[:128]) * terms[128:256] * live).astype(BF16)
        tb = (jax.nn.sigmoid(terms[256:384]) * terms[384:] * live).astype(BF16)
        for n, (half, v) in enumerate(places):
            for k in range(2):
                mid_ref[half + 2 * k, v] = mid[128 * n + 64 * k : 128 * n + 64 * k + 64]
            tri_ref[half, v, :128] = ta[:, 128 * n : 128 * n + 128]
            tri_ref[half, v, 128:] = tb[:, 128 * n : 128 * n + 128]
        return carry

    lax.fori_loop(0, 4, finish, 0, unroll=True)


def outer_update(core, left, own, other, weight, inv, live_plane, pairwise, wp):
    total = left.shape[0]
    vmem = pl.BlockSpec(memory_space=pltpu.VMEM)
    return pl.pallas_call(
        outer_kernel,
        in_specs=[pl.BlockSpec(memory_space=pltpu.SMEM)] + [vmem] * 8,
        out_shape=[
            jax.ShapeDtypeStruct((4, 8, 64, 128), BF16),
            jax.ShapeDtypeStruct((2, 8, 256, 128), BF16),
        ],
        scratch_shapes=[pltpu.VMEM((1024, total), BF16), pltpu.VMEM((4, 1024, 512), BF16)],
        compiler_params=params(20),
        name="outer_update",
    )(core, left, own, other, weight, inv, live_plane, pairwise, wp)


def triangle_kernel(in_ref, out_ref, a_ref, b_ref):
    def assemble(r, carry):
        base = pl.multiple_of(r * 32, 32)
        for t, ref in ((0, a_ref), (1, b_ref)):
            for m in range(4):
                low, high = mix(
                    in_ref[r * 8 + 2 * m, t].astype(F32), in_ref[r * 8 + 2 * m + 1, t].astype(F32)
                )
                ref[pl.ds(base, 16), 128 * m : 128 * m + 128] = low.astype(BF16)
                ref[pl.ds(base + 16, 16), 128 * m : 128 * m + 128] = high.astype(BF16)
        return carry

    lax.fori_loop(0, 16, assemble, 0)

    def multiply(g, carry):
        base = pl.multiple_of(g * 128, 128)
        c = lax.dot_general(a_ref[pl.ds(base, 128), :], b_ref[...], NT, preferred_element_type=F32)
        for part in range(4):
            for m in range(4):
                columns = slice(128 * m, 128 * m + 128)
                even, odd = mix(
                    c[32 * part : 32 * part + 16, columns], c[32 * part + 16 : 32 * part + 32, columns]
                )
                out_ref[(g * 4 + part) * 8 + 2 * m] = even.astype(BF16)
                out_ref[(g * 4 + part) * 8 + 2 * m + 1] = odd.astype(BF16)
        return carry

    lax.fori_loop(0, 4, multiply, 0)


def triangle(blocks):
    return pl.pallas_call(
        triangle_kernel,
        out_shape=jax.ShapeDtypeStruct((128, 16, 128), BF16),
        scratch_shapes=[pltpu.VMEM((512, 512), BF16), pltpu.VMEM((512, 512), BF16)],
        compiler_params=params(16),
        name="triangle",
    )(blocks)


def gate_kernel(mid_ref, wg_ref, out_ref):
    for u in range(16):
        mid = jnp.concatenate([mid_ref[u], mid_ref[16 + u]], axis=0)
        out_ref[u] = jax.nn.sigmoid(
            jnp.dot(layer_norm(mid).astype(BF16), wg_ref[...], preferred_element_type=F32)
        )


def gates(mid, wg):
    return pl.pallas_call(
        gate_kernel,
        out_shape=jax.ShapeDtypeStruct((16, 128, 128), F32),
        compiler_params=params(16),
        name="pair_gate",
    )(mid, wg)


def final_kernel(tri_ref, mid_ref, wt_ref, gate_ref, out_ref):
    for u in range(16):
        combined = tri_ref[u].astype(F32)
        centered = combined - jnp.mean(combined, axis=0, keepdims=True)
        variance = jnp.mean(centered * centered, axis=0, keepdims=True)
        normed = (centered * lax.rsqrt(variance + EPS)).astype(BF16)
        update = jnp.dot(wt_ref[...], normed, preferred_element_type=F32)
        mid = jnp.concatenate([mid_ref[u], mid_ref[16 + u]], axis=0)
        out = (mid.astype(F32) + gate_ref[u] * update.T).astype(BF16)
        out_ref[u] = out[:64]
        out_ref[16 + u] = out[64:]


def final(tri, mid, wt, gate):
    return pl.pallas_call(
        final_kernel,
        out_shape=jax.ShapeDtypeStruct((32, 64, 128), BF16),
        compiler_params=params(16),
        name="pair_final",
    )(tri, mid, wt, gate)


def copy_kernel(in_ref, out_ref):
    out_ref[...] = in_ref[...]


def copied(a):
    return pl.pallas_call(
        copy_kernel,
        out_shape=jax.ShapeDtypeStruct(a.shape, a.dtype),
        compiler_params=params(8),
        name="copied",
    )(a)


def body(
    alignment,
    pairwise,
    residue_mask,
    sequence_mask,
    attention_input_weight,
    attention_output_weight,
    bias_project,
    outer_factor_weight,
    outer_output,
    tri_project,
    tri_gate,
    tri_output,
):
    row = lax.axis_index(ROW)
    col = lax.axis_index(COL)
    core = lax.axis_index("core")
    swap = [(0, 1), (1, 0)]
    res_live = residue_mask.astype(F32)
    seq_live = sequence_mask.astype(F32)
    row_live = lax.dynamic_slice_in_dim(res_live, row * 32, 32)
    col_live = lax.dynamic_slice_in_dim(res_live, col * 64, 64)
    my_seqs = lax.dynamic_slice_in_dim(seq_live, col * 80 + row * 5, 5)

    blocks = lax.all_to_all(
        pair_bias(pairwise, bias_project.T).reshape(32, 64, 128),
        ROW + ("zh",),
        split_axis=0,
        concat_axis=0,
        tiled=True,
    )
    live_plane = row_live[:, None] * col_live[None, :]
    inv = 1.0 / jnp.maximum(jnp.sum(seq_live) * live_plane, 1.0)

    def pairs(a):
        return a.reshape(2, 16, 64).transpose(1, 0, 2).reshape(2, 8, 1, 128)

    weight = outer_output.reshape(32, 2, 16, 128).transpose(3, 2, 1, 0).reshape(128, 1024)
    win = attention_input_weight.reshape(256, 1024).T
    wp = tri_project.reshape(128, 512).T
    wt = tri_output.T
    wl = jnp.tile(outer_factor_weight[:, 0], (1, 4))
    wr = outer_factor_weight[:, 1].T
    live_cols = jnp.broadcast_to(res_live[:, None], (512, 128))
    blocks, weight, wp, wt, inv, live_plane, win, wl, wr, live_cols, my_seqs = (
        lax.optimization_barrier(
            (
                blocks,
                weight,
                wp,
                wt,
                pairs(inv),
                pairs(live_plane),
                win,
                wl,
                wr,
                live_cols,
                my_seqs,
            )
        )
    )
    outgoing, bias_plane = lax.optimization_barrier(
        (alignment.reshape(16, 5, 32, 256), plane(blocks))
    )
    up, down = ([(i, (i + d) % 4) for i in range(4)] for d in (1, 3))
    left_plane = lax.ppermute(bias_plane, "y", up)
    right_plane = lax.ppermute(bias_plane, "y", down)
    far_plane = jnp.concatenate(
        [lax.ppermute(left_plane[:2], "y", up), lax.ppermute(right_plane[2:], "y", down)], axis=0
    )
    own = [bias_plane, left_plane, far_plane, right_plane]
    other = [lax.ppermute(b, "core", swap) for b in own]
    sequences = lax.all_to_all(outgoing, ROW, split_axis=0, concat_axis=0, tiled=True)
    out_seq, factors = attention(
        jnp.stack([core, lax.axis_index("y")]),
        my_seqs,
        own + other,
        sequences,
        win,
        attention_output_weight,
        wl,
        wr,
        res_live.reshape(1, 512),
        live_cols,
    )
    factors = lax.all_to_all(
        factors.reshape(128, 80, 128), ALL, split_axis=0, concat_axis=0, tiled=True
    )
    out_seq, factors = lax.optimization_barrier((out_seq, factors))
    factors = factors.reshape(640, 16, 128)
    right_own = factors[:, 8:].reshape(640, 1024)
    right_other = lax.ppermute(right_own, "core", swap)
    left = factors[:, :8].reshape(640, 1024)
    alignment_output = lax.all_to_all(
        out_seq, ROW, split_axis=0, concat_axis=0, tiled=True
    ).reshape(80, 32, 256)

    mid, tri = outer_update(
        core.reshape(1),
        left,
        right_own,
        right_other,
        weight,
        inv,
        live_plane,
        pairwise.reshape(4, 8, 64, 128),
        wp,
    )
    tri = tri.reshape(16, 2, 128, 128).transpose(2, 1, 0, 3)
    tri, alignment_output = lax.optimization_barrier((tri, alignment_output))
    alignment_output = copied(alignment_output)
    blocks = lax.all_to_all(tri, ALL, split_axis=0, concat_axis=0, tiled=True)
    product, mid = lax.optimization_barrier((triangle(blocks), mid.reshape(32, 64, 128)))
    combined = lax.all_to_all(product, ALL, split_axis=0, concat_axis=0, tiled=True)
    pair_output_state = final(combined.transpose(1, 0, 2), mid, wt, gates(mid, tri_gate))
    return (alignment_output, pair_output_state)


def solution(mesh):
    fine = Mesh(mesh.devices.reshape(4, 2, 2, 2, 4), ALL)
    placed = (P(COL, ROW, None), P(ROW, COL, None)) + (P(),) * 10
    return jax.shard_map(
        body,
        mesh=fine,
        in_specs=placed,
        out_specs=(P(COL, ROW, None), P(ROW, COL, None)),
        check_vma=False,
    )
```

```python
import jax
import jax.numpy as jnp
from jax import lax
from jax.experimental import pallas as pl
from jax.experimental.pallas import tpu as pltpu
from jax.sharding import Mesh, PartitionSpec as P

EPS = 1e-05
BIG = 1000000000.0
LOG2E = 1.4426950408889634
F32 = jnp.float32
BF16 = jnp.bfloat16
ROW = ("x", "zl", "core")
COL = ("zh", "y")
ALL = ROW + COL
CHIP = ("x", "zl", "zh", "y")
NT = (((1,), (1,)), ((), ()))
TN = (((0,), (0,)), ((), ()))
MB = 1 << 20


def layer_norm(v):
    v = v.astype(F32)
    centered = v - jnp.mean(v, axis=-1, keepdims=True)
    variance = jnp.mean(centered * centered, axis=-1, keepdims=True)
    return centered * lax.rsqrt(variance + EPS)


def low_lanes(shape):
    return lax.broadcasted_iota(jnp.int32, shape, len(shape) - 1) < 64


def mix(first, second):
    keep = low_lanes(first.shape)
    turn = len(first.shape) - 1
    return (
        jnp.where(keep, first, pltpu.roll(second, 64, turn)),
        jnp.where(keep, pltpu.roll(first, 64, turn), second),
    )


def params(mib):
    return pltpu.CompilerParams(vmem_limit_bytes=mib * MB)


def bias_kernel(pair_ref, weight_ref, out_ref, normed_ref, bias_ref):
    normed_ref[...] = layer_norm(pair_ref[...])
    for w in range(16):
        block = jnp.concatenate([normed_ref[:, jq * 16 + w, :] for jq in range(4)], axis=0)
        bias_ref[:, w, :] = lax.dot_general(
            weight_ref[...], block.astype(BF16), NT, preferred_element_type=F32
        )
    for core in range(2):
        chunk = bias_ref[4 * core : 4 * core + 4].reshape(64, 128).astype(BF16)
        for xz in range(8):
            for zh in range(2):
                out_ref[xz, core, zh] = chunk


def pair_bias(pairwise, weight):
    return pl.pallas_call(
        bias_kernel,
        out_shape=jax.ShapeDtypeStruct((8, 2, 2, 64, 128), BF16),
        scratch_shapes=[pltpu.VMEM((32, 64, 128), F32), pltpu.VMEM((8, 16, 128), F32)],
        compiler_params=params(16),
        name="pair_bias",
    )(pairwise, weight)


def plane_kernel(in_ref, out_ref):
    group = lax.broadcasted_iota(jnp.int32, (16, 128), 1) // 32
    for zh in range(2):
        for hh in range(4):
            for x in range(4):
                parts = [
                    in_ref[(x * 4 + g) * 2 + zh, 16 * hh : 16 * hh + 16, :].astype(F32)
                    for g in range(4)
                ]
                for jq in range(4):
                    turned = [
                        part if g == jq else pltpu.roll(part, 32 * ((g - jq) % 4), 1)
                        for g, part in enumerate(parts)
                    ]
                    row = jnp.where(
                        group < 2,
                        jnp.where(group == 0, turned[0], turned[1]),
                        jnp.where(group == 2, turned[2], turned[3]),
                    )
                    base = 64 * zh + 16 * jq
                    out_ref[hh, base : base + 16, 128 * x : 128 * x + 128] = row.astype(BF16)


def plane(blocks):
    return pl.pallas_call(
        plane_kernel,
        out_shape=jax.ShapeDtypeStruct((4, 128, 512), BF16),
        compiler_params=params(8),
        name="bias_plane",
    )(blocks)


def attention_kernel(
    place_ref,
    own0_ref,
    own1_ref,
    own2_ref,
    own3_ref,
    other0_ref,
    other1_ref,
    other2_ref,
    other3_ref,
    x_ref,
    win_ref,
    live_col_ref,
    out_ref,
    factor_ref,
    bias_ref,
    qt_ref,
    k_ref,
    vt_ref,
    acc_ref,
    live_ref,
):
    heads = bias_ref.shape[0]
    step = pl.program_id(0)

    @pl.when(step == 0)
    def _():
        live_ref[...] = live_col_ref[...].T[:8]
        core, y = place_ref[0], place_ref[1]
        own = (own0_ref, own1_ref, own2_ref, own3_ref)
        other = (other0_ref, other1_ref, other2_ref, other3_ref)
        for refs, side in ((own, core), (other, 1 - core)):
            for d in range(4):
                source = lax.rem(y + 4 - d, 4)
                for zh in range(2):
                    rows = pl.ds(pl.multiple_of(256 * zh + 64 * source, 64), 64)
                    penalty = (live_col_ref[rows, :] - 1.0) * BIG
                    for m in range(4):
                        lanes = slice(128 * m, 128 * m + 128)
                        for hh in range(4):
                            bias_ref[4 * side + hh, rows, lanes] = (
                                refs[d][hh, 64 * zh : 64 * zh + 64, lanes].astype(F32) * LOG2E
                                + penalty
                            )

    x = x_ref[:, 0].reshape(512, 256)
    normed = layer_norm(x).astype(BF16)

    def project(t):
        return lax.dot_general(
            win_ref[256 * t : 256 * t + 256], normed, NT, preferred_element_type=F32
        )

    qt_ref[...] = (project(0) * (32 ** (-0.5) * LOG2E)).astype(BF16)
    k_ref[...] = lax.dot_general(
        normed, win_ref[256:512], NT, preferred_element_type=F32
    ).astype(BF16)
    vt_ref[:, :32] = project(2).astype(BF16).reshape(heads, 32, 512)
    vt_ref[:, 32:] = jnp.ones((heads, 16, 512), BF16)
    row_head = lax.broadcasted_iota(jnp.int32, (128, 512), 0) // 32

    def scores(h):
        lanes = slice(128 * (h // 4), 128 * (h // 4) + 128)
        q_h = jnp.where(row_head == h % 4, qt_ref[lanes, :], jnp.zeros((), BF16))
        s = jnp.dot(k_ref[:, lanes], q_h, preferred_element_type=F32) + bias_ref[h]
        return s, jnp.max(s, axis=0, keepdims=True)

    def values(h, p):
        o = jnp.dot(vt_ref[h], p, preferred_element_type=F32)
        acc_ref[32 * h : 32 * h + 32, :] = o[:32] / o[32:33]

    s, top = scores(0)
    p = None
    for h in range(heads):
        ahead = scores(h + 1) if h + 1 < heads else None
        if p is not None:
            values(h - 1, p)
        p = jnp.exp2(s - top).astype(BF16)
        if ahead is not None:
            s, top = ahead
    values(heads - 1, p)
    attended = (acc_ref[...] * jax.nn.sigmoid(project(3))).T.astype(BF16)
    out = (
        x.astype(F32) + jnp.dot(attended, win_ref[1024:1280], preferred_element_type=F32)
    ).astype(BF16)
    out_ref[:, 0] = out.reshape(16, 32, 256)
    second = layer_norm(out).astype(BF16)
    seq_live = place_ref[2 + step].astype(F32)
    left = lax.dot_general(second, win_ref[1280:1408], NT, preferred_element_type=F32)
    left = (left * (live_col_ref[...] * seq_live)).reshape(16, 4, 8, 128)
    group = lax.broadcasted_iota(jnp.int32, (16, 8, 128), 2) // 32
    packed = left[:, 0]
    for q in range(1, 4):
        packed = jnp.where(group == q, left[:, q], packed)
    right = lax.dot_general(win_ref[1408:1440], second, NT, preferred_element_type=F32)
    right = right * (live_ref[:1] * seq_live)
    for m in range(4):
        tile = right[:, 128 * m : 128 * m + 128]
        for c, chunk in enumerate(mix(tile[:16], tile[16:])):
            for core in range(2):
                half = chunk[8 * core : 8 * core + 8]
                for xz in range(8):
                    factor_ref[xz, core, 2 * m + c, 0] = jnp.concatenate(
                        [packed[2 * xz + core], half], axis=0
                    ).astype(BF16)


def attention(place, biases, x, win, live_col):
    count = x.shape[1]
    smem = pl.BlockSpec(memory_space=pltpu.SMEM)

    def whole(a):
        return pl.BlockSpec(a.shape, lambda s: (0,) * a.ndim)

    def per_seq(*dims):
        return pl.BlockSpec(dims, lambda s: (0, s) + (0,) * (len(dims) - 2))

    return pl.pallas_call(
        attention_kernel,
        grid=(count,),
        in_specs=[
            smem,
            *(whole(b) for b in biases),
            per_seq(16, 1, 32, 256),
            whole(win),
            whole(live_col),
        ],
        out_specs=[
            per_seq(16, 1, 32, 256),
            pl.BlockSpec((8, 2, 8, 1, 16, 128), lambda s: (0, 0, 0, s, 0, 0)),
        ],
        out_shape=[
            jax.ShapeDtypeStruct(x.shape, BF16),
            jax.ShapeDtypeStruct((8, 2, 8, count, 16, 128), BF16),
        ],
        scratch_shapes=[
            pltpu.VMEM((8, 512, 512), F32),
            pltpu.VMEM((256, 512), BF16),
            pltpu.VMEM((512, 256), BF16),
            pltpu.VMEM((8, 48, 512), BF16),
            pltpu.VMEM((256, 512), F32),
            pltpu.VMEM((8, 512), F32),
        ],
        compiler_params=params(52),
        name="row_attention",
    )(place, *biases, x, win, live_col)


def outer_kernel(
    core_ref,
    l_ref,
    own_ref,
    other_ref,
    w_ref,
    inv_ref,
    plane_ref,
    pair_ref,
    wp_ref,
    mid_ref,
    tri_ref,
    lt_ref,
    x_ref,
):
    for v in range(8):
        rows = slice(128 * v, 128 * v + 128)
        lt_ref[rows, :] = l_ref[:, rows].astype(F32).T.astype(BF16)
    for ref, core in ((own_ref, core_ref[0]), (other_ref, 1 - core_ref[0])):

        def some(n, carry):
            lanes = pl.ds(pl.multiple_of(n * 256, 256), 256)
            product = jnp.dot(lt_ref[...], ref[:, lanes], preferred_element_type=F32)
            for k in range(2):
                base = pl.multiple_of(core * 512 + n * 128 + 64 * k, 64)
                for v in range(8):
                    for half in range(2):
                        at = 128 * v + 32 * half
                        low, high = mix(
                            product[at : at + 32, 128 * k : 128 * k + 128],
                            product[at + 64 : at + 96, 128 * k : 128 * k + 128],
                        )
                        place = (v % 2) * 256 + 128 * half
                        columns = slice(place, place + 128)
                        x_ref[v // 2, pl.ds(base, 32), columns] = low.astype(BF16)
                        x_ref[v // 2, pl.ds(base + 32, 32), columns] = high.astype(BF16)
            return carry

        lax.fori_loop(0, 4, some, 0, unroll=2)

    def finish(g, carry):
        update = jnp.dot(w_ref[...], x_ref[g], preferred_element_type=F32)
        places = [(half, 2 * g + e) for e in range(2) for half in range(2)]
        inv = jnp.concatenate([inv_ref[half, v] for half, v in places], axis=1)
        live = jnp.concatenate([plane_ref[half, v] for half, v in places], axis=1)
        before = jnp.concatenate(
            [pair_ref[half + 2 * k, v] for half, v in places for k in range(2)], axis=0
        )
        mid = (before.astype(F32) + (update * inv).T).astype(BF16)
        normed = layer_norm(mid).astype(BF16)
        terms = lax.dot_general(wp_ref[...], normed, NT, preferred_element_type=F32)
        ta = (jax.nn.sigmoid(terms[:128]) * terms[128:256] * live).astype(BF16)
        tb = (jax.nn.sigmoid(terms[256:384]) * terms[384:] * live).astype(BF16)
        for n, (half, v) in enumerate(places):
            for k in range(2):
                mid_ref[half + 2 * k, v] = mid[128 * n + 64 * k : 128 * n + 64 * k + 64]
            tri_ref[half, v, :128] = ta[:, 128 * n : 128 * n + 128]
            tri_ref[half, v, 128:] = tb[:, 128 * n : 128 * n + 128]
        return carry

    lax.fori_loop(0, 4, finish, 0, unroll=True)


def outer_update(core, left, own, other, weight, inv, live_plane, pairwise, wp):
    total = left.shape[0]
    vmem = pl.BlockSpec(memory_space=pltpu.VMEM)
    return pl.pallas_call(
        outer_kernel,
        in_specs=[pl.BlockSpec(memory_space=pltpu.SMEM)] + [vmem] * 8,
        out_shape=[
            jax.ShapeDtypeStruct((4, 8, 64, 128), BF16),
            jax.ShapeDtypeStruct((2, 8, 256, 128), BF16),
        ],
        scratch_shapes=[pltpu.VMEM((1024, total), BF16), pltpu.VMEM((4, 1024, 512), BF16)],
        compiler_params=params(20),
        name="outer_update",
    )(core, left, own, other, weight, inv, live_plane, pairwise, wp)


def triangle_kernel(in_ref, out_ref, a_ref, b_ref):
    def assemble(r, carry):
        base = pl.multiple_of(r * 32, 32)
        for t, ref in ((0, a_ref), (1, b_ref)):
            for m in range(4):
                low, high = mix(
                    in_ref[r * 8 + 2 * m, t].astype(F32), in_ref[r * 8 + 2 * m + 1, t].astype(F32)
                )
                ref[pl.ds(base, 16), 128 * m : 128 * m + 128] = low.astype(BF16)
                ref[pl.ds(base + 16, 16), 128 * m : 128 * m + 128] = high.astype(BF16)
        return carry

    lax.fori_loop(0, 16, assemble, 0)

    def multiply(g, carry):
        base = pl.multiple_of(g * 128, 128)
        c = lax.dot_general(a_ref[pl.ds(base, 128), :], b_ref[...], NT, preferred_element_type=F32)
        for part in range(4):
            for m in range(4):
                columns = slice(128 * m, 128 * m + 128)
                even, odd = mix(
                    c[32 * part : 32 * part + 16, columns], c[32 * part + 16 : 32 * part + 32, columns]
                )
                out_ref[(g * 4 + part) * 8 + 2 * m] = even.astype(BF16)
                out_ref[(g * 4 + part) * 8 + 2 * m + 1] = odd.astype(BF16)
        return carry

    lax.fori_loop(0, 4, multiply, 0)


def triangle(blocks):
    return pl.pallas_call(
        triangle_kernel,
        out_shape=jax.ShapeDtypeStruct((128, 16, 128), BF16),
        scratch_shapes=[pltpu.VMEM((512, 512), BF16), pltpu.VMEM((512, 512), BF16)],
        compiler_params=params(16),
        name="triangle",
    )(blocks)


def gate_kernel(mid_ref, wg_ref, out_ref):
    for u in range(16):
        mid = jnp.concatenate([mid_ref[u], mid_ref[16 + u]], axis=0)
        out_ref[u] = jax.nn.sigmoid(
            jnp.dot(layer_norm(mid).astype(BF16), wg_ref[...], preferred_element_type=F32)
        )


def gates(mid, wg):
    return pl.pallas_call(
        gate_kernel,
        out_shape=jax.ShapeDtypeStruct((16, 128, 128), F32),
        compiler_params=params(16),
        name="pair_gate",
    )(mid, wg)


def final_kernel(tri_ref, mid_ref, wt_ref, gate_ref, out_ref):
    for u in range(16):
        combined = tri_ref[u].astype(F32)
        centered = combined - jnp.mean(combined, axis=0, keepdims=True)
        variance = jnp.mean(centered * centered, axis=0, keepdims=True)
        normed = (centered * lax.rsqrt(variance + EPS)).astype(BF16)
        update = jnp.dot(wt_ref[...], normed, preferred_element_type=F32)
        mid = jnp.concatenate([mid_ref[u], mid_ref[16 + u]], axis=0)
        out = (mid.astype(F32) + gate_ref[u] * update.T).astype(BF16)
        out_ref[u] = out[:64]
        out_ref[16 + u] = out[64:]


def final(tri, mid, wt, gate):
    return pl.pallas_call(
        final_kernel,
        out_shape=jax.ShapeDtypeStruct((32, 64, 128), BF16),
        compiler_params=params(16),
        name="pair_final",
    )(tri, mid, wt, gate)


def copy_kernel(in_ref, out_ref):
    out_ref[...] = in_ref[...]


def copied(a):
    return pl.pallas_call(
        copy_kernel,
        out_shape=jax.ShapeDtypeStruct(a.shape, a.dtype),
        compiler_params=params(8),
        name="copied",
    )(a)


def body(
    alignment,
    pairwise,
    residue_mask,
    sequence_mask,
    attention_input_weight,
    attention_output_weight,
    bias_project,
    outer_factor_weight,
    outer_output,
    tri_project,
    tri_gate,
    tri_output,
):
    row = lax.axis_index(ROW)
    col = lax.axis_index(COL)
    core = lax.axis_index("core")
    swap = [(0, 1), (1, 0)]
    res_live = residue_mask.astype(F32)
    seq_live = sequence_mask.astype(F32)
    row_live = lax.dynamic_slice_in_dim(res_live, row * 32, 32)
    col_live = lax.dynamic_slice_in_dim(res_live, col * 64, 64)
    my_seqs = lax.dynamic_slice_in_dim(sequence_mask, col * 80 + row * 5, 5)
    scalars = jnp.concatenate([jnp.stack([core, lax.axis_index("y")]), my_seqs])

    blocks = lax.all_to_all(
        pair_bias(pairwise, bias_project.T).reshape(32, 64, 128),
        ROW + ("zh",),
        split_axis=0,
        concat_axis=0,
        tiled=True,
    )
    live_plane = row_live[:, None] * col_live[None, :]
    inv = 1.0 / jnp.maximum(jnp.sum(seq_live) * live_plane, 1.0)

    def pairs(a):
        return a.reshape(2, 16, 64).transpose(1, 0, 2).reshape(2, 8, 1, 128)

    weight = outer_output.reshape(32, 2, 16, 128).transpose(3, 2, 1, 0).reshape(128, 1024)
    wp = tri_project.reshape(128, 512).T
    wt = tri_output.T
    wl = outer_factor_weight[:, 0].T
    win = jnp.concatenate(
        [
            attention_input_weight.reshape(256, 1024).T,
            attention_output_weight,
            wl,
            wl,
            wl,
            wl,
            outer_factor_weight[:, 1].T,
        ],
        axis=0,
    )
    live_cols = jnp.broadcast_to(res_live[:, None], (512, 128))
    blocks, weight, wp, wt, inv, live_plane, win, live_cols, scalars = (
        lax.optimization_barrier(
            (
                blocks,
                weight,
                wp,
                wt,
                pairs(inv),
                pairs(live_plane),
                win,
                live_cols,
                scalars,
            )
        )
    )
    outgoing, bias_plane = lax.optimization_barrier(
        (alignment.reshape(16, 5, 32, 256), plane(blocks))
    )
    up, down = ([(i, (i + d) % 4) for i in range(4)] for d in (1, 3))
    left_plane = lax.ppermute(bias_plane, "y", up)
    right_plane = lax.ppermute(bias_plane, "y", down)
    far_plane = jnp.concatenate(
        [lax.ppermute(left_plane[:2], "y", up), lax.ppermute(right_plane[2:], "y", down)], axis=0
    )
    own = [bias_plane, left_plane, far_plane, right_plane]
    other = [lax.ppermute(b, "core", swap) for b in own]
    sequences = lax.all_to_all(outgoing, ROW, split_axis=0, concat_axis=0, tiled=True)
    out_seq, factors = attention(scalars, own + other, sequences, win, live_cols)
    factors = lax.all_to_all(
        factors.reshape(128, 80, 128), ALL, split_axis=0, concat_axis=0, tiled=True
    )
    out_seq, factors = lax.optimization_barrier((out_seq, factors))
    factors = factors.reshape(640, 16, 128)
    right_own = factors[:, 8:].reshape(640, 1024)
    right_other = lax.ppermute(right_own, "core", swap)
    left = factors[:, :8].reshape(640, 1024)
    alignment_output = lax.all_to_all(
        out_seq, ROW, split_axis=0, concat_axis=0, tiled=True
    ).reshape(80, 32, 256)

    mid, tri = outer_update(
        core.reshape(1),
        left,
        right_own,
        right_other,
        weight,
        inv,
        live_plane,
        pairwise.reshape(4, 8, 64, 128),
        wp,
    )
    tri = tri.reshape(16, 2, 128, 128).transpose(2, 1, 0, 3)
    tri, alignment_output = lax.optimization_barrier((tri, alignment_output))
    alignment_output = copied(alignment_output)
    blocks = lax.all_to_all(tri, ALL, split_axis=0, concat_axis=0, tiled=True)
    product, mid = lax.optimization_barrier((triangle(blocks), mid.reshape(32, 64, 128)))
    combined = lax.all_to_all(product, ALL, split_axis=0, concat_axis=0, tiled=True)
    pair_output_state = final(combined.transpose(1, 0, 2), mid, wt, gates(mid, tri_gate))
    return (alignment_output, pair_output_state)


def solution(mesh):
    fine = Mesh(mesh.devices.reshape(4, 2, 2, 2, 4), ALL)
    placed = (P(COL, ROW, None), P(ROW, COL, None)) + (P(),) * 10
    return jax.shard_map(
        body,
        mesh=fine,
        in_specs=placed,
        out_specs=(P(COL, ROW, None), P(ROW, COL, None)),
        check_vma=False,
    )
```

```python
import jax
import jax.numpy as jnp
from jax import lax
from jax.experimental import pallas as pl
from jax.experimental.pallas import tpu as pltpu
from jax.sharding import Mesh, PartitionSpec as P

EPS = 1e-05
BIG = 1000000000.0
LOG2E = 1.4426950408889634
F32 = jnp.float32
BF16 = jnp.bfloat16
ROW = ("x", "zl", "core")
COL = ("zh", "y")
ALL = ROW + COL
CHIP = ("x", "zl", "zh", "y")
NT = (((1,), (1,)), ((), ()))
TN = (((0,), (0,)), ((), ()))
MB = 1 << 20


def layer_norm(v):
    v = v.astype(F32)
    centered = v - jnp.mean(v, axis=-1, keepdims=True)
    variance = jnp.mean(centered * centered, axis=-1, keepdims=True)
    return centered * lax.rsqrt(variance + EPS)


def low_lanes(shape):
    return lax.broadcasted_iota(jnp.int32, shape, len(shape) - 1) < 64


def mix(first, second):
    keep = low_lanes(first.shape)
    turn = len(first.shape) - 1
    return (
        jnp.where(keep, first, pltpu.roll(second, 64, turn)),
        jnp.where(keep, pltpu.roll(first, 64, turn), second),
    )


def params(mib):
    return pltpu.CompilerParams(vmem_limit_bytes=mib * MB)


def bias_kernel(pair_ref, weight_ref, out_ref, normed_ref, bias_ref):
    normed_ref[...] = layer_norm(pair_ref[...])
    for w in range(16):
        block = jnp.concatenate([normed_ref[:, jq * 16 + w, :] for jq in range(4)], axis=0)
        bias_ref[:, w, :] = lax.dot_general(
            weight_ref[...], block.astype(BF16), NT, preferred_element_type=F32
        )
    for core in range(2):
        chunk = bias_ref[4 * core : 4 * core + 4].reshape(64, 128).astype(BF16)
        for xz in range(8):
            for zh in range(2):
                out_ref[xz, core, zh] = chunk


def pair_bias(pairwise, weight):
    return pl.pallas_call(
        bias_kernel,
        out_shape=jax.ShapeDtypeStruct((8, 2, 2, 64, 128), BF16),
        scratch_shapes=[pltpu.VMEM((32, 64, 128), F32), pltpu.VMEM((8, 16, 128), F32)],
        compiler_params=params(16),
        name="pair_bias",
    )(pairwise, weight)


def plane_kernel(in_ref, out_ref):
    group = lax.broadcasted_iota(jnp.int32, (16, 128), 1) // 32
    for zh in range(2):
        for hh in range(4):
            for x in range(4):
                parts = [
                    in_ref[(x * 4 + g) * 2 + zh, 16 * hh : 16 * hh + 16, :].astype(F32)
                    for g in range(4)
                ]
                for jq in range(4):
                    turned = [
                        part if g == jq else pltpu.roll(part, 32 * ((g - jq) % 4), 1)
                        for g, part in enumerate(parts)
                    ]
                    row = jnp.where(
                        group < 2,
                        jnp.where(group == 0, turned[0], turned[1]),
                        jnp.where(group == 2, turned[2], turned[3]),
                    )
                    base = 64 * zh + 16 * jq
                    out_ref[hh, base : base + 16, 128 * x : 128 * x + 128] = row.astype(BF16)


def plane(blocks):
    return pl.pallas_call(
        plane_kernel,
        out_shape=jax.ShapeDtypeStruct((4, 128, 512), BF16),
        compiler_params=params(8),
        name="bias_plane",
    )(blocks)


def attention_kernel(
    place_ref,
    own0_ref,
    own1_ref,
    own2_ref,
    own3_ref,
    other0_ref,
    other1_ref,
    other2_ref,
    other3_ref,
    x_ref,
    win_ref,
    live_col_ref,
    out_ref,
    factor_ref,
    bias_ref,
    qt_ref,
    k_ref,
    vt_ref,
    acc_ref,
    live_ref,
):
    heads = bias_ref.shape[0]
    step = pl.program_id(0)

    @pl.when(step == 0)
    def _():
        live_ref[...] = live_col_ref[...].T[:8]
        core, y = place_ref[0], place_ref[1]
        own = (own0_ref, own1_ref, own2_ref, own3_ref)
        other = (other0_ref, other1_ref, other2_ref, other3_ref)
        for refs, side in ((own, core), (other, 1 - core)):
            for d in range(4):
                source = lax.rem(y + 4 - d, 4)
                for zh in range(2):
                    rows = pl.ds(pl.multiple_of(256 * zh + 64 * source, 64), 64)
                    penalty = (live_col_ref[rows, :] - 1.0) * BIG
                    for m in range(4):
                        lanes = slice(128 * m, 128 * m + 128)
                        for hh in range(4):
                            bias_ref[4 * side + hh, rows, lanes] = (
                                refs[d][hh, 64 * zh : 64 * zh + 64, lanes].astype(F32) * LOG2E
                                + penalty
                            )

    x = x_ref[:, 0].reshape(512, 256)
    normed = layer_norm(x).astype(BF16)

    def project(t):
        return lax.dot_general(
            win_ref[256 * t : 256 * t + 256], normed, NT, preferred_element_type=F32
        )

    qt_ref[...] = (project(0) * (32 ** (-0.5) * LOG2E)).astype(BF16)
    k_ref[...] = lax.dot_general(
        normed, win_ref[256:512], NT, preferred_element_type=F32
    ).astype(BF16)
    vt_ref[:, :32] = project(2).astype(BF16).reshape(heads, 32, 512)
    vt_ref[:, 32:] = jnp.ones((heads, 16, 512), BF16)
    row_head = lax.broadcasted_iota(jnp.int32, (128, 512), 0) // 32

    def scores(h):
        lanes = slice(128 * (h // 4), 128 * (h // 4) + 128)
        q_h = jnp.where(row_head == h % 4, qt_ref[lanes, :], jnp.zeros((), BF16))
        s = jnp.dot(k_ref[:, lanes], q_h, preferred_element_type=F32) + bias_ref[h]
        return s, jnp.max(s, axis=0, keepdims=True)

    def values(h, p):
        o = jnp.dot(vt_ref[h], p, preferred_element_type=F32)
        acc_ref[32 * h : 32 * h + 32, :] = o[:32] / o[32:33]

    s, top = scores(0)
    p = None
    for h in range(heads):
        ahead = scores(h + 1) if h + 1 < heads else None
        if p is not None:
            values(h - 1, p)
        p = jnp.exp2(s - top).astype(BF16)
        if ahead is not None:
            s, top = ahead
    values(heads - 1, p)
    attended = (acc_ref[...] * jax.nn.sigmoid(project(3))).T.astype(BF16)
    out = (
        x.astype(F32) + jnp.dot(attended, win_ref[1024:1280], preferred_element_type=F32)
    ).astype(BF16)
    out_ref[:, 0] = out.reshape(16, 32, 256)
    second = layer_norm(out).astype(BF16)
    seq_live = place_ref[2 + step].astype(F32)
    left = lax.dot_general(second, win_ref[1280:1408], NT, preferred_element_type=F32)
    left = (left * (live_col_ref[...] * seq_live)).reshape(16, 4, 8, 128)
    group = lax.broadcasted_iota(jnp.int32, (16, 8, 128), 2) // 32
    packed = left[:, 0]
    for q in range(1, 4):
        packed = jnp.where(group == q, left[:, q], packed)
    right = lax.dot_general(win_ref[1408:1440], second, NT, preferred_element_type=F32)
    right = right * (live_ref[:1] * seq_live)
    for m in range(4):
        tile = right[:, 128 * m : 128 * m + 128]
        for c, chunk in enumerate(mix(tile[:16], tile[16:])):
            for core in range(2):
                half = chunk[8 * core : 8 * core + 8]
                for xz in range(8):
                    factor_ref[xz, core, 2 * m + c, 0] = jnp.concatenate(
                        [packed[2 * xz + core], half], axis=0
                    ).astype(BF16)


def attention(place, biases, x, win, live_col):
    count = x.shape[1]
    smem = pl.BlockSpec(memory_space=pltpu.SMEM)

    def whole(a):
        return pl.BlockSpec(a.shape, lambda s: (0,) * a.ndim)

    def per_seq(*dims):
        return pl.BlockSpec(dims, lambda s: (0, s) + (0,) * (len(dims) - 2))

    return pl.pallas_call(
        attention_kernel,
        grid=(count,),
        in_specs=[
            smem,
            *(whole(b) for b in biases),
            per_seq(16, 1, 32, 256),
            whole(win),
            whole(live_col),
        ],
        out_specs=[
            per_seq(16, 1, 32, 256),
            pl.BlockSpec((8, 2, 8, 1, 16, 128), lambda s: (0, 0, 0, s, 0, 0)),
        ],
        out_shape=[
            jax.ShapeDtypeStruct(x.shape, BF16),
            jax.ShapeDtypeStruct((8, 2, 8, count, 16, 128), BF16),
        ],
        scratch_shapes=[
            pltpu.VMEM((8, 512, 512), F32),
            pltpu.VMEM((256, 512), BF16),
            pltpu.VMEM((512, 256), BF16),
            pltpu.VMEM((8, 48, 512), BF16),
            pltpu.VMEM((256, 512), F32),
            pltpu.VMEM((8, 512), F32),
        ],
        compiler_params=params(52),
        name="row_attention",
    )(place, *biases, x, win, live_col)


def outer_kernel(
    core_ref,
    l_ref,
    own_ref,
    other_ref,
    w_ref,
    inv_ref,
    plane_ref,
    pair_ref,
    wp_ref,
    mid_ref,
    tri_ref,
    lt_ref,
    x_ref,
):
    for v in range(8):
        rows = slice(128 * v, 128 * v + 128)
        lt_ref[rows, :] = l_ref[:, rows].astype(F32).T.astype(BF16)
    for ref, core in ((own_ref, core_ref[0]), (other_ref, 1 - core_ref[0])):

        def some(n, carry):
            lanes = pl.ds(pl.multiple_of(n * 256, 256), 256)
            product = jnp.dot(lt_ref[...], ref[:, lanes], preferred_element_type=F32)
            for k in range(2):
                base = pl.multiple_of(core * 512 + n * 128 + 64 * k, 64)
                for v in range(8):
                    for half in range(2):
                        at = 128 * v + 32 * half
                        low, high = mix(
                            product[at : at + 32, 128 * k : 128 * k + 128],
                            product[at + 64 : at + 96, 128 * k : 128 * k + 128],
                        )
                        place = (v % 2) * 256 + 128 * half
                        columns = slice(place, place + 128)
                        x_ref[v // 2, pl.ds(base, 32), columns] = low.astype(BF16)
                        x_ref[v // 2, pl.ds(base + 32, 32), columns] = high.astype(BF16)
            return carry

        lax.fori_loop(0, 4, some, 0, unroll=2)

    def finish(g, carry):
        update = jnp.dot(w_ref[...], x_ref[g], preferred_element_type=F32)
        places = [(half, 2 * g + e) for e in range(2) for half in range(2)]
        inv = jnp.concatenate([inv_ref[half, v] for half, v in places], axis=1)
        live = jnp.concatenate([plane_ref[half, v] for half, v in places], axis=1)
        before = jnp.concatenate(
            [pair_ref[half + 2 * k, v] for half, v in places for k in range(2)], axis=0
        )
        mid = (before.astype(F32) + (update * inv).T).astype(BF16)
        normed = layer_norm(mid).astype(BF16)
        terms = lax.dot_general(wp_ref[...], normed, NT, preferred_element_type=F32)
        ta = (jax.nn.sigmoid(terms[:128]) * terms[128:256] * live).astype(BF16)
        tb = (jax.nn.sigmoid(terms[256:384]) * terms[384:] * live).astype(BF16)
        for n, (half, v) in enumerate(places):
            for k in range(2):
                mid_ref[half + 2 * k, v] = mid[128 * n + 64 * k : 128 * n + 64 * k + 64]
            tri_ref[half, v, :128] = ta[:, 128 * n : 128 * n + 128]
            tri_ref[half, v, 128:] = tb[:, 128 * n : 128 * n + 128]
        return carry

    lax.fori_loop(0, 4, finish, 0, unroll=True)


def outer_update(core, left, own, other, weight, inv, live_plane, pairwise, wp):
    total = left.shape[0]
    vmem = pl.BlockSpec(memory_space=pltpu.VMEM)
    return pl.pallas_call(
        outer_kernel,
        in_specs=[pl.BlockSpec(memory_space=pltpu.SMEM)] + [vmem] * 8,
        out_shape=[
            jax.ShapeDtypeStruct((4, 8, 64, 128), BF16),
            jax.ShapeDtypeStruct((2, 8, 256, 128), BF16),
        ],
        scratch_shapes=[pltpu.VMEM((1024, total), BF16), pltpu.VMEM((4, 1024, 512), BF16)],
        compiler_params=params(20),
        name="outer_update",
    )(core, left, own, other, weight, inv, live_plane, pairwise, wp)


def triangle_kernel(in_ref, out_ref, a_ref, b_ref):
    def assemble(r, carry):
        base = pl.multiple_of(r * 32, 32)
        for t, ref in ((0, a_ref), (1, b_ref)):
            for m in range(4):
                low, high = mix(
                    in_ref[r * 8 + 2 * m, t].astype(F32), in_ref[r * 8 + 2 * m + 1, t].astype(F32)
                )
                ref[pl.ds(base, 16), 128 * m : 128 * m + 128] = low.astype(BF16)
                ref[pl.ds(base + 16, 16), 128 * m : 128 * m + 128] = high.astype(BF16)
        return carry

    lax.fori_loop(0, 16, assemble, 0, unroll=True)

    def multiply(g, carry):
        base = pl.multiple_of(g * 128, 128)
        c = lax.dot_general(a_ref[pl.ds(base, 128), :], b_ref[...], NT, preferred_element_type=F32)
        for part in range(4):
            for m in range(4):
                columns = slice(128 * m, 128 * m + 128)
                even, odd = mix(
                    c[32 * part : 32 * part + 16, columns], c[32 * part + 16 : 32 * part + 32, columns]
                )
                out_ref[(g * 4 + part) * 8 + 2 * m] = even.astype(BF16)
                out_ref[(g * 4 + part) * 8 + 2 * m + 1] = odd.astype(BF16)
        return carry

    lax.fori_loop(0, 4, multiply, 0, unroll=True)


def triangle(blocks):
    return pl.pallas_call(
        triangle_kernel,
        out_shape=jax.ShapeDtypeStruct((128, 16, 128), BF16),
        scratch_shapes=[pltpu.VMEM((512, 512), BF16), pltpu.VMEM((512, 512), BF16)],
        compiler_params=params(16),
        name="triangle",
    )(blocks)


def gate_kernel(mid_ref, wg_ref, out_ref):
    for u in range(16):
        mid = jnp.concatenate([mid_ref[u], mid_ref[16 + u]], axis=0)
        out_ref[u] = jax.nn.sigmoid(
            jnp.dot(layer_norm(mid).astype(BF16), wg_ref[...], preferred_element_type=F32)
        )


def gates(mid, wg):
    return pl.pallas_call(
        gate_kernel,
        out_shape=jax.ShapeDtypeStruct((16, 128, 128), F32),
        compiler_params=params(16),
        name="pair_gate",
    )(mid, wg)


def final_kernel(tri_ref, mid_ref, wt_ref, gate_ref, out_ref):
    for u in range(16):
        combined = tri_ref[u].astype(F32)
        centered = combined - jnp.mean(combined, axis=0, keepdims=True)
        variance = jnp.mean(centered * centered, axis=0, keepdims=True)
        normed = (centered * lax.rsqrt(variance + EPS)).astype(BF16)
        update = jnp.dot(wt_ref[...], normed, preferred_element_type=F32)
        mid = jnp.concatenate([mid_ref[u], mid_ref[16 + u]], axis=0)
        out = (mid.astype(F32) + gate_ref[u] * update.T).astype(BF16)
        out_ref[u] = out[:64]
        out_ref[16 + u] = out[64:]


def final(tri, mid, wt, gate):
    return pl.pallas_call(
        final_kernel,
        out_shape=jax.ShapeDtypeStruct((32, 64, 128), BF16),
        compiler_params=params(16),
        name="pair_final",
    )(tri, mid, wt, gate)


def copy_kernel(in_ref, out_ref):
    out_ref[...] = in_ref[...]


def copied(a):
    return pl.pallas_call(
        copy_kernel,
        out_shape=jax.ShapeDtypeStruct(a.shape, a.dtype),
        compiler_params=params(8),
        name="copied",
    )(a)


def body(
    alignment,
    pairwise,
    residue_mask,
    sequence_mask,
    attention_input_weight,
    attention_output_weight,
    bias_project,
    outer_factor_weight,
    outer_output,
    tri_project,
    tri_gate,
    tri_output,
):
    row = lax.axis_index(ROW)
    col = lax.axis_index(COL)
    core = lax.axis_index("core")
    swap = [(0, 1), (1, 0)]
    res_live = residue_mask.astype(F32)
    seq_live = sequence_mask.astype(F32)
    row_live = lax.dynamic_slice_in_dim(res_live, row * 32, 32)
    col_live = lax.dynamic_slice_in_dim(res_live, col * 64, 64)
    my_seqs = lax.dynamic_slice_in_dim(sequence_mask, col * 80 + row * 5, 5)
    scalars = jnp.concatenate([jnp.stack([core, lax.axis_index("y")]), my_seqs])

    blocks = lax.all_to_all(
        pair_bias(pairwise, bias_project.T).reshape(32, 64, 128),
        ROW + ("zh",),
        split_axis=0,
        concat_axis=0,
        tiled=True,
    )
    live_plane = row_live[:, None] * col_live[None, :]
    inv = 1.0 / jnp.maximum(jnp.sum(seq_live) * live_plane, 1.0)

    def pairs(a):
        return a.reshape(2, 16, 64).transpose(1, 0, 2).reshape(2, 8, 1, 128)

    weight = outer_output.reshape(32, 2, 16, 128).transpose(3, 2, 1, 0).reshape(128, 1024)
    wp = tri_project.reshape(128, 512).T
    wt = tri_output.T
    wl = outer_factor_weight[:, 0].T
    win = jnp.concatenate(
        [
            attention_input_weight.reshape(256, 1024).T,
            attention_output_weight,
            wl,
            wl,
            wl,
            wl,
            outer_factor_weight[:, 1].T,
        ],
        axis=0,
    )
    live_cols = jnp.broadcast_to(res_live[:, None], (512, 128))
    blocks, weight, wp, wt, inv, live_plane, win, live_cols, scalars = (
        lax.optimization_barrier(
            (
                blocks,
                weight,
                wp,
                wt,
                pairs(inv),
                pairs(live_plane),
                win,
                live_cols,
                scalars,
            )
        )
    )
    outgoing, bias_plane = lax.optimization_barrier(
        (alignment.reshape(16, 5, 32, 256), plane(blocks))
    )
    up, down = ([(i, (i + d) % 4) for i in range(4)] for d in (1, 3))
    left_plane = lax.ppermute(bias_plane, "y", up)
    right_plane = lax.ppermute(bias_plane, "y", down)
    far_plane = jnp.concatenate(
        [lax.ppermute(left_plane[:2], "y", up), lax.ppermute(right_plane[2:], "y", down)], axis=0
    )
    own = [bias_plane, left_plane, far_plane, right_plane]
    other = [lax.ppermute(b, "core", swap) for b in own]
    sequences = lax.all_to_all(outgoing, ROW, split_axis=0, concat_axis=0, tiled=True)
    out_seq, factors = attention(scalars, own + other, sequences, win, live_cols)
    factors = lax.all_to_all(
        factors.reshape(128, 80, 128), ALL, split_axis=0, concat_axis=0, tiled=True
    )
    out_seq, factors = lax.optimization_barrier((out_seq, factors))
    factors, far_factors = lax.optimization_barrier(
        (factors, lax.ppermute(factors, "core", swap))
    )
    factors = factors.reshape(640, 16, 128)
    left = factors[:, :8].reshape(640, 1024)
    right_own = factors[:, 8:].reshape(640, 1024)
    right_other = far_factors.reshape(640, 16, 128)[:, 8:].reshape(640, 1024)
    alignment_output = lax.all_to_all(
        out_seq, ROW, split_axis=0, concat_axis=0, tiled=True
    ).reshape(80, 32, 256)

    mid, tri = outer_update(
        core.reshape(1),
        left,
        right_own,
        right_other,
        weight,
        inv,
        live_plane,
        pairwise.reshape(4, 8, 64, 128),
        wp,
    )
    tri = tri.reshape(16, 2, 128, 128).transpose(2, 1, 0, 3)
    tri, alignment_output = lax.optimization_barrier((tri, alignment_output))
    alignment_output = copied(alignment_output)
    blocks = lax.all_to_all(tri, ALL, split_axis=0, concat_axis=0, tiled=True)
    product, mid = lax.optimization_barrier((triangle(blocks), mid.reshape(32, 64, 128)))
    combined = lax.all_to_all(product, ALL, split_axis=0, concat_axis=0, tiled=True)
    pair_output_state = final(combined.transpose(1, 0, 2), mid, wt, gates(mid, tri_gate))
    return (alignment_output, pair_output_state)


def solution(mesh):
    fine = Mesh(mesh.devices.reshape(4, 2, 2, 2, 4), ALL)
    placed = (P(COL, ROW, None), P(ROW, COL, None)) + (P(),) * 10
    return jax.shard_map(
        body,
        mesh=fine,
        in_specs=placed,
        out_specs=(P(COL, ROW, None), P(ROW, COL, None)),
        check_vma=False,
    )
```

```python
import jax
import jax.numpy as jnp
from jax import lax
from jax.experimental import pallas as pl
from jax.experimental.pallas import tpu as pltpu
from jax.sharding import Mesh, PartitionSpec as P

EPS = 1e-05
BIG = 1000000000.0
LOG2E = 1.4426950408889634
F32 = jnp.float32
BF16 = jnp.bfloat16
ROW = ("x", "zl", "core")
COL = ("zh", "y")
ALL = ROW + COL
CHIP = ("x", "zl", "zh", "y")
NT = (((1,), (1,)), ((), ()))
TN = (((0,), (0,)), ((), ()))
MB = 1 << 20


def layer_norm(v):
    v = v.astype(F32)
    centered = v - jnp.mean(v, axis=-1, keepdims=True)
    variance = jnp.mean(centered * centered, axis=-1, keepdims=True)
    return centered * lax.rsqrt(variance + EPS)


def low_lanes(shape):
    return lax.broadcasted_iota(jnp.int32, shape, len(shape) - 1) < 64


def mix(first, second):
    keep = low_lanes(first.shape)
    turn = len(first.shape) - 1
    return (
        jnp.where(keep, first, pltpu.roll(second, 64, turn)),
        jnp.where(keep, pltpu.roll(first, 64, turn), second),
    )


def params(mib):
    return pltpu.CompilerParams(vmem_limit_bytes=mib * MB)


def bias_kernel(pair_ref, weight_ref, out_ref, normed_ref, bias_ref):
    normed_ref[...] = layer_norm(pair_ref[...])
    for w in range(16):
        block = jnp.concatenate([normed_ref[:, jq * 16 + w, :] for jq in range(4)], axis=0)
        bias_ref[:, w, :] = lax.dot_general(
            weight_ref[...], block.astype(BF16), NT, preferred_element_type=F32
        )
    for core in range(2):
        chunk = bias_ref[4 * core : 4 * core + 4].reshape(64, 128).astype(BF16)
        for xz in range(8):
            for zh in range(2):
                out_ref[xz, core, zh] = chunk


def pair_bias(pairwise, weight):
    return pl.pallas_call(
        bias_kernel,
        out_shape=jax.ShapeDtypeStruct((8, 2, 2, 64, 128), BF16),
        scratch_shapes=[pltpu.VMEM((32, 64, 128), F32), pltpu.VMEM((8, 16, 128), F32)],
        compiler_params=params(16),
        name="pair_bias",
    )(pairwise, weight)


def plane_kernel(in_ref, out_ref):
    group = lax.broadcasted_iota(jnp.int32, (16, 128), 1) // 32
    for zh in range(2):
        for hh in range(4):
            for x in range(4):
                parts = [
                    in_ref[(x * 4 + g) * 2 + zh, 16 * hh : 16 * hh + 16, :].astype(F32)
                    for g in range(4)
                ]
                for jq in range(4):
                    turned = [
                        part if g == jq else pltpu.roll(part, 32 * ((g - jq) % 4), 1)
                        for g, part in enumerate(parts)
                    ]
                    row = jnp.where(
                        group < 2,
                        jnp.where(group == 0, turned[0], turned[1]),
                        jnp.where(group == 2, turned[2], turned[3]),
                    )
                    base = 64 * zh + 16 * jq
                    out_ref[hh, base : base + 16, 128 * x : 128 * x + 128] = row.astype(BF16)


def plane(blocks):
    return pl.pallas_call(
        plane_kernel,
        out_shape=jax.ShapeDtypeStruct((4, 128, 512), BF16),
        compiler_params=params(8),
        name="bias_plane",
    )(blocks)


def attention_kernel(
    place_ref,
    own0_ref,
    own1_ref,
    own2_ref,
    own3_ref,
    other0_ref,
    other1_ref,
    other2_ref,
    other3_ref,
    x_ref,
    win_ref,
    live_col_ref,
    out_ref,
    factor_ref,
    bias_ref,
    qt_ref,
    k_ref,
    vt_ref,
    acc_ref,
    live_ref,
    plane_ref,
    sem_ref,
):
    heads = bias_ref.shape[0]
    step = pl.program_id(0)

    copies = [
        pltpu.make_async_copy(ref, plane_ref.at[n], sem_ref.at[n])
        for n, ref in enumerate(
            (
                own0_ref,
                own1_ref,
                own2_ref,
                own3_ref,
                other0_ref,
                other1_ref,
                other2_ref,
                other3_ref,
            )
        )
    ]

    @pl.when(step == 0)
    def _():
        for copy in copies:
            copy.start()

    x = x_ref[:, 0].reshape(512, 256)
    normed = layer_norm(x).astype(BF16)

    def project(t):
        return lax.dot_general(
            win_ref[256 * t : 256 * t + 256], normed, NT, preferred_element_type=F32
        )

    qt_ref[...] = (project(0) * (32 ** (-0.5) * LOG2E)).astype(BF16)
    k_ref[...] = lax.dot_general(
        normed, win_ref[256:512], NT, preferred_element_type=F32
    ).astype(BF16)
    vt_ref[:, :32] = project(2).astype(BF16).reshape(heads, 32, 512)
    vt_ref[:, 32:] = jnp.ones((heads, 16, 512), BF16)
    @pl.when(step == 0)
    def _():
        live_ref[...] = live_col_ref[...].T[:8]
        core, y = place_ref[0], place_ref[1]
        for n, copy in enumerate(copies):
            copy.wait()
            side = core if n < 4 else 1 - core
            source = lax.rem(y + 4 - n % 4, 4)
            for zh in range(2):
                rows = pl.ds(pl.multiple_of(256 * zh + 64 * source, 64), 64)
                penalty = (live_col_ref[rows, :] - 1.0) * BIG
                for m in range(4):
                    lanes = slice(128 * m, 128 * m + 128)
                    for hh in range(4):
                        part = plane_ref[n, hh, 64 * zh : 64 * zh + 64, lanes]
                        bias_ref[4 * side + hh, rows, lanes] = part.astype(F32) * LOG2E + penalty

    row_head = lax.broadcasted_iota(jnp.int32, (128, 512), 0) // 32

    def scores(h):
        lanes = slice(128 * (h // 4), 128 * (h // 4) + 128)
        q_h = jnp.where(row_head == h % 4, qt_ref[lanes, :], jnp.zeros((), BF16))
        s = jnp.dot(k_ref[:, lanes], q_h, preferred_element_type=F32) + bias_ref[h]
        return s, jnp.max(s, axis=0, keepdims=True)

    def values(h, p):
        o = jnp.dot(vt_ref[h], p, preferred_element_type=F32)
        acc_ref[32 * h : 32 * h + 32, :] = o[:32] / o[32:33]

    s, top = scores(0)
    p = None
    for h in range(heads):
        ahead = scores(h + 1) if h + 1 < heads else None
        if p is not None:
            values(h - 1, p)
        p = jnp.exp2(s - top).astype(BF16)
        if ahead is not None:
            s, top = ahead
    values(heads - 1, p)
    attended = (acc_ref[...] * jax.nn.sigmoid(project(3))).T.astype(BF16)
    out = (
        x.astype(F32) + jnp.dot(attended, win_ref[1024:1280], preferred_element_type=F32)
    ).astype(BF16)
    out_ref[:, 0] = out.reshape(16, 32, 256)
    second = layer_norm(out).astype(BF16)
    seq_live = place_ref[2 + step].astype(F32)
    left = lax.dot_general(second, win_ref[1280:1408], NT, preferred_element_type=F32)
    left = (left * (live_col_ref[...] * seq_live)).reshape(16, 4, 8, 128)
    group = lax.broadcasted_iota(jnp.int32, (16, 8, 128), 2) // 32
    packed = left[:, 0]
    for q in range(1, 4):
        packed = jnp.where(group == q, left[:, q], packed)
    right = lax.dot_general(win_ref[1408:1440], second, NT, preferred_element_type=F32)
    right = right * (live_ref[:1] * seq_live)
    for m in range(4):
        tile = right[:, 128 * m : 128 * m + 128]
        for c, chunk in enumerate(mix(tile[:16], tile[16:])):
            for core in range(2):
                half = chunk[8 * core : 8 * core + 8]
                for xz in range(8):
                    factor_ref[xz, core, 2 * m + c, 0] = jnp.concatenate(
                        [packed[2 * xz + core], half], axis=0
                    ).astype(BF16)


def attention(place, biases, x, win, live_col):
    count = x.shape[1]
    smem = pl.BlockSpec(memory_space=pltpu.SMEM)

    def whole(a):
        return pl.BlockSpec(a.shape, lambda s: (0,) * a.ndim)

    def per_seq(*dims):
        return pl.BlockSpec(dims, lambda s: (0, s) + (0,) * (len(dims) - 2))

    return pl.pallas_call(
        attention_kernel,
        grid=(count,),
        in_specs=[
            smem,
            *(pl.BlockSpec(memory_space=pl.ANY) for _ in biases),
            per_seq(16, 1, 32, 256),
            whole(win),
            whole(live_col),
        ],
        out_specs=[
            per_seq(16, 1, 32, 256),
            pl.BlockSpec((8, 2, 8, 1, 16, 128), lambda s: (0, 0, 0, s, 0, 0)),
        ],
        out_shape=[
            jax.ShapeDtypeStruct(x.shape, BF16),
            jax.ShapeDtypeStruct((8, 2, 8, count, 16, 128), BF16),
        ],
        scratch_shapes=[
            pltpu.VMEM((8, 512, 512), F32),
            pltpu.VMEM((256, 512), BF16),
            pltpu.VMEM((512, 256), BF16),
            pltpu.VMEM((8, 48, 512), BF16),
            pltpu.VMEM((256, 512), F32),
            pltpu.VMEM((8, 512), F32),
            pltpu.VMEM((8, 4, 128, 512), BF16),
            pltpu.SemaphoreType.DMA((8,)),
        ],
        compiler_params=params(52),
        name="row_attention",
    )(place, *biases, x, win, live_col)


def outer_kernel(
    core_ref,
    l_ref,
    own_ref,
    other_ref,
    w_ref,
    inv_ref,
    plane_ref,
    pair_ref,
    wp_ref,
    mid_ref,
    tri_ref,
    lt_ref,
    x_ref,
):
    for v in range(8):
        rows = slice(128 * v, 128 * v + 128)
        lt_ref[rows, :] = l_ref[:, rows].astype(F32).T.astype(BF16)
    for ref, core in ((own_ref, core_ref[0]), (other_ref, 1 - core_ref[0])):

        def some(n, carry):
            lanes = pl.ds(pl.multiple_of(n * 256, 256), 256)
            product = jnp.dot(lt_ref[...], ref[:, lanes], preferred_element_type=F32)
            for k in range(2):
                base = pl.multiple_of(core * 512 + n * 128 + 64 * k, 64)
                for v in range(8):
                    for half in range(2):
                        at = 128 * v + 32 * half
                        low, high = mix(
                            product[at : at + 32, 128 * k : 128 * k + 128],
                            product[at + 64 : at + 96, 128 * k : 128 * k + 128],
                        )
                        place = (v % 2) * 256 + 128 * half
                        columns = slice(place, place + 128)
                        x_ref[v // 2, pl.ds(base, 32), columns] = low.astype(BF16)
                        x_ref[v // 2, pl.ds(base + 32, 32), columns] = high.astype(BF16)
            return carry

        lax.fori_loop(0, 4, some, 0, unroll=2)

    def finish(g, carry):
        update = jnp.dot(w_ref[...], x_ref[g], preferred_element_type=F32)
        places = [(half, 2 * g + e) for e in range(2) for half in range(2)]
        inv = jnp.concatenate([inv_ref[half, v] for half, v in places], axis=1)
        live = jnp.concatenate([plane_ref[half, v] for half, v in places], axis=1)
        before = jnp.concatenate(
            [pair_ref[half + 2 * k, v] for half, v in places for k in range(2)], axis=0
        )
        mid = (before.astype(F32) + (update * inv).T).astype(BF16)
        normed = layer_norm(mid).astype(BF16)
        terms = lax.dot_general(wp_ref[...], normed, NT, preferred_element_type=F32)
        ta = (jax.nn.sigmoid(terms[:128]) * terms[128:256] * live).astype(BF16)
        tb = (jax.nn.sigmoid(terms[256:384]) * terms[384:] * live).astype(BF16)
        for n, (half, v) in enumerate(places):
            for k in range(2):
                mid_ref[half + 2 * k, v] = mid[128 * n + 64 * k : 128 * n + 64 * k + 64]
            tri_ref[half, v, :128] = ta[:, 128 * n : 128 * n + 128]
            tri_ref[half, v, 128:] = tb[:, 128 * n : 128 * n + 128]
        return carry

    lax.fori_loop(0, 4, finish, 0, unroll=True)


def outer_update(core, left, own, other, weight, inv, live_plane, pairwise, wp):
    total = left.shape[0]
    vmem = pl.BlockSpec(memory_space=pltpu.VMEM)
    return pl.pallas_call(
        outer_kernel,
        in_specs=[pl.BlockSpec(memory_space=pltpu.SMEM)] + [vmem] * 8,
        out_shape=[
            jax.ShapeDtypeStruct((4, 8, 64, 128), BF16),
            jax.ShapeDtypeStruct((2, 8, 256, 128), BF16),
        ],
        scratch_shapes=[pltpu.VMEM((1024, total), BF16), pltpu.VMEM((4, 1024, 512), BF16)],
        compiler_params=params(20),
        name="outer_update",
    )(core, left, own, other, weight, inv, live_plane, pairwise, wp)


def triangle_kernel(in_ref, out_ref, a_ref, b_ref):
    def assemble(r, carry):
        base = pl.multiple_of(r * 32, 32)
        for t, ref in ((0, a_ref), (1, b_ref)):
            for m in range(4):
                low, high = mix(
                    in_ref[r * 8 + 2 * m, t].astype(F32), in_ref[r * 8 + 2 * m + 1, t].astype(F32)
                )
                ref[pl.ds(base, 16), 128 * m : 128 * m + 128] = low.astype(BF16)
                ref[pl.ds(base + 16, 16), 128 * m : 128 * m + 128] = high.astype(BF16)
        return carry

    lax.fori_loop(0, 16, assemble, 0, unroll=True)

    def multiply(g, carry):
        base = pl.multiple_of(g * 128, 128)
        c = lax.dot_general(a_ref[pl.ds(base, 128), :], b_ref[...], NT, preferred_element_type=F32)
        for part in range(4):
            for m in range(4):
                columns = slice(128 * m, 128 * m + 128)
                even, odd = mix(
                    c[32 * part : 32 * part + 16, columns], c[32 * part + 16 : 32 * part + 32, columns]
                )
                out_ref[(g * 4 + part) * 8 + 2 * m] = even.astype(BF16)
                out_ref[(g * 4 + part) * 8 + 2 * m + 1] = odd.astype(BF16)
        return carry

    lax.fori_loop(0, 4, multiply, 0, unroll=True)


def triangle(blocks):
    return pl.pallas_call(
        triangle_kernel,
        out_shape=jax.ShapeDtypeStruct((128, 16, 128), BF16),
        scratch_shapes=[pltpu.VMEM((512, 512), BF16), pltpu.VMEM((512, 512), BF16)],
        compiler_params=params(16),
        name="triangle",
    )(blocks)


def gate_kernel(mid_ref, wg_ref, out_ref):
    for u in range(16):
        mid = jnp.concatenate([mid_ref[u], mid_ref[16 + u]], axis=0)
        out_ref[u] = jax.nn.sigmoid(
            jnp.dot(layer_norm(mid).astype(BF16), wg_ref[...], preferred_element_type=F32)
        )


def gates(mid, wg):
    return pl.pallas_call(
        gate_kernel,
        out_shape=jax.ShapeDtypeStruct((16, 128, 128), F32),
        compiler_params=params(16),
        name="pair_gate",
    )(mid, wg)


def final_kernel(tri_ref, mid_ref, wt_ref, gate_ref, out_ref):
    for u in range(16):
        combined = tri_ref[u].astype(F32)
        centered = combined - jnp.mean(combined, axis=0, keepdims=True)
        variance = jnp.mean(centered * centered, axis=0, keepdims=True)
        normed = (centered * lax.rsqrt(variance + EPS)).astype(BF16)
        update = jnp.dot(wt_ref[...], normed, preferred_element_type=F32)
        mid = jnp.concatenate([mid_ref[u], mid_ref[16 + u]], axis=0)
        out = (mid.astype(F32) + gate_ref[u] * update.T).astype(BF16)
        out_ref[u] = out[:64]
        out_ref[16 + u] = out[64:]


def final(tri, mid, wt, gate):
    return pl.pallas_call(
        final_kernel,
        out_shape=jax.ShapeDtypeStruct((32, 64, 128), BF16),
        compiler_params=params(16),
        name="pair_final",
    )(tri, mid, wt, gate)


def copy_kernel(in_ref, out_ref):
    out_ref[...] = in_ref[...]


def copied(a):
    return pl.pallas_call(
        copy_kernel,
        out_shape=jax.ShapeDtypeStruct(a.shape, a.dtype),
        compiler_params=params(8),
        name="copied",
    )(a)


def body(
    alignment,
    pairwise,
    residue_mask,
    sequence_mask,
    attention_input_weight,
    attention_output_weight,
    bias_project,
    outer_factor_weight,
    outer_output,
    tri_project,
    tri_gate,
    tri_output,
):
    row = lax.axis_index(ROW)
    col = lax.axis_index(COL)
    core = lax.axis_index("core")
    swap = [(0, 1), (1, 0)]
    res_live = residue_mask.astype(F32)
    seq_live = sequence_mask.astype(F32)
    row_live = lax.dynamic_slice_in_dim(res_live, row * 32, 32)
    col_live = lax.dynamic_slice_in_dim(res_live, col * 64, 64)
    my_seqs = lax.dynamic_slice_in_dim(sequence_mask, col * 80 + row * 5, 5)
    scalars = jnp.concatenate([jnp.stack([core, lax.axis_index("y")]), my_seqs])

    blocks = lax.all_to_all(
        pair_bias(pairwise, bias_project.T).reshape(32, 64, 128),
        ROW + ("zh",),
        split_axis=0,
        concat_axis=0,
        tiled=True,
    )
    live_plane = row_live[:, None] * col_live[None, :]
    inv = 1.0 / jnp.maximum(jnp.sum(seq_live) * live_plane, 1.0)

    def pairs(a):
        return a.reshape(2, 16, 64).transpose(1, 0, 2).reshape(2, 8, 1, 128)

    weight = outer_output.reshape(32, 2, 16, 128).transpose(3, 2, 1, 0).reshape(128, 1024)
    wp = tri_project.reshape(128, 512).T
    wt = tri_output.T
    wl = outer_factor_weight[:, 0].T
    win = jnp.concatenate(
        [
            attention_input_weight.reshape(256, 1024).T,
            attention_output_weight,
            wl,
            wl,
            wl,
            wl,
            outer_factor_weight[:, 1].T,
        ],
        axis=0,
    )
    live_cols = jnp.broadcast_to(res_live[:, None], (512, 128))
    blocks, weight, wp, wt, inv, live_plane, win, live_cols, scalars = (
        lax.optimization_barrier(
            (
                blocks,
                weight,
                wp,
                wt,
                pairs(inv),
                pairs(live_plane),
                win,
                live_cols,
                scalars,
            )
        )
    )
    outgoing, bias_plane = lax.optimization_barrier(
        (alignment.reshape(16, 5, 32, 256), plane(blocks))
    )
    up, down = ([(i, (i + d) % 4) for i in range(4)] for d in (1, 3))
    left_plane = lax.ppermute(bias_plane, "y", up)
    right_plane = lax.ppermute(bias_plane, "y", down)
    far_plane = jnp.concatenate(
        [lax.ppermute(left_plane[:2], "y", up), lax.ppermute(right_plane[2:], "y", down)], axis=0
    )
    own = [bias_plane, left_plane, far_plane, right_plane]
    other = [lax.ppermute(b, "core", swap) for b in own]
    sequences = lax.all_to_all(outgoing, ROW, split_axis=0, concat_axis=0, tiled=True)
    out_seq, factors = attention(scalars, own + other, sequences, win, live_cols)
    factors = lax.all_to_all(
        factors.reshape(128, 80, 128), ALL, split_axis=0, concat_axis=0, tiled=True
    )
    out_seq, factors = lax.optimization_barrier((out_seq, factors))
    factors, far_factors = lax.optimization_barrier(
        (factors, lax.ppermute(factors, "core", swap))
    )
    factors = factors.reshape(640, 16, 128)
    left = factors[:, :8].reshape(640, 1024)
    right_own = factors[:, 8:].reshape(640, 1024)
    right_other = far_factors.reshape(640, 16, 128)[:, 8:].reshape(640, 1024)
    alignment_output = lax.all_to_all(
        out_seq, ROW, split_axis=0, concat_axis=0, tiled=True
    ).reshape(80, 32, 256)

    mid, tri = outer_update(
        core.reshape(1),
        left,
        right_own,
        right_other,
        weight,
        inv,
        live_plane,
        pairwise.reshape(4, 8, 64, 128),
        wp,
    )
    tri = tri.reshape(16, 2, 128, 128).transpose(2, 1, 0, 3)
    tri, alignment_output = lax.optimization_barrier((tri, alignment_output))
    alignment_output = copied(alignment_output)
    blocks = lax.all_to_all(tri, ALL, split_axis=0, concat_axis=0, tiled=True)
    product, mid = lax.optimization_barrier((triangle(blocks), mid.reshape(32, 64, 128)))
    combined = lax.all_to_all(product, ALL, split_axis=0, concat_axis=0, tiled=True)
    pair_output_state = final(combined.transpose(1, 0, 2), mid, wt, gates(mid, tri_gate))
    return (alignment_output, pair_output_state)


def solution(mesh):
    fine = Mesh(mesh.devices.reshape(4, 2, 2, 2, 4), ALL)
    placed = (P(COL, ROW, None), P(ROW, COL, None)) + (P(),) * 10
    return jax.shard_map(
        body,
        mesh=fine,
        in_specs=placed,
        out_specs=(P(COL, ROW, None), P(ROW, COL, None)),
        check_vma=False,
    )
```

```python
import jax
import jax.numpy as jnp
from jax import lax
from jax.experimental import pallas as pl
from jax.experimental.pallas import tpu as pltpu
from jax.sharding import Mesh, PartitionSpec as P

EPS = 1e-05
BIG = 1000000000.0
LOG2E = 1.4426950408889634
F32 = jnp.float32
BF16 = jnp.bfloat16
ROW = ("x", "zl", "core")
COL = ("zh", "y")
ALL = ROW + COL
CHIP = ("x", "zl", "zh", "y")
NT = (((1,), (1,)), ((), ()))
TN = (((0,), (0,)), ((), ()))
MB = 1 << 20


def layer_norm(v):
    v = v.astype(F32)
    centered = v - jnp.mean(v, axis=-1, keepdims=True)
    variance = jnp.mean(centered * centered, axis=-1, keepdims=True)
    return centered * lax.rsqrt(variance + EPS)


def low_lanes(shape):
    return lax.broadcasted_iota(jnp.int32, shape, len(shape) - 1) < 64


def mix(first, second):
    keep = low_lanes(first.shape)
    turn = len(first.shape) - 1
    return (
        jnp.where(keep, first, pltpu.roll(second, 64, turn)),
        jnp.where(keep, pltpu.roll(first, 64, turn), second),
    )


def params(mib):
    return pltpu.CompilerParams(vmem_limit_bytes=mib * MB)


def bias_kernel(pair_ref, weight_ref, out_ref, normed_ref, bias_ref, held_ref, sem_ref):
    copies = [
        pltpu.make_async_copy(
            pair_ref.at[pl.ds(8 * n, 8)], held_ref.at[pl.ds(8 * n, 8)], sem_ref.at[n]
        )
        for n in range(4)
    ]
    for copy in copies:
        copy.start()
    for n, copy in enumerate(copies):
        copy.wait()
        normed_ref[8 * n : 8 * n + 8] = layer_norm(held_ref[8 * n : 8 * n + 8])
    for w in range(16):
        block = jnp.concatenate([normed_ref[:, jq * 16 + w, :] for jq in range(4)], axis=0)
        bias_ref[:, w, :] = lax.dot_general(
            weight_ref[...], block.astype(BF16), NT, preferred_element_type=F32
        )
    for core in range(2):
        chunk = bias_ref[4 * core : 4 * core + 4].reshape(64, 128).astype(BF16)
        for xz in range(8):
            for zh in range(2):
                out_ref[xz, core, zh] = chunk


def pair_bias(pairwise, weight):
    return pl.pallas_call(
        bias_kernel,
        out_shape=jax.ShapeDtypeStruct((8, 2, 2, 64, 128), BF16),
        in_specs=[
            pl.BlockSpec(memory_space=pl.ANY),
            pl.BlockSpec(memory_space=pltpu.VMEM),
        ],
        scratch_shapes=[
            pltpu.VMEM((32, 64, 128), F32),
            pltpu.VMEM((8, 16, 128), F32),
            pltpu.VMEM((32, 64, 128), BF16),
            pltpu.SemaphoreType.DMA((4,)),
        ],
        compiler_params=params(60),
        name="pair_bias",
    )(pairwise, weight)


def plane_kernel(in_ref, out_ref):
    group = lax.broadcasted_iota(jnp.int32, (16, 128), 1) // 32
    for zh in range(2):
        for hh in range(4):
            for x in range(4):
                parts = [
                    in_ref[(x * 4 + g) * 2 + zh, 16 * hh : 16 * hh + 16, :].astype(F32)
                    for g in range(4)
                ]
                for jq in range(4):
                    turned = [
                        part if g == jq else pltpu.roll(part, 32 * ((g - jq) % 4), 1)
                        for g, part in enumerate(parts)
                    ]
                    row = jnp.where(
                        group < 2,
                        jnp.where(group == 0, turned[0], turned[1]),
                        jnp.where(group == 2, turned[2], turned[3]),
                    )
                    base = 64 * zh + 16 * jq
                    out_ref[hh, base : base + 16, 128 * x : 128 * x + 128] = row.astype(BF16)


def plane(blocks):
    return pl.pallas_call(
        plane_kernel,
        out_shape=jax.ShapeDtypeStruct((4, 128, 512), BF16),
        compiler_params=params(8),
        name="bias_plane",
    )(blocks)


def attention_kernel(
    place_ref,
    own0_ref,
    own1_ref,
    own2_ref,
    own3_ref,
    other0_ref,
    other1_ref,
    other2_ref,
    other3_ref,
    x_ref,
    win_ref,
    live_col_ref,
    out_ref,
    factor_ref,
    bias_ref,
    qt_ref,
    k_ref,
    vt_ref,
    acc_ref,
    live_ref,
):
    heads = bias_ref.shape[0]
    step = pl.program_id(0)

    @pl.when(step == 0)
    def _():
        live_ref[...] = live_col_ref[...].T[:8]
        core, y = place_ref[0], place_ref[1]
        own = (own0_ref, own1_ref, own2_ref, own3_ref)
        other = (other0_ref, other1_ref, other2_ref, other3_ref)
        for refs, side in ((own, core), (other, 1 - core)):
            for d in range(4):
                source = lax.rem(y + 4 - d, 4)
                for zh in range(2):
                    rows = pl.ds(pl.multiple_of(256 * zh + 64 * source, 64), 64)
                    penalty = (live_col_ref[rows, :] - 1.0) * BIG
                    for m in range(4):
                        lanes = slice(128 * m, 128 * m + 128)
                        for hh in range(4):
                            bias_ref[4 * side + hh, rows, lanes] = (
                                refs[d][hh, 64 * zh : 64 * zh + 64, lanes].astype(F32) * LOG2E
                                + penalty
                            )

    x = x_ref[:, 0].reshape(512, 256)
    normed = layer_norm(x).astype(BF16)

    def project(t):
        return lax.dot_general(
            win_ref[256 * t : 256 * t + 256], normed, NT, preferred_element_type=F32
        )

    qt_ref[...] = (project(0) * (32 ** (-0.5) * LOG2E)).astype(BF16)
    k_ref[...] = lax.dot_general(
        normed, win_ref[256:512], NT, preferred_element_type=F32
    ).astype(BF16)
    vt_ref[:, :32] = project(2).astype(BF16).reshape(heads, 32, 512)
    vt_ref[:, 32:] = jnp.ones((heads, 16, 512), BF16)
    row_head = lax.broadcasted_iota(jnp.int32, (128, 512), 0) // 32

    def scores(h):
        lanes = slice(128 * (h // 4), 128 * (h // 4) + 128)
        q_h = jnp.where(row_head == h % 4, qt_ref[lanes, :], jnp.zeros((), BF16))
        s = jnp.dot(k_ref[:, lanes], q_h, preferred_element_type=F32) + bias_ref[h]
        return s, jnp.max(s, axis=0, keepdims=True)

    def values(h, p):
        o = jnp.dot(vt_ref[h], p, preferred_element_type=F32)
        acc_ref[32 * h : 32 * h + 32, :] = o[:32] / o[32:33]

    s, top = scores(0)
    p = None
    for h in range(heads):
        ahead = scores(h + 1) if h + 1 < heads else None
        if p is not None:
            values(h - 1, p)
        p = jnp.exp2(s - top).astype(BF16)
        if ahead is not None:
            s, top = ahead
    values(heads - 1, p)
    attended = (acc_ref[...] * jax.nn.sigmoid(project(3))).T.astype(BF16)
    out = (
        x.astype(F32) + jnp.dot(attended, win_ref[1024:1280], preferred_element_type=F32)
    ).astype(BF16)
    out_ref[:, 0] = out.reshape(16, 32, 256)
    second = layer_norm(out).astype(BF16)
    seq_live = place_ref[2 + step].astype(F32)
    left = lax.dot_general(second, win_ref[1280:1408], NT, preferred_element_type=F32)
    left = (left * (live_col_ref[...] * seq_live)).reshape(16, 4, 8, 128)
    group = lax.broadcasted_iota(jnp.int32, (16, 8, 128), 2) // 32
    packed = left[:, 0]
    for q in range(1, 4):
        packed = jnp.where(group == q, left[:, q], packed)
    right = lax.dot_general(win_ref[1408:1440], second, NT, preferred_element_type=F32)
    right = right * (live_ref[:1] * seq_live)
    for m in range(4):
        tile = right[:, 128 * m : 128 * m + 128]
        for c, chunk in enumerate(mix(tile[:16], tile[16:])):
            for core in range(2):
                half = chunk[8 * core : 8 * core + 8]
                for xz in range(8):
                    factor_ref[xz, core, 2 * m + c, 0] = jnp.concatenate(
                        [packed[2 * xz + core], half], axis=0
                    ).astype(BF16)


def attention(place, biases, x, win, live_col):
    count = x.shape[1]
    smem = pl.BlockSpec(memory_space=pltpu.SMEM)

    def whole(a):
        return pl.BlockSpec(a.shape, lambda s: (0,) * a.ndim)

    def per_seq(*dims):
        return pl.BlockSpec(dims, lambda s: (0, s) + (0,) * (len(dims) - 2))

    return pl.pallas_call(
        attention_kernel,
        grid=(count,),
        in_specs=[
            smem,
            *(whole(b) for b in biases),
            per_seq(16, 1, 32, 256),
            whole(win),
            whole(live_col),
        ],
        out_specs=[
            per_seq(16, 1, 32, 256),
            pl.BlockSpec((8, 2, 8, 1, 16, 128), lambda s: (0, 0, 0, s, 0, 0)),
        ],
        out_shape=[
            jax.ShapeDtypeStruct(x.shape, BF16),
            jax.ShapeDtypeStruct((8, 2, 8, count, 16, 128), BF16),
        ],
        scratch_shapes=[
            pltpu.VMEM((8, 512, 512), F32),
            pltpu.VMEM((256, 512), BF16),
            pltpu.VMEM((512, 256), BF16),
            pltpu.VMEM((8, 48, 512), BF16),
            pltpu.VMEM((256, 512), F32),
            pltpu.VMEM((8, 512), F32),
        ],
        compiler_params=params(52),
        name="row_attention",
    )(place, *biases, x, win, live_col)


def outer_kernel(
    core_ref,
    l_ref,
    own_ref,
    other_ref,
    w_ref,
    inv_ref,
    plane_ref,
    pair_ref,
    wp_ref,
    mid_ref,
    tri_ref,
    lt_ref,
    x_ref,
):
    for v in range(8):
        rows = slice(128 * v, 128 * v + 128)
        lt_ref[rows, :] = l_ref[:, rows].astype(F32).T.astype(BF16)
    for ref, core in ((own_ref, core_ref[0]), (other_ref, 1 - core_ref[0])):

        def some(n, carry):
            lanes = pl.ds(pl.multiple_of(n * 256, 256), 256)
            product = jnp.dot(lt_ref[...], ref[:, lanes], preferred_element_type=F32)
            for k in range(2):
                base = pl.multiple_of(core * 512 + n * 128 + 64 * k, 64)
                for v in range(8):
                    for half in range(2):
                        at = 128 * v + 32 * half
                        low, high = mix(
                            product[at : at + 32, 128 * k : 128 * k + 128],
                            product[at + 64 : at + 96, 128 * k : 128 * k + 128],
                        )
                        place = (v % 2) * 256 + 128 * half
                        columns = slice(place, place + 128)
                        x_ref[v // 2, pl.ds(base, 32), columns] = low.astype(BF16)
                        x_ref[v // 2, pl.ds(base + 32, 32), columns] = high.astype(BF16)
            return carry

        lax.fori_loop(0, 4, some, 0, unroll=2)

    def finish(g, carry):
        update = jnp.dot(w_ref[...], x_ref[g], preferred_element_type=F32)
        places = [(half, 2 * g + e) for e in range(2) for half in range(2)]
        inv = jnp.concatenate([inv_ref[half, v] for half, v in places], axis=1)
        live = jnp.concatenate([plane_ref[half, v] for half, v in places], axis=1)
        before = jnp.concatenate(
            [pair_ref[half + 2 * k, v] for half, v in places for k in range(2)], axis=0
        )
        mid = (before.astype(F32) + (update * inv).T).astype(BF16)
        normed = layer_norm(mid).astype(BF16)
        terms = lax.dot_general(wp_ref[...], normed, NT, preferred_element_type=F32)
        ta = (jax.nn.sigmoid(terms[:128]) * terms[128:256] * live).astype(BF16)
        tb = (jax.nn.sigmoid(terms[256:384]) * terms[384:] * live).astype(BF16)
        for n, (half, v) in enumerate(places):
            for k in range(2):
                mid_ref[half + 2 * k, v] = mid[128 * n + 64 * k : 128 * n + 64 * k + 64]
            tri_ref[half, v, :128] = ta[:, 128 * n : 128 * n + 128]
            tri_ref[half, v, 128:] = tb[:, 128 * n : 128 * n + 128]
        return carry

    lax.fori_loop(0, 4, finish, 0, unroll=True)


def outer_update(core, left, own, other, weight, inv, live_plane, pairwise, wp):
    total = left.shape[0]
    vmem = pl.BlockSpec(memory_space=pltpu.VMEM)
    return pl.pallas_call(
        outer_kernel,
        in_specs=[pl.BlockSpec(memory_space=pltpu.SMEM)] + [vmem] * 8,
        out_shape=[
            jax.ShapeDtypeStruct((4, 8, 64, 128), BF16),
            jax.ShapeDtypeStruct((2, 8, 256, 128), BF16),
        ],
        scratch_shapes=[pltpu.VMEM((1024, total), BF16), pltpu.VMEM((4, 1024, 512), BF16)],
        compiler_params=params(20),
        name="outer_update",
    )(core, left, own, other, weight, inv, live_plane, pairwise, wp)


def triangle_kernel(in_ref, out_ref, a_ref, b_ref):
    def assemble(r, carry):
        base = pl.multiple_of(r * 32, 32)
        for t, ref in ((0, a_ref), (1, b_ref)):
            for m in range(4):
                low, high = mix(
                    in_ref[r * 8 + 2 * m, t].astype(F32), in_ref[r * 8 + 2 * m + 1, t].astype(F32)
                )
                ref[pl.ds(base, 16), 128 * m : 128 * m + 128] = low.astype(BF16)
                ref[pl.ds(base + 16, 16), 128 * m : 128 * m + 128] = high.astype(BF16)
        return carry

    lax.fori_loop(0, 16, assemble, 0, unroll=True)

    def multiply(g, carry):
        base = pl.multiple_of(g * 128, 128)
        c = lax.dot_general(a_ref[pl.ds(base, 128), :], b_ref[...], NT, preferred_element_type=F32)
        for part in range(4):
            for m in range(4):
                columns = slice(128 * m, 128 * m + 128)
                even, odd = mix(
                    c[32 * part : 32 * part + 16, columns], c[32 * part + 16 : 32 * part + 32, columns]
                )
                out_ref[(g * 4 + part) * 8 + 2 * m] = even.astype(BF16)
                out_ref[(g * 4 + part) * 8 + 2 * m + 1] = odd.astype(BF16)
        return carry

    lax.fori_loop(0, 4, multiply, 0, unroll=True)


def triangle(blocks):
    return pl.pallas_call(
        triangle_kernel,
        out_shape=jax.ShapeDtypeStruct((128, 16, 128), BF16),
        scratch_shapes=[pltpu.VMEM((512, 512), BF16), pltpu.VMEM((512, 512), BF16)],
        compiler_params=params(16),
        name="triangle",
    )(blocks)


def gate_kernel(mid_ref, wg_ref, out_ref):
    for u in range(16):
        mid = jnp.concatenate([mid_ref[u], mid_ref[16 + u]], axis=0)
        out_ref[u] = jax.nn.sigmoid(
            jnp.dot(layer_norm(mid).astype(BF16), wg_ref[...], preferred_element_type=F32)
        )


def gates(mid, wg):
    return pl.pallas_call(
        gate_kernel,
        out_shape=jax.ShapeDtypeStruct((16, 128, 128), F32),
        compiler_params=params(16),
        name="pair_gate",
    )(mid, wg)


def final_kernel(tri_ref, mid_ref, wt_ref, gate_ref, out_ref):
    for u in range(16):
        combined = tri_ref[u].astype(F32)
        centered = combined - jnp.mean(combined, axis=0, keepdims=True)
        variance = jnp.mean(centered * centered, axis=0, keepdims=True)
        normed = (centered * lax.rsqrt(variance + EPS)).astype(BF16)
        update = jnp.dot(wt_ref[...], normed, preferred_element_type=F32)
        mid = jnp.concatenate([mid_ref[u], mid_ref[16 + u]], axis=0)
        out = (mid.astype(F32) + gate_ref[u] * update.T).astype(BF16)
        out_ref[u] = out[:64]
        out_ref[16 + u] = out[64:]


def final(tri, mid, wt, gate):
    return pl.pallas_call(
        final_kernel,
        out_shape=jax.ShapeDtypeStruct((32, 64, 128), BF16),
        compiler_params=params(16),
        name="pair_final",
    )(tri, mid, wt, gate)


def copy_kernel(in_ref, out_ref):
    out_ref[...] = in_ref[...]


def copied(a):
    return pl.pallas_call(
        copy_kernel,
        out_shape=jax.ShapeDtypeStruct(a.shape, a.dtype),
        compiler_params=params(8),
        name="copied",
    )(a)


def body(
    alignment,
    pairwise,
    residue_mask,
    sequence_mask,
    attention_input_weight,
    attention_output_weight,
    bias_project,
    outer_factor_weight,
    outer_output,
    tri_project,
    tri_gate,
    tri_output,
):
    row = lax.axis_index(ROW)
    col = lax.axis_index(COL)
    core = lax.axis_index("core")
    swap = [(0, 1), (1, 0)]
    res_live = residue_mask.astype(F32)
    seq_live = sequence_mask.astype(F32)
    row_live = lax.dynamic_slice_in_dim(res_live, row * 32, 32)
    col_live = lax.dynamic_slice_in_dim(res_live, col * 64, 64)
    my_seqs = lax.dynamic_slice_in_dim(sequence_mask, col * 80 + row * 5, 5)
    scalars = jnp.concatenate([jnp.stack([core, lax.axis_index("y")]), my_seqs])

    blocks = lax.all_to_all(
        pair_bias(pairwise, bias_project.T).reshape(32, 64, 128),
        ROW + ("zh",),
        split_axis=0,
        concat_axis=0,
        tiled=True,
    )
    live_plane = row_live[:, None] * col_live[None, :]
    inv = 1.0 / jnp.maximum(jnp.sum(seq_live) * live_plane, 1.0)

    def pairs(a):
        return a.reshape(2, 16, 64).transpose(1, 0, 2).reshape(2, 8, 1, 128)

    weight = outer_output.reshape(32, 2, 16, 128).transpose(3, 2, 1, 0).reshape(128, 1024)
    wp = tri_project.reshape(128, 512).T
    wt = tri_output.T
    wl = outer_factor_weight[:, 0].T
    win = jnp.concatenate(
        [
            attention_input_weight.reshape(256, 1024).T,
            attention_output_weight,
            wl,
            wl,
            wl,
            wl,
            outer_factor_weight[:, 1].T,
        ],
        axis=0,
    )
    live_cols = jnp.broadcast_to(res_live[:, None], (512, 128))
    blocks, weight, wp, wt, inv, live_plane, win, live_cols, scalars = (
        lax.optimization_barrier(
            (
                blocks,
                weight,
                wp,
                wt,
                pairs(inv),
                pairs(live_plane),
                win,
                live_cols,
                scalars,
            )
        )
    )
    outgoing, bias_plane = lax.optimization_barrier(
        (alignment.reshape(16, 5, 32, 256), plane(blocks))
    )
    up, down = ([(i, (i + d) % 4) for i in range(4)] for d in (1, 3))
    left_plane = lax.ppermute(bias_plane, "y", up)
    right_plane = lax.ppermute(bias_plane, "y", down)
    far_plane = jnp.concatenate(
        [lax.ppermute(left_plane[:2], "y", up), lax.ppermute(right_plane[2:], "y", down)], axis=0
    )
    own = [bias_plane, left_plane, far_plane, right_plane]
    other = [lax.ppermute(b, "core", swap) for b in own]
    sequences = lax.all_to_all(outgoing, ROW, split_axis=0, concat_axis=0, tiled=True)
    out_seq, factors = attention(scalars, own + other, sequences, win, live_cols)
    factors = lax.all_to_all(
        factors.reshape(128, 80, 128), ALL, split_axis=0, concat_axis=0, tiled=True
    )
    out_seq, factors = lax.optimization_barrier((out_seq, factors))
    factors, far_factors = lax.optimization_barrier(
        (factors, lax.ppermute(factors, "core", swap))
    )
    factors = factors.reshape(640, 16, 128)
    left = factors[:, :8].reshape(640, 1024)
    right_own = factors[:, 8:].reshape(640, 1024)
    right_other = far_factors.reshape(640, 16, 128)[:, 8:].reshape(640, 1024)
    alignment_output = lax.all_to_all(
        out_seq, ROW, split_axis=0, concat_axis=0, tiled=True
    ).reshape(80, 32, 256)

    mid, tri = outer_update(
        core.reshape(1),
        left,
        right_own,
        right_other,
        weight,
        inv,
        live_plane,
        pairwise.reshape(4, 8, 64, 128),
        wp,
    )
    tri = tri.reshape(16, 2, 128, 128).transpose(2, 1, 0, 3)
    tri, alignment_output = lax.optimization_barrier((tri, alignment_output))
    alignment_output = copied(alignment_output)
    blocks = lax.all_to_all(tri, ALL, split_axis=0, concat_axis=0, tiled=True)
    product, mid = lax.optimization_barrier((triangle(blocks), mid.reshape(32, 64, 128)))
    combined = lax.all_to_all(product, ALL, split_axis=0, concat_axis=0, tiled=True)
    pair_output_state = final(combined.transpose(1, 0, 2), mid, wt, gates(mid, tri_gate))
    return (alignment_output, pair_output_state)


def solution(mesh):
    fine = Mesh(mesh.devices.reshape(4, 2, 2, 2, 4), ALL)
    placed = (P(COL, ROW, None), P(ROW, COL, None)) + (P(),) * 10
    return jax.shard_map(
        body,
        mesh=fine,
        in_specs=placed,
        out_specs=(P(COL, ROW, None), P(ROW, COL, None)),
        check_vma=False,
    )
```
